32 devices in a mesh: seq: 32 (over z, y, x, core).
Axes of the slice: x: 2, y: 2, z: 4, core: 2. Of those that a mesh axis runs over, the one named last changes fastest.
Arguments:
- block_input: float32 [4096, 2048], P('seq'), may hold values from -6 to 6
- start_flags: int32 [4096], P('seq'), may hold values from 0 to 1, as said below
- norm_gain: bfloat16 [2048], replicated, may hold values from 0.5 to 1.5
- gate_weight: bfloat16 [2048, 2730], P('seq'), may hold values from -0.125 to 0.125
- linear_weight: bfloat16 [2048, 2730], P('seq'), may hold values from -0.125 to 0.125
- conv_taps: bfloat16 [4, 2730], replicated, may hold values from -3 to 3
- conv_bias: bfloat16 [2730], replicated, may hold values from -2 to 2
- reset_weight: bfloat16 [10, 273, 273], replicated, may hold values from -0.375 to 0.375
- reset_bias: bfloat16 [2730], replicated, may hold values from -3 to 3
- input_weight: bfloat16 [10, 273, 273], replicated, may hold values from -0.375 to 0.375
- input_bias: bfloat16 [2730], replicated, may hold values from -3 to 3
- decay_param: bfloat16 [2730], replicated, may hold values from 6 to 14
- out_weight: bfloat16 [2048, 2730], P('seq'), may hold values from -0.109375 to 0.109375
- feed_norm_gain: bfloat16 [2048], replicated, may hold values from 0.5 to 1.5
- feed_gate_weight: bfloat16 [2048, 6144], P('seq'), may hold values from -0.125 to 0.125
- feed_value_weight: bfloat16 [2048, 6144], P('seq'), may hold values from -0.125 to 0.125
- feed_down_weight: bfloat16 [2048, 6144], P('seq'), may hold values from -0.078125 to 0.078125
- output_grad: float32 [4096, 2048], P('seq'), may hold values from -6 to 6
Outputs:
- block_output: float32 [4096, 2048], P('seq')
- input_grad: float32 [4096, 2048], P('seq')
- grad_norm_gain: float32 [2048], replicated
- grad_gate_weight: float32 [2048, 2730], P('seq')
- grad_linear_weight: float32 [2048, 2730], P('seq')
- grad_conv_taps: float32 [4, 2730], replicated
- grad_conv_bias: float32 [2730], replicated
- grad_reset_weight: float32 [10, 273, 273], replicated
- grad_reset_bias: float32 [2730], replicated
- grad_input_weight: float32 [10, 273, 273], replicated
- grad_input_bias: float32 [2730], replicated
- grad_decay_param: float32 [2730], replicated
- grad_out_weight: float32 [2048, 2730], P('seq')
- grad_feed_norm_gain: float32 [2048], replicated
- grad_feed_gate_weight: float32 [2048, 6144], P('seq')
- grad_feed_value_weight: float32 [2048, 6144], P('seq')
- grad_feed_down_weight: float32 [2048, 6144], P('seq')
The draws below stay inside these ranges and needn't reach their ends.
Inputs may be any that keep to these rules, and one draw needn't show every extreme that they name: start_flags is 1 at token 0. The stream is a packing of 2 rows of 2048 tokens each. Each row begins with a 1 and holds at most three documents.
All inputs are finite; a program needn't handle non-finite values.
Results may differ from the reference program's by a relative error of at most 0.008.
The reference program's roundings to bfloat16 on the way count: a program that leaves them out, or rounds other values in their place, can miss the bound.
Values may be sent and summed in bfloat16 or wider, within the bound.
No kernel may reach another device: no remote copies, remote signals or barrier semaphores. Data moves between devices by JAX's collectives and lax.ppermute only.
A program may use at most 832 MiB of HBM per device.

```python
import jax
import jax.numpy as jnp
from jax import lax

D = 2048
R = 2730
F = 6144
HEADS = 10
BLOCK = 273
TOK_DEV = 128
SHORT_ROW = 2048
TOKENS = 4096
LONG_ROWS = 0
ROWS = 2


def draw_start_flags(key, part):
    key = jax.random.fold_in(key, 11)
    split_keys = jax.random.split(key, 7)
    row_kinds = jax.random.permutation(split_keys[0], jnp.array([1] * LONG_ROWS + [0] * (ROWS - LONG_ROWS), dtype=jnp.int32))
    row_lengths = (SHORT_ROW + 3 * SHORT_ROW * row_kinds).astype(jnp.int32)
    row_ends = jnp.cumsum(row_lengths).astype(jnp.int32)
    row_begins = (row_ends - row_lengths).astype(jnp.int32)
    loose_cuts = jax.random.randint(split_keys[1], (ROWS, 2), row_begins[:, None] + 1, row_ends[:, None], dtype=jnp.int32)
    lowest_edge = ((row_begins + 2) // TOK_DEV + 1).astype(jnp.int32)
    highest_edge = ((row_ends - 3) // TOK_DEV).astype(jnp.int32)
    first_edge = jax.random.randint(split_keys[2], (ROWS,), lowest_edge, highest_edge, dtype=jnp.int32)
    second_edge = jax.random.randint(split_keys[3], (ROWS,), first_edge + 1, highest_edge + 1, dtype=jnp.int32)
    early_cut = first_edge * TOK_DEV + jax.random.randint(split_keys[4], (ROWS,), 1, 3, dtype=jnp.int32)
    late_cut = second_edge * TOK_DEV - jax.random.randint(split_keys[5], (ROWS,), 1, 3, dtype=jnp.int32)
    chosen = jax.random.randint(split_keys[6], (), 0, ROWS, dtype=jnp.int32)
    forced = jnp.arange(ROWS, dtype=jnp.int32) == chosen
    first_split = jnp.where(forced, early_cut, loose_cuts[:, 0]).astype(jnp.int32)
    second_split = jnp.where(forced, late_cut, loose_cuts[:, 1]).astype(jnp.int32)
    flag_marks = jnp.zeros((TOKENS,), jnp.int32)
    flag_marks = flag_marks.at[row_begins].set(1).at[first_split].set(1).at[second_split].set(1)
    return flag_marks


def spiked(drawn, rng, source, target, parts, factor):
    owner, partner = [(jnp.arange(drawn.shape[position]) // (drawn.shape[position] // parts)).reshape([-1 if axis == position else 1 for axis in range(drawn.ndim)]) for position in (source, target)]
    chosen = jax.random.permutation(rng, parts)[partner]
    strong = (owner == chosen) | (owner == (partner + parts // 2) % parts)
    return jnp.where(strong, factor * drawn, drawn)


def block_levels(key, dims, cuts, least, high):
    loudness, own = 1.0, jax.random.fold_in(key, 6)
    for dim, shards_of in cuts:
        draws = jnp.exp(jax.random.uniform(jax.random.fold_in(own, dim), (shards_of,), jnp.float32, least / len(cuts), high / len(cuts)))
        loudness = loudness * jnp.repeat(draws, dims[dim] // shards_of).reshape([-1 if axis == dim else 1 for axis in range(len(dims))])
    return loudness


def scatter_about(stream_key, dims, width, reach, pieces=(), kind=jnp.bfloat16):
    entries = jax.random.normal(stream_key, dims, jnp.float32) * width
    if len(pieces) > 0:
        entries = block_levels(stream_key, dims, pieces, -0.22, 0.18) * entries
    return jnp.clip(entries, min=-reach, max=reach).astype(kind)


def heavy_noise(own_key, dims, deviation, reach, cuts, heavy, held_as=jnp.bfloat16):
    values = deviation * jax.random.normal(own_key, dims, jnp.float32)
    if cuts:
        values = values * block_levels(own_key, dims, cuts, -0.22, 0.18)
    return jnp.clip(spiked(values, jax.random.fold_in(own_key, 3), *heavy), -reach, reach).astype(held_as)


def setup_inputs(seed: int = 0) -> dict:
    arg_keys = jax.random.split(jax.random.key(seed), 19)
    return {
        "block_input": scatter_about(arg_keys[0], (TOKENS, D), 1.0, 6.0, ((0, 32),), jnp.float32),
        "start_flags": draw_start_flags(jax.random.fold_in(arg_keys[18], 71), 0),
        "norm_gain": jnp.clip(1.0 + 0.1 * jax.random.normal(arg_keys[2], (D,), jnp.float32), 0.5, 1.5).astype(jnp.bfloat16),
        "gate_weight": scatter_about(arg_keys[3], (D, R), D ** -0.5, 0.125, ((0, 32),)),
        "linear_weight": scatter_about(arg_keys[4], (D, R), D ** -0.5, 0.125, ((0, 32),)),
        "conv_taps": scatter_about(arg_keys[5], (4, R), 4 ** -0.5, 3.0),
        "conv_bias": scatter_about(arg_keys[6], (R,), 0.3, 2.0),
        "reset_weight": scatter_about(arg_keys[7], (HEADS, BLOCK, BLOCK), BLOCK ** -0.5, 0.375),
        "reset_bias": scatter_about(arg_keys[8], (R,), 0.5, 3.0),
        "input_weight": scatter_about(arg_keys[9], (HEADS, BLOCK, BLOCK), BLOCK ** -0.5, 0.375),
        "input_bias": scatter_about(arg_keys[10], (R,), 0.5, 3.0),
        "decay_param": jnp.clip(jax.random.uniform(arg_keys[11], (R,), jnp.float32, 6.0, 14.0), 6.0, 14.0).astype(jnp.bfloat16),
        "out_weight": scatter_about(arg_keys[12], (D, R), R ** -0.5, 0.109375, ((0, 32),)),
        "feed_norm_gain": jnp.clip(1.0 + 0.1 * jax.random.normal(arg_keys[13], (D,), jnp.float32), 0.5, 1.5).astype(jnp.bfloat16),
        "feed_gate_weight": scatter_about(arg_keys[14], (D, F), D ** -0.5, 0.125, ((0, 32),)),
        "feed_value_weight": scatter_about(arg_keys[15], (D, F), D ** -0.5, 0.125, ((0, 32),)),
        "feed_down_weight": scatter_about(arg_keys[16], (D, F), F ** -0.5, 0.078125, ((0, 32),)),
        "output_grad": heavy_noise(arg_keys[17], (TOKENS, D), 1.0, 6.0, ((0, 32),), (0, 1, 32, 2.75), jnp.float32),
    }


@jax.custom_vjp
def low(v):
    return lax.optimization_barrier(v.astype(jnp.bfloat16)).astype(jnp.float32)

@jax.custom_vjp
def low_back(v):
    return v

def low_keep(v):
    return (low(v), None)

def low_pass(kept, grad):
    return (grad,)

def back_keep(v):
    return (v, None)

def back_low(kept, grad):
    return (low(grad),)
low.defvjp(low_keep, low_pass)
low_back.defvjp(back_keep, back_low)
ROOT_GUARD = 0.001
HIGHEST_PRECISION = lax.Precision.HIGHEST

def product(left_side, right_side):
    return jnp.dot(left_side, right_side, precision=HIGHEST_PRECISION, preferred_element_type=jnp.float32)

def product_last(left_side, right_side):
    return lax.dot_general(left_side, right_side, (((1,), (1,)), ((), ())), precision=HIGHEST_PRECISION, preferred_element_type=jnp.float32)

def rms_scale(values):
    return lax.rsqrt(lax.optimization_barrier(jnp.mean(values * values, axis=-1, keepdims=True)) + 1e-06)

def block_gate(conv_out, weight, bias):
    blocks_in = conv_out.reshape(conv_out.shape[0], weight.shape[0], weight.shape[1])
    mixed_out = jnp.einsum('thi,hij->thj', blocks_in, weight, precision=HIGHEST_PRECISION)
    return mixed_out.reshape(conv_out.shape) + bias

def causal_conv(linear, conv_taps, conv_bias, document):
    running = linear * conv_taps[0] + conv_bias
    for shift_by in range(1, 4):
        shifted = jnp.concatenate([jnp.zeros((shift_by, linear.shape[1]), jnp.float32), linear[:-shift_by]], axis=0)
        same_doc = jnp.concatenate([jnp.zeros((shift_by,), jnp.float32), (document[shift_by:] == document[:-shift_by]).astype(jnp.float32)])
        running = running + shifted * conv_taps[shift_by] * same_doc[:, None]
    return running

def recurrence(decay_rate, driven):

    def advance(state_now, inputs):
        state_now = inputs[0] * state_now + inputs[1]
        return (state_now, state_now)
    final_state, states = lax.scan(advance, jnp.zeros((decay_rate.shape[1],), jnp.float32), (decay_rate, driven))
    return states

def feed_block(normed_two, feed_gate_weight, feed_value_weight, feed_down_weight):
    inner_gate = low_back(product(normed_two, feed_gate_weight))
    inner_value = low_back(product(normed_two, feed_value_weight))
    hidden = low(jax.nn.gelu(inner_gate) * inner_value)
    return low_back(product_last(hidden, feed_down_weight))

def forward(block_input, norm_gain, gate_weight, linear_weight, conv_taps, conv_bias, reset_weight, reset_bias, input_weight, input_bias, decay_param, out_weight, feed_norm_gain, feed_gate_weight, feed_value_weight, feed_down_weight, start_flags):
    document = jnp.cumsum(start_flags).astype(jnp.int32)
    starts = start_flags.astype(jnp.float32)[:, None]
    keep_mask = 1.0 - starts
    normed = low(block_input * rms_scale(block_input) * norm_gain)
    gate_pre = low_back(product(normed, gate_weight))
    linear = low_back(product(normed, linear_weight))
    conv_out = low(causal_conv(linear, conv_taps, conv_bias, document))
    reset_gate = jax.nn.sigmoid(low_back(block_gate(conv_out, reset_weight, reset_bias)))
    input_gate = jax.nn.sigmoid(low_back(block_gate(conv_out, input_weight, input_bias)))
    log_decay = -8.0 * reset_gate * jax.nn.softplus(-decay_param)
    decay_rate = jnp.exp(log_decay) * keep_mask
    multiplier = keep_mask * jnp.sqrt(1.0 - decay_rate * decay_rate + ROOT_GUARD) + starts
    states = recurrence(decay_rate, multiplier * input_gate * conv_out)
    mixed = low(states * jax.nn.gelu(gate_pre))
    middle = block_input + low_back(product_last(mixed, out_weight))
    normed_two = low(middle * rms_scale(middle) * feed_norm_gain)
    row_blocks = normed_two.reshape(16, -1, normed_two.shape[1])

    def run_block(row_block):
        return feed_block(row_block, feed_gate_weight, feed_value_weight, feed_down_weight)
    feed_out = lax.map(jax.checkpoint(run_block), row_blocks).reshape(middle.shape)
    return middle + feed_out

def reference(block_input, start_flags, norm_gain, gate_weight, linear_weight, conv_taps, conv_bias, reset_weight, reset_bias, input_weight, input_bias, decay_param, out_weight, feed_norm_gain, feed_gate_weight, feed_value_weight, feed_down_weight, output_grad):
    floats = tuple((tensor_in.astype(jnp.float32) for tensor_in in (block_input, norm_gain, gate_weight, linear_weight, conv_taps, conv_bias, reset_weight, reset_bias, input_weight, input_bias, decay_param, out_weight, feed_norm_gain, feed_gate_weight, feed_value_weight, feed_down_weight)))

    def run_forward(*params):
        return forward(*params, start_flags)
    block_output, pull_back = jax.vjp(run_forward, *floats)
    grads = pull_back(output_grad.astype(jnp.float32))
    return (block_output, grads[0], grads[1], grads[2], grads[3], grads[4], grads[5], grads[6], grads[7], grads[8], grads[9], grads[10], grads[11], grads[12], grads[13], grads[14], grads[15])
```

```python
import functools

import jax
import jax.numpy as jnp
from jax import lax
from jax.experimental import pallas as pl
from jax.experimental.pallas import tpu as pltpu
from jax.sharding import PartitionSpec as P

AXIS = "seq"
ROOT_GUARD = 0.001
SIDE = 8
CORE, XBIT, YBIT, LBIT, HBIT = 1, 2, 4, 8, 16
EXTRA = {0: 8, 6: 9}
F32, BF16 = jnp.float32, jnp.bfloat16


def place_in_side(i):
    return ((i >> 3) & 1) * 4 + (i & 3)


def mask_of(j):
    return (j & 3) | ((j >> 2) & 1) * LBIT


def swap(v, mask, only=None):
    n = lax.axis_size(AXIS)
    pairs = [(i, i ^ mask) for i in range(n) if only is None or place_in_side(i) in only]
    return lax.ppermute(v, AXIS, pairs)


def far_masks():
    n, masks, m = lax.axis_size(AXIS), [], HBIT
    while m < n:
        masks.append(m)
        m *= 2
    return masks + [YBIT]


def side_groups():
    n = lax.axis_size(AXIS)
    return [
        [b | mask_of(j) for j in range(SIDE)] for b in range(n) if b & (CORE | XBIT | LBIT) == 0
    ]


def dot(a, b):
    return lax.dot_general(a, b, (((1,), (0,)), ((), ())), preferred_element_type=F32)


def dot_last(a, b):
    return lax.dot_general(a, b, (((1,), (1,)), ((), ())), preferred_element_type=F32)


def dot_first(a, b):
    return lax.dot_general(a, b, (((0,), (0,)), ((), ())), preferred_element_type=F32)


def gather_side(x):
    half = x.shape[0] // 2
    by_l, by_x = swap(x, LBIT), swap(x, XBIT)
    both = jnp.concatenate([swap(by_l[:half], XBIT), swap(by_x[half:], LBIT)])
    found = []
    for own in (x, by_x, by_l, both):
        found += [own, swap(own, CORE)]
    return found


def scatter_side(blocks):
    rows, width = blocks[0].shape
    sent = swap(jnp.concatenate([b.astype(BF16) for b in blocks[1::2]]), CORE).reshape(
        4, rows, width
    )
    kept = [blocks[2 * i] + sent[i].astype(F32) for i in range(4)]
    half = width // 2
    ka, kb = [k[:, :half] for k in kept], [k[:, half:] for k in kept]

    def pair(first, second, mask):
        got = swap(jnp.concatenate([first, second]).astype(BF16), mask).astype(F32)
        return got[:rows], got[rows:]

    a0, a1 = pair(ka[2], ka[3], LBIT)
    b0, b1 = pair(kb[1], kb[3], XBIT)
    a_last = swap((ka[1] + a1).astype(BF16), XBIT).astype(F32)
    b_last = swap((kb[2] + b1).astype(BF16), LBIT).astype(F32)
    return jnp.concatenate([ka[0] + a0 + a_last, kb[0] + b0 + b_last], axis=1)


def gather_far(x, only=None):
    chunks = [x]
    for m in far_masks():
        chunks += [swap(c, m, only) for c in chunks]
    return chunks


def scatter_far(x, axis, only=None):
    for m in reversed(far_masks()):
        half = x.shape[axis] // 2
        kept = lax.slice_in_dim(x, 0, half, axis=axis)
        sent = lax.slice_in_dim(x, half, 2 * half, axis=axis)
        x = kept + swap(sent.astype(BF16), m, only).astype(F32)
    return x


def flips(v, me, y_axis, h_axis):
    v = jnp.where((me & YBIT) != 0, jnp.flip(v, y_axis), v)
    size, m = v.shape[h_axis], HBIT
    step = 1
    while step < size:
        shape = v.shape
        split = shape[:h_axis] + (size // (2 * step), 2, step) + shape[h_axis + 1 :]
        w = v.reshape(split)
        w = jnp.where((me & m) != 0, jnp.flip(w, h_axis + 1), w)
        v = w.reshape(shape)
        m *= 2
        step *= 2
    return v


def to_near(v, me):
    lead, k = v.shape[:-1], v.ndim - 1
    n, width = lax.axis_size(AXIS), v.shape[-1]
    high = n // 16
    w = v.reshape(lead + (high, 2, 2, width // (high * 4)))
    w = flips(w, me, k + 2, k)
    order = tuple(range(k)) + (k + 2, k, k + 1, k + 3)
    return w.transpose(order).reshape(v.shape)


def from_near(v, me):
    lead, k = v.shape[:-1], v.ndim - 1
    n, width = lax.axis_size(AXIS), v.shape[-1]
    high = n // 16
    w = v.reshape(lead + (2, high, 2, width // (high * 4)))
    w = flips(w, me, k, k + 1)
    order = tuple(range(k)) + (k + 1, k + 2, k, k + 3)
    return w.transpose(order).reshape(v.shape)


def rms_scale(values):
    return lax.rsqrt(jnp.mean(values * values, axis=-1, keepdims=True) + 1e-06)


def norm_back(grad_normed, values, scale, gain):
    scaled = grad_normed * gain
    return scale * scaled - values * (scale * scale * scale) * jnp.mean(
        scaled * values, axis=-1, keepdims=True
    )


def gelu_pair(v):
    k = 0.7978845608028654
    sq = v * v
    th = jnp.tanh(k * v * (1.0 + 0.044715 * sq))
    half = 0.5 * (1.0 + th)
    act = v * half
    slope = half + 0.5 * v * (1.0 - th * th) * (k * (1.0 + 3.0 * 0.044715 * sq))
    return act, slope


NB = 8
UNROLL = 8


def scan_kernel(a_ref, b_ref, p_ref, s_ref):
    bl = a_ref.shape[0] // NB

    def rows(i):
        return pl.ds(i, NB, stride=bl)

    def step(i, c):
        p, s = c
        a, b = a_ref[rows(i), :], b_ref[rows(i), :]
        p, s = p * a, a * s + b
        p_ref[rows(i), :] = p
        s_ref[rows(i), :] = s
        return p, s

    def steps(o, c):
        for k in range(UNROLL):
            c = step(o * UNROLL + k, c)
        return c

    shape = (NB, a_ref.shape[1])
    p, s = lax.fori_loop(0, bl // UNROLL, steps, (jnp.ones(shape, F32), jnp.zeros(shape, F32)))
    half = NB // 2
    for seg in range(2):
        j = seg * half
        cp, cs = p[j : j + 1], s[j : j + 1]
        for j in range(seg * half + 1, seg * half + half):
            sl = pl.ds(j * bl, bl)
            pv = p_ref[sl, :]
            s_ref[sl, :] = s_ref[sl, :] + pv * cs
            p_ref[sl, :] = pv * cp
            cs = s[j : j + 1] + p[j : j + 1] * cs
            cp = p[j : j + 1] * cp


def back_scan_kernel(a_ref, b_ref, q_ref, g_ref):
    bl = a_ref.shape[0] // NB

    def rows(i):
        return pl.ds(i, NB, stride=bl)

    def step(i, c):
        ag, aq = c
        b = b_ref[rows(i), :]
        g, q = b + ag, aq
        g_ref[rows(i), :] = g
        q_ref[rows(i), :] = q
        a = a_ref[rows(i), :]
        return a * g, a * q

    def steps(o, c):
        for k in range(UNROLL):
            c = step(bl - 1 - (o * UNROLL + k), c)
        return c

    shape = (NB, a_ref.shape[1])
    hg, hq = lax.fori_loop(0, bl // UNROLL, steps, (jnp.zeros(shape, F32), jnp.ones(shape, F32)))
    half = NB // 2
    for seg in range(2):
        j = seg * half + half - 1
        u, v = hg[j : j + 1], hq[j : j + 1]
        for j in range(seg * half + half - 2, seg * half - 1, -1):
            sl = pl.ds(j * bl, bl)
            qv = q_ref[sl, :]
            g_ref[sl, :] = g_ref[sl, :] + qv * u
            q_ref[sl, :] = qv * v
            u = hg[j : j + 1] + hq[j : j + 1] * u
            v = hq[j : j + 1] * v


def run_scan(kernel, a, b):
    rows, width = a.shape
    spec = pl.BlockSpec((rows, 128), lambda j: (0, j))
    return pl.pallas_call(
        kernel,
        grid=(pl.cdiv(width, 128),),
        in_specs=[spec, spec],
        out_specs=[spec, spec],
        out_shape=[jax.ShapeDtypeStruct((rows, width), F32)] * 2,
        compiler_params=pltpu.CompilerParams(vmem_limit_bytes=32 * 1024 * 1024),
    )(a, b)


def body(
    block_input,
    start_flags,
    norm_gain,
    gate_weight,
    linear_weight,
    conv_taps,
    conv_bias,
    reset_weight,
    reset_bias,
    input_weight,
    input_bias,
    decay_param,
    out_weight,
    feed_norm_gain,
    feed_gate_weight,
    feed_value_weight,
    feed_down_weight,
    output_grad,
):
    n = lax.axis_size(AXIS)
    me = lax.axis_index(AXIS)
    here = ((me >> 3) & 1) * 4 + (me & 3)
    tok, width = block_input.shape
    heads, blk = reset_weight.shape[:2]
    rows_w = gate_weight.shape[0]
    feed = feed_gate_weight.shape[1]
    fs = feed // SIDE
    high = n // 16
    groups = side_groups()
    only = tuple(EXTRA)
    extra_here = jnp.where(here == only[1], EXTRA[only[1]], EXTRA[only[0]])
    has_extra = (here == only[0]) | (here == only[1])

    def exchange(v):
        return lax.all_to_all(v, AXIS, 0, 0, axis_index_groups=groups, tiled=True)

    def head_parts(w):
        w = w.reshape(rows_w, heads, blk)
        zero = jnp.zeros((rows_w, blk), w.dtype)
        return jnp.stack(
            [
                jnp.concatenate([w[:, s], w[:, EXTRA[s]] if s in EXTRA else zero], axis=1)
                for s in range(SIDE)
            ]
        )

    def feed_parts(w):
        return w.reshape(rows_w, SIDE, fs).transpose(1, 0, 2)

    def mixer_full(parts):
        shard = parts.reshape(SIDE * rows_w, 2 * blk).T
        first = gather_far(shard[:blk])
        second = gather_far(shard[blk:], only)
        return jnp.concatenate(
            [jnp.concatenate(first, axis=1), jnp.concatenate(second, axis=1)], axis=0
        )

    def feed_full(parts):
        return jnp.concatenate(gather_far(parts.reshape(SIDE * rows_w, fs)), axis=0)

    mix_parts = exchange(
        jnp.stack([head_parts(gate_weight), head_parts(linear_weight)], axis=1)
    )
    out_parts = exchange(head_parts(out_weight))
    feed_parts_all = exchange(
        jnp.stack(
            [feed_parts(w) for w in (feed_gate_weight, feed_value_weight, feed_down_weight)], axis=1
        )
    )
    gate_t, linear_t = mixer_full(mix_parts[:, 0]), mixer_full(mix_parts[:, 1])
    out_t = mixer_full(out_parts)
    w_gate, w_value, w_down = (feed_full(feed_parts_all[:, i]) for i in range(3))

    def pick(p):
        first = lax.dynamic_index_in_dim(p, here, 0, False)
        second = lax.dynamic_index_in_dim(p, extra_here, 0, False)
        return first, jnp.where(has_extra, second, jnp.zeros_like(second))

    def pick_vector(p):
        return jnp.concatenate(pick(p.astype(F32).reshape(heads, blk)))

    def pick_square(p):
        first, second = pick(p)
        return jnp.pad(first, ((0, blk), (0, blk))) + jnp.pad(second, ((blk, 0), (blk, 0)))

    taps = [pick_vector(conv_taps[k]) for k in range(4)]
    c_bias, r_bias, i_bias = (pick_vector(p) for p in (conv_bias, reset_bias, input_bias))
    decay_float = pick_vector(decay_param)
    r_square, i_square = pick_square(reset_weight), pick_square(input_weight)

    flags = lax.all_gather(
        start_flags.astype(F32), AXIS, axis_index_groups=groups, tiled=True
    )
    side_tok = SIDE * tok
    seg_tok = side_tok // 2
    starts = flags.reshape(side_tok, 1)
    keep = 1.0 - starts
    keep_seg = keep.reshape(2, seg_tok, 1)

    gain_one = to_near(norm_gain.astype(F32), me)
    gain_two = to_near(feed_norm_gain.astype(F32), me)
    x = to_near(block_input, me)
    top = to_near(output_grad, me)

    def canonical(blocks):
        buf = jnp.zeros((SIDE * blocks[0].shape[0], blocks[0].shape[1]), blocks[0].dtype)
        for j, b in enumerate(blocks):
            buf = lax.dynamic_update_slice(buf, b, ((here ^ j) * b.shape[0], 0))
        return buf

    def uncanonical(v):
        return [lax.dynamic_slice_in_dim(v, (here ^ j) * tok, tok, 0) for j in range(SIDE)]

    def blocks_of(v):
        return [v[j * tok : (j + 1) * tok] for j in range(SIDE)]

    scale_one = rms_scale(x)
    normed = (x * scale_one * gain_one).astype(BF16)
    normed_all = canonical(gather_side(normed))
    top_low = top.astype(BF16)
    top_all = jnp.concatenate(gather_side(top_low))

    linear = dot_last(normed_all, linear_t)
    gate_pre = dot_last(normed_all, gate_t)
    cw = linear.shape[1]
    lin_seg = linear.reshape(2, seg_tok, cw)
    k_last = keep_seg[:, seg_tok - 1 :]
    k_mid = k_last * keep_seg[:, seg_tok - 2 : seg_tok - 1]
    tail_keep = jnp.concatenate([k_mid, k_last, jnp.ones_like(k_last)], axis=1)
    tails = lin_seg[:, -3:] * tail_keep
    in_y = (me & YBIT) != 0
    tails_y = swap(tails, YBIT)
    fore = [(i - HBIT + YBIT, i) for i in range(HBIT, n) if i & YBIT == 0]
    back = [(b, a) for a, b in fore]
    tails_h = lax.ppermute(tails[1], AXIS, fore)
    halo = jnp.stack(
        [jnp.where(in_y, tails_y[0], tails_h), jnp.where(in_y, tails_y[1], tails_y[0])]
    )
    ext = jnp.concatenate([halo, lin_seg], axis=1)
    one_col = jnp.ones((2, 3, 1), F32)
    keep_ext = jnp.concatenate([one_col, keep_seg], axis=1)

    def behind(v, k):
        return v[:, 3 - k : 3 - k + seg_tok]

    same, running = [], None
    for k in range(3):
        running = behind(keep_ext, k) if running is None else running * behind(keep_ext, k)
        same.append(running)
    conv = lin_seg * taps[0] + c_bias
    for k in range(1, 4):
        conv = conv + behind(ext, k) * taps[k] * same[k - 1]
    conv_low = conv.astype(BF16).reshape(side_tok, cw)
    conv_value = conv_low.astype(F32)
    reset_gate = jax.nn.sigmoid(dot(conv_low, r_square) + r_bias)
    input_gate = jax.nn.sigmoid(dot(conv_low, i_square) + i_bias)
    soft_rate = jax.nn.softplus(-decay_float)
    decay = jnp.exp(-8.0 * reset_gate * soft_rate) * keep
    root = jnp.sqrt(1.0 - decay * decay + ROOT_GUARD)
    multiplier = keep * root + starts
    driven = multiplier * input_gate * conv_value
    decay_acc, local_states = run_scan(scan_kernel, decay, driven)

    here_far = [(me >> 2) & 1, me >> 4]

    def chain(scale_part, value_part, reverse):
        pair = jnp.stack([scale_part, value_part])
        found = jnp.stack(gather_far(pair))
        found = found.reshape(2, high, 2, 2, cw)
        found = flips(found, me, 0, 1)
        found = found.transpose(2, 1, 3, 0, 4).reshape(2, 4 * high, cw)
        order = range(4 * high - 1, -1, -1) if reverse else range(4 * high)
        state, incoming = jnp.zeros((cw,), F32), [None] * (4 * high)
        for g in order:
            incoming[g] = state
            state = found[0, g] * state + found[1, g]
        incoming = jnp.stack(incoming).reshape(high, 2, 2, cw)
        return incoming[here_far[1], :, here_far[0]]

    acc_seg = decay_acc.reshape(2, seg_tok, cw)
    loc_seg = local_states.reshape(2, seg_tok, cw)
    incoming = chain(acc_seg[:, -1], loc_seg[:, -1], False)
    states_seg = loc_seg + acc_seg * incoming[:, None]
    states = states_seg.reshape(side_tok, cw)
    gate_act, gate_slope = gelu_pair(gate_pre)
    mixed = (states * gate_act).astype(BF16)
    middle = x + scatter_side(uncanonical(dot(mixed, out_t)))

    scale_two = rms_scale(middle)
    normed_two = (middle * scale_two * gain_two).astype(BF16)
    two_all = jnp.concatenate(gather_side(normed_two))
    inner_gate = dot(two_all, w_gate)
    inner_value = dot(two_all, w_value)
    grad_hidden = dot(top_all, w_down)
    feed_act, feed_slope = gelu_pair(inner_gate)
    hidden = (feed_act * inner_value).astype(BF16)
    grad_ig = (grad_hidden * inner_value * feed_slope).astype(BF16)
    grad_iv = (grad_hidden * feed_act).astype(BF16)
    grad_normed_two = scatter_side(
        blocks_of(dot_last(grad_ig, w_gate) + dot_last(grad_iv, w_value))
    )
    block_output = middle + scatter_side(blocks_of(dot_last(hidden, w_down)))
    grad_gain_two = jnp.sum(grad_normed_two * middle * scale_two, axis=0)
    grad_middle = top + norm_back(grad_normed_two, middle, scale_two, gain_two)
    grad_branch = grad_middle.astype(BF16)
    branch_all = canonical(gather_side(grad_branch))

    def feed_grad(g):
        shard = scatter_far(g, 0).astype(BF16).reshape(SIDE, rows_w, fs)
        return exchange(shard).transpose(1, 0, 2).reshape(rows_w, feed).astype(F32)

    grad_w_gate = feed_grad(dot_first(two_all, grad_ig))
    grad_w_value = feed_grad(dot_first(two_all, grad_iv))
    grad_w_down = feed_grad(dot_first(top_all, hidden))

    grad_mixed = dot_last(branch_all, out_t)
    grad_gate_pre = (grad_mixed * states * gate_slope).astype(BF16)
    suffix, local_grads = run_scan(back_scan_kernel, decay, grad_mixed * gate_act)
    suf_seg = suffix.reshape(2, seg_tok, cw)
    lg_seg = local_grads.reshape(2, seg_tok, cw)
    first_decay = decay.reshape(2, seg_tok, cw)[:, 0]
    from_right = chain(first_decay * suf_seg[:, 0], first_decay * lg_seg[:, 0], True)
    grad_states = (lg_seg + suf_seg * from_right[:, None]).reshape(side_tok, cw)
    prior = jnp.concatenate([incoming[:, None], states_seg[:, :-1]], axis=1).reshape(side_tok, cw)
    grad_log = decay * (
        grad_states * prior - grad_states * input_gate * conv_value * decay / root
    )
    grad_decay = jnp.sum(8.0 * reset_gate * grad_log, axis=0) * jax.nn.sigmoid(-decay_float)
    grad_reset_pre = (-8.0 * soft_rate * grad_log * reset_gate * (1.0 - reset_gate)).astype(BF16)
    grad_input_pre = (
        grad_states * multiplier * conv_value * input_gate * (1.0 - input_gate)
    ).astype(BF16)
    grad_conv = (
        grad_states * multiplier * input_gate
        + dot_last(grad_reset_pre, r_square)
        + dot_last(grad_input_pre, i_square)
    )
    grad_r_bias = jnp.sum(grad_reset_pre.astype(F32), axis=0)
    grad_i_bias = jnp.sum(grad_input_pre.astype(F32), axis=0)
    gc_seg = grad_conv.reshape(2, seg_tok, cw)
    grad_c_bias = jnp.sum(grad_conv, axis=0)
    grad_taps = [jnp.sum(gc_seg * lin_seg, axis=(0, 1))]
    for k in range(1, 4):
        grad_taps.append(jnp.sum(gc_seg * behind(ext, k) * same[k - 1], axis=(0, 1)))
    h0 = keep_seg[:, 0:1]
    h1 = h0 * keep_seg[:, 1:2]
    h2 = h1 * keep_seg[:, 2:3]
    head_rows = gc_seg[:, :3] * jnp.concatenate([h0, h1, h2], axis=1)
    heads_y = swap(head_rows, YBIT)
    heads_h = lax.ppermute(head_rows[0], AXIS, back)
    after = jnp.stack(
        [jnp.where(in_y, heads_y[1], heads_y[0]), jnp.where(in_y, heads_h, heads_y[1])]
    )
    gc_ext = jnp.concatenate([gc_seg, after], axis=1)
    keep_after = jnp.concatenate([keep_seg, one_col], axis=1)
    grad_linear = gc_seg * taps[0]
    running = None
    for k in range(1, 4):
        ahead = keep_after[:, k : k + seg_tok]
        running = ahead if running is None else running * ahead
        grad_linear = grad_linear + gc_ext[:, k : k + seg_tok] * taps[k] * running
    grad_linear_low = grad_linear.astype(BF16).reshape(side_tok, cw)
    grad_normed = scatter_side(
        uncanonical(dot(grad_gate_pre, gate_t) + dot(grad_linear_low, linear_t))
    )
    grad_gain_one = jnp.sum(grad_normed * x * scale_one, axis=0)
    input_grad = grad_middle + norm_back(grad_normed, x, scale_one, gain_one)

    def mixer_shard(g):
        first = scatter_far(g[:blk], 1)
        second = scatter_far(g[blk:], 1, only)
        both = jnp.concatenate([first, second], axis=0).astype(BF16)
        return both.T.reshape(SIDE, rows_w, 2 * blk)

    def mixer_out(v):
        first = v[:, :, :blk].transpose(1, 0, 2).reshape(rows_w, SIDE * blk)
        return jnp.concatenate([first] + [v[s, :, blk:] for s in EXTRA], axis=1).astype(F32)

    grad_w_out = mixer_out(exchange(mixer_shard(dot_first(mixed, branch_all))))
    grad_w_mix = exchange(
        jnp.stack(
            [
                mixer_shard(dot_first(grad_gate_pre, normed_all)),
                mixer_shard(dot_first(grad_linear_low, normed_all)),
            ],
            axis=1,
        )
    )

    def head_squares(slot):
        sl = slice(slot * blk, (slot + 1) * blk)
        squares = jnp.concatenate(
            [
                dot_first(conv_low[:, sl], grad_reset_pre[:, sl]),
                dot_first(conv_low[:, sl], grad_input_pre[:, sl]),
            ],
            axis=1,
        )
        vectors = [grad_r_bias, grad_i_bias, grad_decay, grad_c_bias] + grad_taps
        vectors = jnp.stack([v[sl] for v in vectors]).reshape(4, 2 * blk)
        return jnp.concatenate([squares, vectors])

    def total_far(v, only=None):
        for m in far_masks():
            low = v.astype(BF16)
            v = low.astype(F32) + swap(low, m, only).astype(F32)
        return v.astype(BF16)

    first = canonical(gather_side_rows(total_far(head_squares(0))))
    second = total_far(head_squares(1), only)
    second = canonical(gather_side_rows(second))
    pack = blk + 4
    first = first.reshape(SIDE, -1, 2 * blk)
    second = second.reshape(SIDE, -1, 2 * blk)[jnp.array(only)]
    packs = jnp.concatenate([first, second])[:, :pack].astype(F32)
    grad_r_weight, grad_i_weight = packs[:, :blk, :blk], packs[:, :blk, blk:]
    vec = packs[:, blk:].reshape(heads, 8, blk).transpose(1, 0, 2).reshape(8, heads * blk)

    gains = jnp.stack([from_near(grad_gain_one, me), from_near(grad_gain_two, me)])
    gains = gains.reshape(-1, 256)
    for m in [CORE, XBIT, LBIT] + far_masks():
        gains = gains + swap(gains, m)
    gains = gains.reshape(2, width)

    return (
        from_near(block_output, me),
        from_near(input_grad, me),
        gains[0],
        mixer_out(grad_w_mix[:, 0]),
        mixer_out(grad_w_mix[:, 1]),
        vec[4:],
        vec[3],
        grad_r_weight,
        vec[0],
        grad_i_weight,
        vec[1],
        vec[2],
        grad_w_out,
        gains[1],
        grad_w_gate,
        grad_w_value,
        grad_w_down,
    )


def gather_side_rows(v):
    rows = v.shape[0]
    full = -(-rows // 32) * 32
    return gather_side(jnp.pad(v, ((0, full - rows), (0, 0))))


def solution(mesh):
    split, whole = P(AXIS, None), P()
    in_specs = (split, P(AXIS), whole, split, split) + (whole,) * 7
    in_specs += (split, whole, split, split, split, split)
    out_specs = (split, split, whole, split, split) + (whole,) * 7
    out_specs += (split, whole, split, split, split)
    return jax.shard_map(body, mesh=mesh, in_specs=in_specs, out_specs=out_specs, check_vma=False)
```

```python
import functools

import jax
import jax.numpy as jnp
from jax import lax
from jax.experimental import pallas as pl
from jax.experimental.pallas import tpu as pltpu
from jax.sharding import PartitionSpec as P

AXIS = "seq"
ROOT_GUARD = 0.001
F32, BF16 = jnp.float32, jnp.bfloat16
SIDE = 8
XBIT, CBIT = 2, 1
EXTRA = {0: 8, 6: 9}
SLOT = 288
CW = 640
HALO = 16
SHORT_ROW = 2048
UNROLL = 4


def lbit(n):
    return 8 if n == 32 else 4


def far_masks(n):
    masks, m = [], n // 2
    while m >= 4:
        if m != lbit(n):
            masks.append(m)
        m //= 2
    return masks


def row_span(n, tok):
    return SHORT_ROW // tok if n * tok == 2 * SHORT_ROW else n


def side_mask(q, n):
    return (q & 1) * XBIT | ((q >> 1) & 1) * lbit(n) | ((q >> 2) & 1) * CBIT


def side_place(d, n):
    x = (d >> (XBIT.bit_length() - 1)) & 1
    l = (d >> (lbit(n).bit_length() - 1)) & 1
    return x + l * 2 + ((d >> (CBIT.bit_length() - 1)) & 1) * 4


def side_code(i, n):
    return (i & 3) | (((i & lbit(n)) != 0) * 4)


def side_groups(n):
    low = XBIT | CBIT | lbit(n)
    return [
        sorted(b | side_mask(q, n) for q in range(SIDE)) for b in range(n) if b & low == 0
    ]


def far_groups(n):
    low = XBIT | CBIT | lbit(n)
    return [[i for i in range(n) if i & low == side_mask(q, n)] for q in range(SIDE)]


def far_mask_of(r, n):
    return sum(m for k, m in enumerate(far_masks(n)) if (r >> k) & 1)


def near_units(n, me):
    low = 2 if lbit(n) == 8 else 3
    units = []
    for r in range(n // SIDE):
        for l in range(SIDE >> low):
            u = 0
            for k, m in enumerate(far_masks(n)):
                bit = lax.shift_right_logical(me, m.bit_length() - 1) & 1
                u = u + ((bit ^ ((r >> k) & 1)) << (m.bit_length() - 1 - low))
            units.append(u + (l << (lbit(n).bit_length() - 1 - low) if low == 2 else 0))
    return units


def fixed_units(n):
    low = 2 if lbit(n) == 8 else 3
    base = [g[0] for g in side_groups(n)]
    return [
        (b | (l * lbit(n) if low == 2 else 0)) >> low for b in base for l in range(SIDE >> low)
    ]


def swap(v, mask, only=None):
    n = lax.axis_size(AXIS)
    pairs = [(i, i ^ mask) for i in range(n) if only is None or side_code(i, n) in only]
    return lax.ppermute(v, AXIS, pairs)


def dot(a, b):
    return lax.dot_general(a, b, (((1,), (0,)), ((), ())), preferred_element_type=F32)


def dot_last(a, b):
    return lax.dot_general(a, b, (((1,), (1,)), ((), ())), preferred_element_type=F32)


def dot_first(a, b):
    return lax.dot_general(a, b, (((0,), (0,)), ((), ())), preferred_element_type=F32)


def after(v, *deps):
    return lax.optimization_barrier((v, *deps))[0]


def kernel_call(kernel, ins, outs, scratch=(), smem=1, us=3):
    specs = [pl.BlockSpec(memory_space=pltpu.SMEM)] * smem
    specs += [pl.BlockSpec(memory_space=pltpu.VMEM)] * (len(ins) - smem)
    return pl.pallas_call(
        kernel,
        in_specs=specs,
        out_specs=[pl.BlockSpec(memory_space=pltpu.VMEM)] * len(outs),
        out_shape=[jax.ShapeDtypeStruct(s, d) for s, d in outs],
        scratch_shapes=list(scratch),
        compiler_params=pltpu.CompilerParams(vmem_limit_bytes=60 * 1024 * 1024),
        cost_estimate=pl.CostEstimate(
            flops=us * 10**9, bytes_accessed=us * 3 * 10**6, transcendentals=0
        ),
    )(*ins)


def gather_side(x, main=None, marks=(None, None)):
    n = lax.axis_size(AXIS)
    half = x.shape[0] // 32 * 16
    by_l, by_x = swap(x, lbit(n)), swap(x, XBIT)
    if marks[0] is not None:
        by_l, by_x = after((by_l, by_x), marks[0])
    low, high = swap(by_l[:half], XBIT), swap(by_x[half:], lbit(n))
    if marks[1] is not None:
        low, high = after((low, high), marks[1])
    if main is None:
        mine = jnp.concatenate([x, by_x, by_l, low, high])
        return mine, swap(mine, CBIT)
    cut = main - half
    mine = jnp.concatenate([x[:main], by_x[:main], by_l[:main], low, high[:cut]])
    rest = jnp.concatenate([x[main:], by_x[main:], by_l[main:], high[cut:]])
    return mine, swap(mine, CBIT), rest, swap(rest, CBIT)


def first_sum_kernel(mine, recv, send_a, send_b, keep_a, keep_b):
    tok, half = mine.shape[0] // 4, mine.shape[1] // 2
    step = 16

    def tile(i, _):
        for b in range(4):
            rows = pl.ds(pl.multiple_of(b * tok + i * step, step), step)
            at = lambda k: pl.ds(pl.multiple_of(k * tok + i * step, step), step)
            va = mine[rows, :half] + recv[rows, :half].astype(F32)
            vb = mine[rows, half:] + recv[rows, half:].astype(F32)
            if b < 2:
                keep_a[at(b), :] = va
            else:
                send_a[at(b - 2), :] = va.astype(BF16)
            if b % 2 == 0:
                keep_b[at(b // 2), :] = vb
            else:
                send_b[at(b // 2), :] = vb.astype(BF16)
        return 0

    lax.fori_loop(0, tok // step, tile, 0)


def second_sum_kernel(keep_a, recv_a, keep_b, recv_b, send_a, send_b, last):
    tok, half = send_a.shape
    step = 16

    def tile(i, _):
        own = pl.ds(pl.multiple_of(i * step, step), step)
        far = pl.ds(pl.multiple_of(tok + i * step, step), step)
        last[own, :half] = keep_a[own, :] + recv_a[own, :].astype(F32)
        last[own, half:] = keep_b[own, :] + recv_b[own, :].astype(F32)
        send_a[own, :] = (keep_a[far, :] + recv_a[far, :].astype(F32)).astype(BF16)
        send_b[own, :] = (keep_b[far, :] + recv_b[far, :].astype(F32)).astype(BF16)
        return 0

    lax.fori_loop(0, tok // step, tile, 0)


def scatter_side(mine, theirs, mark=None, mark_last=None):
    n = lax.axis_size(AXIS)
    rows, width = mine.shape
    tok, half = rows // 4, width // 2
    recv = swap(theirs, CBIT)
    send_a, send_b, keep_a, keep_b = kernel_call(
        first_sum_kernel,
        (mine, recv),
        [((2 * tok, half), BF16)] * 2 + [((2 * tok, half), F32)] * 2,
        smem=0,
    )
    recv_a, recv_b = swap(send_a, lbit(n)), swap(send_b, XBIT)
    if mark is not None:
        keep_a = after(keep_a, mark)
    send_a, send_b, last = kernel_call(
        second_sum_kernel,
        (keep_a, recv_a, keep_b, recv_b),
        [((tok, half), BF16)] * 2 + [((tok, width), F32)],
        smem=0,
    )
    parts = (last, swap(send_a, XBIT), swap(send_b, lbit(n)))
    if mark_last is not None:
        parts = after(parts, mark_last)
    return parts, keep_a, last


def rms_scale(values):
    return lax.rsqrt(jnp.mean(values * values, axis=-1, keepdims=True) + 1e-06)


def unit_slice(u, size):
    return pl.ds(pl.multiple_of(u * size, 128), size)


def put_units(out, rows, value_ref, value_rows, units, size):
    for p, u in enumerate(units):
        out[rows, p * size : (p + 1) * size] = value_ref[value_rows, unit_slice(u, size)]


def tail_kernel(x, gain, flags, out):
    v = x[...]
    out[...] = (v * rms_scale(v) * gain[...]).astype(BF16)
    row = lax.broadcasted_iota(jnp.int32, (HALO, 128), 0) == 0
    out[:, :128] = jnp.where(row, flags[...], out[:, :128].astype(F32)).astype(BF16)


ROWS = 32


def norm_one_kernel(n, me, x, gain, flags, tail, out, held):
    units = near_units(n, me[0])
    size = x.shape[1] // len(units)
    tok = x.shape[0]
    for i in range(tok // ROWS):
        rows = slice(i * ROWS, (i + 1) * ROWS)
        v = x[rows, :]
        held[...] = v * rms_scale(v) * gain[...]
        for p, u in enumerate(units):
            out[rows, p * size : (p + 1) * size] = held[:, unit_slice(u, size)].astype(BF16)
    halo = slice(tok, tok + HALO)
    put_units(out, halo, tail, slice(0, HALO), units, size)
    row = lax.broadcasted_iota(jnp.int32, (HALO, 128), 0)
    first = out[halo, :128].astype(F32)
    both = jnp.where(row == 0, flags[...], first)
    both = jnp.where(row == 1, tail[:, :128].astype(F32)[0:1], both)
    out[halo, :128] = both.astype(BF16)


def top_kernel(n, g, out):
    units = fixed_units(n)
    size = g.shape[1] // len(units)
    for p, u in enumerate(units):
        out[:, p * size : (p + 1) * size] = g[:, u * size : (u + 1) * size].astype(BF16)


def summed(last, ra, rb, rows, p, size):
    half = ra.shape[1]
    a, b = p * size, (p + 1) * size
    if b <= half:
        extra = ra[rows, a:b]
    else:
        extra = rb[rows, a - half : b - half]
    return last[rows, a:b] + extra.astype(F32)


def norm_two_kernel(n, me, x, gain, last, ra, rb, middle, out, held):
    units = near_units(n, me[0])
    size = x.shape[1] // len(units)
    for i in range(x.shape[0] // ROWS):
        rows = slice(i * ROWS, (i + 1) * ROWS)
        for p, u in enumerate(units):
            held[:, unit_slice(u, size)] = summed(last, ra, rb, rows, p, size)
        v = held[...] + x[rows, :]
        middle[rows, :] = v
        w = (v * rms_scale(v) * gain[...]).astype(BF16)
        for p, u in enumerate(fixed_units(n)):
            out[rows, p * size : (p + 1) * size] = w[:, u * size : (u + 1) * size]


def add_kernel(n, middle, last, ra, rb, out):
    units = fixed_units(n)
    size = middle.shape[1] // len(units)
    for p, u in enumerate(units):
        at = slice(u * size, (u + 1) * size)
        out[:, at] = middle[:, at] + summed(last, ra, rb, slice(None), p, size)


def norm_back(grad_normed, values, gain):
    scale = rms_scale(values)
    scaled = grad_normed * gain
    back = scale * scaled - values * (scale * scale * scale) * jnp.mean(
        scaled * values, axis=-1, keepdims=True
    )
    return back, grad_normed * values * scale


def middle_back_kernel(n, me, values, base, gain, last, ra, rb, grad, branch, gain_grad, held):
    units = near_units(n, me[0])
    size = values.shape[1] // len(units)
    total = jnp.zeros((1, values.shape[1]), F32)
    for i in range(values.shape[0] // ROWS):
        rows = slice(i * ROWS, (i + 1) * ROWS)
        for p, u in enumerate(fixed_units(n)):
            held[:, u * size : (u + 1) * size] = summed(last, ra, rb, rows, p, size)
        back, part = norm_back(held[...], values[rows, :], gain[...])
        total = total + jnp.sum(part, axis=0, keepdims=True)
        out = base[rows, :] + back
        grad[rows, :] = out
        held[...] = out
        for p, u in enumerate(units):
            branch[rows, p * size : (p + 1) * size] = held[:, unit_slice(u, size)].astype(BF16)
    gain_grad[...] = total


def input_back_kernel(n, me, values, base, gain, last, ra, rb, grad, gain_grad, held):
    units = near_units(n, me[0])
    size = values.shape[1] // len(units)
    total = jnp.zeros((1, values.shape[1]), F32)
    for i in range(values.shape[0] // ROWS):
        rows = slice(i * ROWS, (i + 1) * ROWS)
        for p, u in enumerate(units):
            held[:, unit_slice(u, size)] = summed(last, ra, rb, rows, p, size)
        back, part = norm_back(held[...], values[rows, :], gain[...])
        total = total + jnp.sum(part, axis=0, keepdims=True)
        grad[rows, :] = base[rows, :] + back
    gain_grad[...] = total


def gelu_pair(v):
    k = 0.7978845608028654
    sq = v * v
    th = jnp.tanh(k * v * (1.0 + 0.044715 * sq))
    half = 0.5 * (1.0 + th)
    slope = half + 0.5 * v * (1.0 - th * th) * (k * (1.0 + 3.0 * 0.044715 * sq))
    return v * half, slope


def strided(i, tok):
    return pl.ds(i, SIDE, stride=tok)


TILES = CW // 128


def cols(c):
    return slice(c * 128, (c + 1) * 128)


def join(tiles):
    return jnp.concatenate(tiles, axis=1)


def stepwise(tok, step, state, reverse=False):
    def some(o, state):
        for k in range(UNROLL):
            i = o * UNROLL + k
            state = step(tok - 1 - i if reverse else i, state)
        return state

    return lax.fori_loop(0, tok // UNROLL, some, state)


def step_rows(i):
    return pl.ds(pl.multiple_of(i * SIDE, SIDE), SIDE)


def mixer_kernel(
    lin_mine, lin_theirs, halo, keep, halo_keep, taps, r_sq, i_sq, vec,
    lin, low, rg, ig, dec, acc, loc, before, totals, conv,
):
    tok = conv.shape[1] // SIDE
    four = 4 * tok
    for c in range(TILES):
        lin[c, :four, :] = lin_mine[:, CW + c * 128 : CW + (c + 1) * 128]
        lin[c, four:, :] = lin_theirs[:, CW + c * 128 : CW + (c + 1) * 128]
        conv[c, : SIDE * HALO, :] = halo[:, cols(c)]
        for k in range(3):
            before[c, k * SIDE : (k + 1) * SIDE, :] = conv[c, strided(HALO - 1 - k, HALO), :]

    for c in range(TILES):
        t0, t1, t2, t3 = (taps[k : k + 1, cols(c)] for k in range(4))
        bias = vec[0:1, cols(c)]

        def conv_step(i, state):
            v1, v2, v3, k1, k2 = state
            v0 = lin[c, strided(i, tok), :]
            k0 = keep[step_rows(i), :]
            conv[c, strided(i, tok), :] = (
                v0 * t0 + bias + k0 * (v1 * t1 + k1 * (v2 * t2 + k2 * (v3 * t3)))
            )
            return v0, v1, v2, k0, k1

        start = tuple(before[c, k * SIDE : (k + 1) * SIDE, :] for k in range(3))
        start += (halo_keep[2 * SIDE :, :], halo_keep[SIDE : 2 * SIDE, :])
        stepwise(tok, conv_step, start)

    def gates(b, _):
        rows = pl.ds(pl.multiple_of(b * tok, tok), tok)
        low_here = join([conv[c, rows, :].astype(BF16) for c in range(TILES)])
        low[rows, :] = low_here
        r = jax.nn.sigmoid(dot(low_here, r_sq[...]) + vec[1:2, :])
        i = jax.nn.sigmoid(dot(low_here, i_sq[...]) + vec[2:3, :])
        for c in range(TILES):
            conv[c, rows, :] = low_here[:, cols(c)].astype(F32)
            rg[c, rows, :] = r[:, cols(c)]
            ig[c, rows, :] = i[:, cols(c)]
        return 0

    lax.fori_loop(0, SIDE, gates, 0)

    def scan_step(i, state):
        at = strided(i, tok)
        k0 = keep[step_rows(i), :]
        out = []
        for c in range(TILES):
            p, s = state[c]
            a = jnp.exp(rg[c, at, :] * vec[3:4, cols(c)]) * k0
            root = jnp.sqrt(1.0 - a * a + ROOT_GUARD)
            b = (k0 * root + (1.0 - k0)) * ig[c, at, :] * conv[c, at, :]
            p, s = p * a, a * s + b
            dec[c, at, :] = a
            acc[c, at, :] = p
            loc[c, at, :] = s
            out.append((p, s))
        return tuple(out)

    shape = (SIDE, 128)
    start = tuple((jnp.ones(shape, F32), jnp.zeros(shape, F32)) for _ in range(TILES))
    found = stepwise(tok, scan_step, start)
    for c in range(TILES):
        totals[:SIDE, cols(c)], totals[SIDE:, cols(c)] = found[c]


def gelu_kernel(gate_mine, gate_theirs, act, slope):
    four = gate_mine.shape[0]

    def tile(i, _):
        rows = pl.ds(pl.multiple_of(i * 16, 16), 16)
        later = pl.ds(pl.multiple_of(four + i * 16, 16), 16)
        for src, dst in ((gate_mine, rows), (gate_theirs, later)):
            for c in range(TILES):
                act[c, dst, :], slope[c, dst, :] = gelu_pair(src[rows, cols(c)])
        return 0

    lax.fori_loop(0, four // 16, tile, 0)


def chain_kernel(n, span, reverse, me_ref, *refs):
    *parts, out, held = refs
    me = me_ref[0]
    state = jnp.zeros((1, CW), F32)
    order = range(span - 1, -1, -1) if reverse else range(span)
    near = [m for m in far_masks(n) if m < span]

    def place(d):
        r = 0
        for k, m in enumerate(near):
            r = r + (((d >> (m.bit_length() - 1)) & 1) << k)
        return r, side_place(d, n)

    both = 2 * SIDE
    for r, part in enumerate(parts):
        for k in range(both):
            held[r * both + k, 0:1, :] = part[k : k + 1, :]
    base = len(parts) * both
    for i in order:
        r, q = place((me & (span - 1)) ^ i)
        held[base + i, 0:1, :] = state
        scale = held[r * both + q, 0:1, :]
        value = held[r * both + SIDE + q, 0:1, :]
        state = scale * state + value
    for q in range(SIDE):
        at = base + ((me & (span - 1)) ^ side_mask(q, n))
        out[q, :, :] = jnp.broadcast_to(held[at, 0:1, :], (8, CW))


def states_kernel(acc, loc, incoming, act, slope, states, mixed, slope_states):
    tok = acc.shape[1] // SIDE
    for q in range(SIDE):

        def tile(i, _):
            rows = pl.ds(pl.multiple_of(q * tok + i * 16, 16), 16)
            out = []
            for c in range(TILES):
                s = loc[c, rows, :] + acc[c, rows, :] * incoming[q, 0:1, cols(c)]
                states[c, rows, :] = s
                slope_states[c, rows, :] = s * slope[c, rows, :]
                out.append((s * act[c, rows, :]).astype(BF16))
            mixed[rows, :] = join(out)
            return 0

        lax.fori_loop(0, tok // 16, tile, 0)


def back_scan_kernel(gm_mine, gm_theirs, act, dec, grads, suffix, totals):
    tok = act.shape[1] // SIDE
    four = 4 * tok
    for c in range(TILES):
        grads[c, :four, :] = gm_mine[:, cols(c)] * act[c, :four, :]
        grads[c, four:, :] = gm_theirs[:, cols(c)] * act[c, four:, :]

    def step(i, state):
        at = strided(i, tok)
        out = []
        for c in range(TILES):
            ag, aq = state[c]
            g = grads[c, at, :] + ag
            grads[c, at, :] = g
            suffix[c, at, :] = aq
            a = dec[c, at, :]
            out.append((a * g, a * aq))
        return tuple(out)

    shape = (SIDE, 128)
    start = tuple((jnp.zeros(shape, F32), jnp.ones(shape, F32)) for _ in range(TILES))
    found = stepwise(tok, step, start, True)
    for c in range(TILES):
        totals[SIDE:, cols(c)], totals[:SIDE, cols(c)] = found[c]


def gate_back_kernel(gm_mine, gm_theirs, slope_states, out):
    four = gm_mine.shape[0]

    def tile(i, _):
        rows = pl.ds(pl.multiple_of(i * 16, 16), 16)
        later = pl.ds(pl.multiple_of(four + i * 16, 16), 16)
        for src, dst in ((gm_mine, rows), (gm_theirs, later)):
            out[dst, :] = join(
                [(src[rows, cols(c)] * slope_states[c, dst, :]).astype(BF16) for c in range(TILES)]
            )
        return 0

    lax.fori_loop(0, four // 16, tile, 0)


def mixer_back_kernel(
    grads, suffix, from_later, dec, rg, ig, low, states, incoming, lin, before, keep, halo_keep,
    keep_rows, r_sq, i_sq, vec, g_reset, g_input, g_conv, sums, heads,
):
    tok = dec.shape[1] // SIDE
    zero = jnp.zeros((1, 128), F32)

    def block(b, totals):
        rows = pl.ds(pl.multiple_of(b * tok, tok), tok)
        k = keep_rows[rows, :]
        at_first = lax.broadcasted_iota(jnp.int32, (tok, 128), 0) == 0
        out, g_rs, g_is, base = [], [], [], []
        for c in range(TILES):
            gs = grads[c, rows, :] + suffix[c, rows, :] * from_later[b, 0:1, cols(c)]
            a, r, i_g = dec[c, rows, :], rg[c, rows, :], ig[c, rows, :]
            v = low[rows, cols(c)].astype(F32)
            root = jnp.sqrt(1.0 - a * a + ROOT_GUARD)
            mult = k * root + (1.0 - k)
            prior = pltpu.roll(states[c, rows, :], 1, 0)
            prior = jnp.where(at_first, incoming[b, 0:1, cols(c)], prior)
            gv = gs * v
            glr = a * (gs * prior - gv * i_g * a / root) * r
            g_r = (vec[3:4, cols(c)] * glr * (1.0 - r)).astype(BF16)
            gm = gs * mult * i_g
            g_i = (gm * v * (1.0 - i_g)).astype(BF16)
            out.append(
                (
                    totals[c][0] + jnp.sum(glr, axis=0, keepdims=True),
                    totals[c][1] + jnp.sum(g_r.astype(F32), axis=0, keepdims=True),
                    totals[c][2] + jnp.sum(g_i.astype(F32), axis=0, keepdims=True),
                )
            )
            g_rs.append(g_r)
            g_is.append(g_i)
            g_conv[c, rows, :] = gm
        g_r, g_i = join(g_rs), join(g_is)
        g_reset[rows, :] = g_r
        g_input[rows, :] = g_i
        more = dot_last(g_r, r_sq[...]) + dot_last(g_i, i_sq[...])
        for c in range(TILES):
            g_conv[c, rows, :] = g_conv[c, rows, :] + more[:, cols(c)]
        return tuple(out)

    found = lax.fori_loop(0, SIDE, block, ((zero,) * 3,) * TILES)
    for c in range(TILES):
        dec_sum, r_sum, i_sum = found[c]
        sums[0:1, cols(c)] = r_sum
        sums[1:2, cols(c)] = i_sum
        sums[2:3, cols(c)] = -vec[4:5, cols(c)] * dec_sum

    blank = jnp.zeros((SIDE, 128), F32)
    for c in range(TILES):

        def tap_step(i, state):
            v1, v2, v3, k1, k2, s0, s1, s2, s3, sb = state
            v0 = lin[c, strided(i, tok), :]
            k0 = keep[step_rows(i), :]
            g0 = g_conv[c, strided(i, tok), :]
            g1 = g0 * k0
            g2 = g1 * k1
            g3 = g2 * k2
            return (
                (v0, v1, v2, k0, k1)
                + (s0 + g0 * v0, s1 + g1 * v1, s2 + g2 * v2, s3 + g3 * v3, sb + g0)
            )

        start = tuple(before[c, k * SIDE : (k + 1) * SIDE, :] for k in range(3))
        start += (halo_keep[2 * SIDE :, :], halo_keep[SIDE : 2 * SIDE, :]) + (blank,) * 5
        end = stepwise(tok, tap_step, start)
        per_row = [jnp.sum(v, axis=0, keepdims=True) for v in end[5:]]
        sums[3:4, cols(c)] = per_row[4]
        for j in range(4):
            sums[4 + j : 5 + j, cols(c)] = per_row[j]
        k = None
        for i in range(3):
            k_i = keep[i * SIDE : (i + 1) * SIDE, :]
            k = k_i if k is None else k * k_i
            heads[i * SIDE : (i + 1) * SIDE, cols(c)] = g_conv[c, strided(i, tok), :] * k


def linear_back_kernel(n, span, me_ref, g_conv, keep, taps, *refs):
    *parts, out, held, after, conv = refs
    me = me_ref[0]
    tok = g_conv.shape[1] // SIDE
    rows3 = 3 * SIDE
    for k, part in enumerate(parts):
        for m in range(rows3):
            held[k * rows3 + m, 0:1, :] = part[m : m + 1, :]
    low_far = far_masks(n)[-1]
    side = XBIT | CBIT | lbit(n)
    for q in range(SIDE):
        nxt = (me ^ side_mask(q, n)) + 1
        d = nxt ^ me
        far = d & ~side
        ok = ((nxt & (span - 1)) != 0).astype(F32)
        which = jnp.where(far == 0, 0, jnp.where(far == low_far, 1, len(parts) - 1))
        for m in range(3):
            at = which * rows3 + m * SIDE + side_place(d, n)
            after[m * SIDE + q : m * SIDE + q + 1, :] = held[at, 0:1, :] * ok
    one = jnp.ones((SIDE, 128), F32)
    for c in range(TILES):
        t0, t1, t2, t3 = (taps[k : k + 1, cols(c)] for k in range(4))

        def step(i, state):
            g1, g2, g3, k1, k2, k3 = state
            g0 = g_conv[c, strided(i, tok), :]
            conv[c, strided(i, tok), :] = g0 * t0 + k1 * (g1 * t1 + k2 * (g2 * t2 + k3 * (g3 * t3)))
            return g0, g1, g2, keep[step_rows(i), :], k1, k2

        start = tuple(after[m * SIDE : (m + 1) * SIDE, cols(c)] for m in range(3))
        stepwise(tok, step, start + (one, one, one), True)

    def tile(i, _):
        rows = pl.ds(pl.multiple_of(i * 16, 16), 16)
        out[rows, :] = join([conv[c, rows, :].astype(BF16) for c in range(TILES)])
        return 0

    lax.fori_loop(0, SIDE * tok // 16, tile, 0)


def heads_kernel(blk, gate, linear, out_w, first, second):
    first[...] = jnp.zeros(first.shape, BF16)
    second[...] = jnp.zeros(second.shape, BF16)
    for k, w in enumerate((gate, linear, out_w)):
        at = slice(k * SLOT, k * SLOT + blk)
        for s in range(SIDE):
            first[s, :, at] = w[:, s * blk : (s + 1) * blk]
        for s, e in EXTRA.items():
            second[s, :, at] = w[:, e * blk : (e + 1) * blk]


def feed_parts_kernel(*refs):
    *weights, out = refs
    rows, size = weights[0].shape[0], out.shape[2]
    for k, w in enumerate(weights):
        for s in range(SIDE):
            out[s, k * rows : (k + 1) * rows, :] = w[:, s * size : (s + 1) * size]


def feed_join_kernel(parts, out):
    size = parts.shape[2]
    for s in range(SIDE):
        out[:, s * size : (s + 1) * size] = parts[s, :, :].astype(F32)


def turn_kernel(parts, *outs):
    rows = parts.shape[1]
    turned = parts[...].reshape(SIDE * rows, parts.shape[2]).T
    at = 0
    for out in outs:
        out[...] = turned[at : at + out.shape[0]]
        at += out.shape[0]


def assemble_kernel(count, which, *refs):
    first, extra, out = refs[:count], refs[count : 2 * count], refs[2 * count]
    size = first[0].shape[1]
    for r in range(count):
        lanes = slice(r * size, (r + 1) * size)
        for m, k in enumerate(which):
            out[m * CW : m * CW + SLOT, lanes] = first[r][m * SLOT : (m + 1) * SLOT, :]
            out[m * CW + SLOT : m * CW + 2 * SLOT, lanes] = extra[r][k * SLOT : (k + 1) * SLOT, :]
            out[m * CW + 2 * SLOT : (m + 1) * CW, lanes] = jnp.zeros((CW - 2 * SLOT, size), BF16)


def turn_back_kernel(*refs):
    *parts, out = refs
    rows = out.shape[1]
    flat = jnp.concatenate([p[...] for p in parts])
    out[:, :, : flat.shape[0]] = flat.T.reshape(SIDE, rows, flat.shape[0])


def head_rows_kernel(blk, parts, *outs):
    count = len(outs)
    for k, out in enumerate(outs):
        for s in range(SIDE):
            at = k * SLOT
            out[:, s * blk : (s + 1) * blk] = parts[s, :, at : at + blk].astype(F32)
        for s, e in EXTRA.items():
            at = (count + k) * SLOT
            out[:, e * blk : (e + 1) * blk] = parts[s, :, at : at + blk].astype(F32)


def packs_kernel(n, blk, me_ref, mine, theirs, eight, nine, r_out, i_out, vec_out):
    me = me_ref[0]

    def put(ref, e, shift):
        def lanes(v):
            return v[:, shift : shift + blk]

        r_out[e, :, :] = lanes(ref[:SLOT, :384].astype(F32))[:blk]
        i_out[e, :, :] = lanes(ref[:SLOT, 384:].astype(F32))[:blk]
        vec_out[:, e * blk : (e + 1) * blk] = lanes(ref[SLOT:, :384].astype(F32)[:8])

    for s in range(SIDE):
        i = (s & 3) | ((s >> 2) * lbit(n))
        d = jnp.int32(i) ^ (me & (XBIT | CBIT | lbit(n)))
        q = ((d >> (XBIT.bit_length() - 1)) & 1) + ((d >> (lbit(n).bit_length() - 1)) & 1) * 2
        own = ((d >> (CBIT.bit_length() - 1)) & 1) == 0

        @pl.when(own)
        def _():
            put(mine.at[q], s, 0)

        @pl.when(jnp.logical_not(own))
        def _():
            put(theirs.at[q], s, 0)

    put(eight, EXTRA[0], 32)
    put(nine, EXTRA[6], 32)


def body(
    block_input,
    start_flags,
    norm_gain,
    gate_weight,
    linear_weight,
    conv_taps,
    conv_bias,
    reset_weight,
    reset_bias,
    input_weight,
    input_bias,
    decay_param,
    out_weight,
    feed_norm_gain,
    feed_gate_weight,
    feed_value_weight,
    feed_down_weight,
    output_grad,
):
    n = lax.axis_size(AXIS)
    me = lax.axis_index(AXIS)
    me1 = me.reshape(1)
    here = side_code(me, n)
    tok, width = block_input.shape
    heads_count, blk = reset_weight.shape[:2]
    rows_w = gate_weight.shape[0]
    feed = feed_gate_weight.shape[1]
    fs = feed // SIDE
    masks = far_masks(n)
    groups, far = side_groups(n), far_groups(n)
    only = tuple(EXTRA)
    has_extra = (here == only[0]) | (here == only[1])
    extra_here = jnp.where(here == only[1], EXTRA[only[1]], EXTRA[only[0]])
    four = 4 * tok
    side_tok = SIDE * tok
    cols_w = SIDE * rows_w
    places = n // SIDE
    count = len(masks)

    def exchange(v):
        return lax.all_to_all(v, AXIS, 0, 0, axis_index_groups=groups, tiled=True)

    def gather_far(x, sel=None):
        chunks = [x]
        for m in masks:
            chunks += [swap(c, m, sel) for c in chunks]
        return chunks

    gain_one = norm_gain.astype(F32)[None]
    gain_two = feed_norm_gain.astype(F32)[None]
    flags = start_flags.astype(F32)[None]
    parts, more_parts = kernel_call(
        functools.partial(heads_kernel, blk),
        (gate_weight, linear_weight, out_weight),
        [((SIDE, rows_w, 3 * SLOT + 32), BF16)] * 2,
        smem=0,
    )
    tail = kernel_call(
        tail_kernel,
        (after(block_input[-HALO:], parts), gain_one, flags),
        [((HALO, width), BF16)],
        smem=0,
        us=1,
    )[0]
    tail = lax.ppermute(tail, AXIS, [(i, i + 1) for i in range(n - 1)])
    packet = kernel_call(
        functools.partial(norm_one_kernel, n),
        (me1, block_input, gain_one, flags, tail),
        [((tok + HALO, width), BF16)],
        [pltpu.VMEM((ROWS, width), F32)],
    )[0]
    f_parts = kernel_call(
        feed_parts_kernel,
        (after(feed_gate_weight, packet), feed_value_weight, feed_down_weight),
        [((SIDE, 3 * rows_w, fs), BF16)],
        smem=0,
    )[0]
    top = kernel_call(
        functools.partial(top_kernel, n),
        (after(output_grad, f_parts),),
        [((tok, width), BF16)],
        smem=0,
    )[0]
    parts = exchange(parts)
    p_mix, p_out = kernel_call(
        turn_kernel, (parts,), [((k * SLOT, cols_w), BF16) for k in (2, 1)], smem=0
    )
    more_parts = exchange(after(more_parts, parts))
    f_parts = exchange(after(f_parts, more_parts))
    p_extra = kernel_call(turn_kernel, (more_parts,), [((3 * SLOT, cols_w), BF16)], smem=0)[0]

    def gather_start(x, count=2, sel=None):
        return [x] + [swap(x, m, sel) for m in masks[:count]]

    def gather_later(chunks, sel=None, mark=None):
        chunks = list(chunks)
        if mark is not None:
            chunks[1] = after(chunks[1], mark)
        if len(chunks) == 3:
            chunks.append(swap(chunks[1], masks[1], sel))
        for m in masks[len(chunks).bit_length() - 1 :]:
            chunks += [swap(c, m, sel) for c in chunks]
        return chunks

    packet = after(packet, p_mix)
    c_mix = gather_start(p_mix)
    half = tok // 2
    by_l, by_x = swap(packet, lbit(n)), swap(packet, XBIT)
    (c_mix, by_l, by_x, p_extra) = lax.optimization_barrier((c_mix, by_l, by_x, p_extra))
    c_mix = gather_later(c_mix)
    c_extra = gather_start(p_extra, 1, only)
    low, high = swap(by_l[:half], XBIT), swap(by_x[half:], lbit(n))
    (c_mix, c_extra, low, high, p_out) = lax.optimization_barrier(
        (c_mix, c_extra, low, high, p_out)
    )
    f_parts = after(f_parts, c_extra)
    c_extra = gather_later(c_extra, only)
    c_out = gather_start(p_out, 1)
    f_parts = f_parts.reshape(SIDE, 3, rows_w, fs)
    norm_mine = jnp.concatenate([packet[:tok], by_x[:tok], by_l[:tok], low, high[:half]])
    halo_mine = jnp.concatenate([packet[tok:], by_x[tok:], by_l[tok:], high[half:]])
    norm_theirs, halo_theirs = swap(norm_mine, CBIT), swap(halo_mine, CBIT)
    f_parts = [f_parts[:, k].reshape(cols_w, fs) for k in range(3)]
    w_mix = kernel_call(
        functools.partial(assemble_kernel, places, (0, 1)),
        (*c_mix, *c_extra),
        [((2 * CW, width), BF16)],
        smem=0,
        us=5,
    )[0]
    c_out = gather_later([after(p_out, w_mix), c_out[1]], mark=w_mix)
    w_mix = after(w_mix, tuple(f_parts))

    def feed_full(part):
        return lax.all_gather(part, AXIS, axis_index_groups=far, tiled=True)

    w_down, w_gate, w_value = (feed_full(f_parts[k]) for k in (2, 0, 1))

    def pick(p):
        one = lax.dynamic_index_in_dim(p, here, 0, False)
        two = lax.dynamic_index_in_dim(p, extra_here, 0, False)
        return one, jnp.where(has_extra, two, jnp.zeros_like(two))

    vectors = jnp.concatenate(
        [conv_taps]
        + [v[None] for v in (conv_bias, reset_bias, input_bias, decay_param)]
    ).astype(F32)
    vectors = vectors.reshape(8, heads_count, blk).transpose(1, 0, 2)
    vec_one, vec_two = pick(vectors)
    gap = ((0, 0), (0, SLOT - blk))
    vectors = jnp.concatenate([jnp.pad(vec_one, gap), jnp.pad(vec_two, gap)], axis=1)
    vectors = jnp.pad(vectors, ((0, 0), (0, CW - 2 * SLOT)))
    taps = vectors[:4]
    decay_float = vectors[7]
    vec = jnp.concatenate(
        [
            vectors[4:7],
            (-8.0 * jax.nn.softplus(-decay_float))[None],
            (-8.0 * jax.nn.sigmoid(-decay_float))[None],
            jnp.zeros((3, CW), F32),
        ]
    )

    def square(p):
        one, two = pick(p)
        low = CW - SLOT - blk
        return jnp.pad(one, ((0, CW - blk),) * 2) + jnp.pad(two, ((SLOT, low),) * 2)

    r_sq, i_sq = square(reset_weight), square(input_weight)

    halo_all = jnp.concatenate([halo_mine, halo_theirs])
    flag_rows = halo_all.reshape(SIDE, HALO, width)[:, :2, :128].astype(F32)
    keep_blocks = 1.0 - flag_rows[:, 0]
    keep = jnp.broadcast_to(keep_blocks.T[:, :, None], (tok, SIDE, 128)).reshape(side_tok, 128)
    keep_rows = jnp.broadcast_to(keep_blocks[:, :, None], (SIDE, tok, 128)).reshape(side_tok, 128)
    halo_keep = 1.0 - flag_rows[:, 1, tok - 3 :]
    halo_keep = jnp.broadcast_to(halo_keep.T[:, :, None], (3, SIDE, 128)).reshape(3 * SIDE, 128)

    pre_mine, pre_theirs = dot_last(norm_mine, w_mix), dot_last(norm_theirs, w_mix)
    halo = dot_last(halo_all, w_mix[CW:])
    top = after(top, w_mix)
    top_l, top_x = swap(top, lbit(n)), swap(top, XBIT)
    flat, wide = (side_tok, CW), (TILES, side_tok, 128)
    lin, low, rg, ig, dec, acc, loc, before, totals = kernel_call(
        mixer_kernel,
        (pre_mine, pre_theirs, halo, keep, halo_keep, taps, r_sq, i_sq, vec),
        [(wide, F32), (flat, BF16)]
        + [(wide, F32)] * 5
        + [((TILES, 3 * SIDE, 128), F32), ((2 * SIDE, CW), F32)],
        [pltpu.VMEM(wide, F32)],
        smem=0,
        us=29,
    )

    span = row_span(n, tok)

    def chain(totals, reverse, mark):
        near = [far_mask_of(r, n) for r in range(1, n // SIDE)]
        parts = [totals] + [swap(totals, m) for m in near if m < span]
        parts = after(tuple(parts), mark)
        return kernel_call(
            functools.partial(chain_kernel, n, span, reverse),
            (me1, *parts),
            [((SIDE, 8, CW), F32)],
            [pltpu.VMEM((len(parts) * 2 * SIDE + span, 8, CW), F32)],
            us=2,
        )[0]

    top_l, top_x = after((top_l, top_x), totals)
    top_low, top_high = swap(top_l[: tok // 2], XBIT), swap(top_x[tok // 2 :], lbit(n))
    gate_halves = after((pre_mine, pre_theirs), totals, top_l)
    act, slope = kernel_call(gelu_kernel, gate_halves, [(wide, F32)] * 2, smem=0, us=7)
    c_out, c_extra = after((tuple(c_out), tuple(c_extra)), act)
    w_out = kernel_call(
        functools.partial(assemble_kernel, places, (2,)),
        (*c_out, *c_extra),
        [((CW, width), BF16)],
        smem=0,
    )[0]
    incoming = chain(totals, False, w_out)
    top_mine = jnp.concatenate([top, top_x, top_l, top_low, top_high])
    incoming = after(incoming, top_low, top_high)
    states, mixed, slope_states = kernel_call(
        states_kernel,
        (acc, loc, incoming, act, slope),
        [(wide, F32), (flat, BF16), (wide, F32)],
        smem=0,
        us=8,
    )
    theirs = dot(mixed[four:], w_out).astype(BF16)
    mixed_mine = after(mixed[:four], theirs)
    parts, mark_one, mark_two = scatter_side(dot(mixed_mine, w_out), theirs)
    top_theirs = swap(after(top_mine, mark_one), CBIT)
    gh_mine = dot(after(top_mine, mark_one), w_down)
    parts = after(parts, gh_mine)
    held = pltpu.VMEM((ROWS, width), F32)
    middle, normed_two = kernel_call(
        functools.partial(norm_two_kernel, n),
        (me1, block_input, gain_two, *parts),
        [((tok, width), F32), ((tok, width), BF16)],
        [held],
    )

    gh_theirs = dot(after(top_theirs, normed_two), w_down)
    two_mine, two_theirs = gather_side(normed_two, marks=(gh_theirs, None))

    def feed_half(two, grad_hidden):
        inner_gate, inner_value = dot(two, w_gate), dot(two, w_value)
        act, slope = gelu_pair(inner_gate)
        hidden = (act * inner_value).astype(BF16)
        grad_ig = (grad_hidden * inner_value * slope).astype(BF16)
        grad_iv = (grad_hidden * act).astype(BF16)
        return hidden, grad_ig, grad_iv

    hid_t, gig_t, giv_t = feed_half(two_theirs, gh_theirs)
    back_t = (dot_last(gig_t, w_gate) + dot_last(giv_t, w_value)).astype(BF16)
    two_mine = after(two_mine, back_t)
    hid_m, gig_m, giv_m = feed_half(two_mine, gh_mine)
    back_m = dot_last(gig_m, w_gate) + dot_last(giv_m, w_value)

    def feed_grad(a_m, b_m, a_t, b_t, mark):
        a_m, a_t = after((a_m, a_t), mark)
        return (dot_first(a_m, b_m) + dot_first(a_t, b_t)).astype(BF16)

    def halve(x, m, axis, mark, sel):
        half = x.shape[axis] // 2
        kept = lax.slice_in_dim(x, 0, half, axis=axis)
        got = swap(lax.slice_in_dim(x, half, 2 * half, axis=axis), m, sel)
        if mark is not None:
            got = after(got, mark)
        return (kept.astype(F32) + got.astype(F32)).astype(BF16)

    def far_first(x, axis, mark=None, sel=None):
        return halve(x, masks[-1], axis, mark, sel)

    def far_rest(x, axis, mark=None, sel=None):
        for m in reversed(masks[:-1]):
            x = halve(x, m, axis, mark, sel)
        return x

    parts, mark_one, mark_two = scatter_side(back_m, back_t)
    feed_mark = mark_two
    fg_down = feed_grad(top_mine, hid_m, top_theirs, hid_t, mark_one)
    fg_gate = feed_grad(two_mine, gig_m, two_theirs, gig_t, (mark_two, fg_down))
    parts = after(parts, fg_gate)
    grad_middle, branch, gain_grad_two = kernel_call(
        functools.partial(middle_back_kernel, n),
        (me1, middle, output_grad, gain_two, *parts),
        [((tok, width), F32), ((tok, width), BF16), ((1, width), F32)],
        [held],
    )
    fg_value = feed_grad(two_mine, giv_m, two_theirs, giv_t, branch)
    hid_t, hid_m = after((hid_t, hid_m), fg_value)
    out_t = dot_last(hid_t, w_down).astype(BF16)
    out_m = dot_last(after(hid_m, out_t), w_down)
    branch_mine, branch_theirs = gather_side(branch, marks=(fg_value, out_m))

    gm_theirs = dot_last(branch_theirs, w_out)
    gm_mine = dot_last(branch_mine, w_out)
    grads, suffix, totals = kernel_call(
        back_scan_kernel,
        (gm_mine, gm_theirs, act, dec),
        [(wide, F32), (wide, F32), ((2 * SIDE, CW), F32)],
        smem=0,
        us=16,
    )
    scan_done = totals
    slope_states = after(slope_states, totals)
    grad_gate = kernel_call(
        gate_back_kernel, (gm_mine, gm_theirs, slope_states), [(flat, BF16)], smem=0
    )[0]

    def mixer_grad(grad, mine, theirs):
        return (dot_first(grad[:four], mine) + dot_first(grad[four:], theirs)).astype(BF16)

    def feed_send(shard):
        return exchange(shard.reshape(SIDE, rows_w, fs))

    def feed_rows(v, mark):
        return kernel_call(
            feed_join_kernel, (after(v, mark),), [((rows_w, feed), F32)], smem=0, us=2
        )[0]

    mixed_late = after(mixed, grad_gate)
    go = mixer_grad(mixed_late, branch_mine, branch_theirs)
    def feed_sum(g):
        return lax.psum_scatter(g, AXIS, axis_index_groups=far, tiled=True)

    down_sum = feed_sum(after(fg_down, feed_mark))
    gate_sum = feed_sum(after(fg_gate, branch))
    value_sum = feed_sum(fg_value)
    sent_down = feed_send(after(down_sum, scan_done))
    from_later = chain(totals, True, (go, sent_down))
    go = after(go, from_later)
    go0, go1 = far_first(go[:SLOT], 1), far_first(go[SLOT : 2 * SLOT], 1, None, only)
    g_reset, g_input, g_conv, sums, heads = kernel_call(
        mixer_back_kernel,
        (
            grads, suffix, from_later, dec, rg, ig, low, states, incoming, lin, before, keep,
            halo_keep, keep_rows, r_sq, i_sq, vec,
        ),
        [(flat, BF16)] * 2 + [(wide, F32), ((8, CW), F32), ((3 * SIDE, CW), F32)],
        smem=0,
        us=21,
    )
    heads_y = swap(heads, masks[-1])
    head_parts = [heads, heads_y]
    if span == n:
        low_far = masks[-1]
        side = XBIT | CBIT | lbit(n)
        pairs = []
        for i in range(n):
            for j in range(n):
                last = (i | side) + 1
                if last < n and (j & ~side) == (last & ~side) and (j & side) == (i & side):
                    if ((i ^ j) & ~side) != low_far:
                        pairs.append((j, i))
        head_parts.append(lax.ppermute(heads, AXIS, pairs))
    low_late = after(low, heads)
    sq_r, sq_i = dot_first(low_late, g_reset), dot_first(low_late, g_input)

    rows = SLOT + HALO

    def pack(slot):
        r0, c0 = slot * SLOT, slot * 256
        squares = jnp.concatenate(
            [sq_r[r0 : r0 + SLOT, c0 : c0 + 384], sq_i[r0 : r0 + SLOT, c0 : c0 + 384]], axis=1
        )
        vecs = jnp.pad(sums[:, c0 : c0 + 384], ((0, 8), (0, 384)))
        return jnp.concatenate([squares, vecs]).astype(BF16)

    def total_far(v, m, sel=None):
        return (v.astype(F32) + swap(v, m, sel).astype(F32)).astype(BF16)

    packed_one, packed_two = after((pack(0), pack(1)), heads_y)
    packed_one = total_far(packed_one, masks[-1])
    packed_two = total_far(packed_two, masks[-1], only)

    out_parts, out_one, out_two = scatter_side(after(out_m, scan_done), out_t, heads)
    head_parts = after(tuple(head_parts), sq_i, out_two)
    grad_lin = kernel_call(
        functools.partial(linear_back_kernel, n, span),
        (me1, g_conv, keep, taps, *head_parts),
        [(flat, BF16)],
        [
            pltpu.VMEM((9 * SIDE, 8, CW), F32),
            pltpu.VMEM((3 * SIDE, CW), F32),
            pltpu.VMEM(wide, F32),
        ],
        us=8,
    )[0]
    sent_gate = feed_send(after(gate_sum, grad_lin))
    grad_lin = after(grad_lin, out_parts)
    grad_pre = jnp.concatenate([grad_gate, grad_lin], axis=1)
    back_t = dot(grad_pre[four:], w_mix).astype(BF16)
    back_m = dot(after(grad_pre[:four], back_t), w_mix)
    parts, mark_one, mark_two = scatter_side(
        back_m, back_t, (go0, go1, packed_one, packed_two)
    )
    go0, go1 = far_rest(after(go0, mark_two), 1), far_rest(after(go1, mark_two), 1, None, only)
    packed_one, packed_two = after((packed_one, packed_two), mark_two)
    for m in masks[:-1]:
        packed_one, packed_two = total_far(packed_one, m), total_far(packed_two, m, only)
    block_output = kernel_call(
        functools.partial(add_kernel, n),
        (after(middle, mark_one), *out_parts),
        [((tok, width), F32)],
        smem=0,
    )[0]

    gp = mixer_grad(after(grad_pre, mark_one), norm_mine, norm_theirs)
    gp0 = jnp.concatenate([gp[:SLOT], gp[CW : CW + SLOT]])
    gp1 = jnp.concatenate([gp[SLOT : 2 * SLOT], gp[CW + SLOT : CW + 2 * SLOT]])
    gp0, gp1 = after((gp0, gp1), mark_two)
    gp0, gp1 = far_first(gp0, 1), far_first(gp1, 1, None, only)
    input_grad, gain_grad_one = kernel_call(
        functools.partial(input_back_kernel, n),
        (me1, block_input, grad_middle, gain_one, *after(parts, block_output)),
        [((tok, width), F32), ((1, width), F32)],
        [held],
    )
    done = input_grad
    sent_value = feed_send(after(value_sum, done))
    grad_w_down = feed_rows(sent_down, done)
    grad_w_gate = feed_rows(sent_gate, done)
    grad_w_value = feed_rows(sent_value, done)

    def to_rows(parts, kinds):
        size = (2 * kinds * SLOT + 127) // 128 * 128
        back = kernel_call(turn_back_kernel, parts, [((SIDE, rows_w, size), BF16)], smem=0)[0]
        return kernel_call(
            functools.partial(head_rows_kernel, blk),
            (exchange(back),),
            [((rows_w, heads_count * blk), F32)] * kinds,
            smem=0,
        )

    gp0, gp1 = far_rest(gp0, 1), far_rest(gp1, 1, None, only)
    go0, go1 = after((go0, go1), done)
    grad_w_out = to_rows((go0, go1), 1)[0]
    grad_w_g, grad_w_l = to_rows((gp0, gp1), 2)

    pack_one, pack_two = after((packed_one, packed_two), done)
    packs_mine, packs_theirs = gather_side(pack_one)
    two_x = swap(pack_two, XBIT, only)
    head = here >> 1
    mine_is_eight = (head == 0) | (head == 1)
    both = jnp.where(head == 0, pack_two, jnp.where(head == 3, pack_two, two_x))
    two_l = swap(both, lbit(n))
    eight = jnp.where(mine_is_eight, both, two_l)
    nine = jnp.where(mine_is_eight, two_l, both)
    pair = jnp.stack([eight, nine])
    pair_c = swap(pair, CBIT)
    pair = jnp.where((here & 1) == 0, pair, pair_c)
    shape = (4, rows, 768)
    grad_r_weight, grad_i_weight, small = kernel_call(
        functools.partial(packs_kernel, n, blk),
        (me1, packs_mine.reshape(shape), packs_theirs.reshape(shape), pair[0], pair[1]),
        [((heads_count, blk, blk), F32)] * 2 + [((8, heads_count * blk), F32)],
    )

    gains = jnp.concatenate([gain_grad_one, gain_grad_two]).reshape(-1, 256)
    gains = gains + swap(gains, CBIT)
    rest = [XBIT, lbit(n)] + masks
    while rest:
        one, two, rest = rest[0], rest[1], rest[2:]
        gains = (gains + swap(gains, one)) + (swap(gains, two) + swap(gains, one | two))
    gains = gains.reshape(2, width)

    return (
        block_output,
        input_grad,
        gains[0],
        grad_w_g,
        grad_w_l,
        small[4:],
        small[3],
        grad_r_weight,
        small[0],
        grad_i_weight,
        small[1],
        small[2],
        grad_w_out,
        gains[1],
        grad_w_gate,
        grad_w_value,
        grad_w_down,
    )


def solution(mesh):
    split, whole = P(AXIS, None), P()
    in_specs = (split, P(AXIS), whole, split, split) + (whole,) * 7
    in_specs += (split, whole, split, split, split, split)
    out_specs = (split, split, whole, split, split) + (whole,) * 7
    out_specs += (split, whole, split, split, split)
    return jax.shard_map(body, mesh=mesh, in_specs=in_specs, out_specs=out_specs, check_vma=False)
```

```python
import functools

import jax
import jax.numpy as jnp
from jax import lax
from jax.experimental import pallas as pl
from jax.experimental.pallas import tpu as pltpu
from jax.sharding import PartitionSpec as P

AXIS = "seq"
ROOT_GUARD = 0.001
F32, BF16 = jnp.float32, jnp.bfloat16
SIDE = 8
XBIT, CBIT = 2, 1
EXTRA = {0: 8, 6: 9}
SLOT = 288
CW = 640
HALO = 16
SHORT_ROW = 2048
UNROLL = 4


def lbit(n):
    return 8 if n == 32 else 4


def far_masks(n):
    masks, m = [], n // 2
    while m >= 4:
        if m != lbit(n):
            masks.append(m)
        m //= 2
    return masks


def row_span(n, tok):
    return SHORT_ROW // tok if n * tok == 2 * SHORT_ROW else n


def side_mask(q, n):
    return (q & 1) * XBIT | ((q >> 1) & 1) * lbit(n) | ((q >> 2) & 1) * CBIT


def side_place(d, n):
    x = (d >> (XBIT.bit_length() - 1)) & 1
    l = (d >> (lbit(n).bit_length() - 1)) & 1
    return x + l * 2 + ((d >> (CBIT.bit_length() - 1)) & 1) * 4


def side_code(i, n):
    return (i & 3) | (((i & lbit(n)) != 0) * 4)


def side_groups(n):
    low = XBIT | CBIT | lbit(n)
    return [
        sorted(b | side_mask(q, n) for q in range(SIDE)) for b in range(n) if b & low == 0
    ]


def far_groups(n):
    low = XBIT | CBIT | lbit(n)
    return [[i for i in range(n) if i & low == side_mask(q, n)] for q in range(SIDE)]


def far_mask_of(r, n):
    return sum(m for k, m in enumerate(far_masks(n)) if (r >> k) & 1)


def near_units(n, me):
    low = 2 if lbit(n) == 8 else 3
    units = []
    for r in range(n // SIDE):
        for l in range(SIDE >> low):
            u = 0
            for k, m in enumerate(far_masks(n)):
                bit = lax.shift_right_logical(me, m.bit_length() - 1) & 1
                u = u + ((bit ^ ((r >> k) & 1)) << (m.bit_length() - 1 - low))
            units.append(u + (l << (lbit(n).bit_length() - 1 - low) if low == 2 else 0))
    return units


def fixed_units(n):
    low = 2 if lbit(n) == 8 else 3
    base = [g[0] for g in side_groups(n)]
    return [
        (b | (l * lbit(n) if low == 2 else 0)) >> low for b in base for l in range(SIDE >> low)
    ]


def swap(v, mask, only=None):
    n = lax.axis_size(AXIS)
    pairs = [(i, i ^ mask) for i in range(n) if only is None or side_code(i, n) in only]
    return lax.ppermute(v, AXIS, pairs)


def dot(a, b):
    return lax.dot_general(a, b, (((1,), (0,)), ((), ())), preferred_element_type=F32)


def dot_last(a, b):
    return lax.dot_general(a, b, (((1,), (1,)), ((), ())), preferred_element_type=F32)


def dot_first(a, b):
    return lax.dot_general(a, b, (((0,), (0,)), ((), ())), preferred_element_type=F32)


def after(v, *deps):
    return lax.optimization_barrier((v, *deps))[0]


def kernel_call(kernel, ins, outs, scratch=(), smem=1, us=3):
    specs = [pl.BlockSpec(memory_space=pltpu.SMEM)] * smem
    specs += [pl.BlockSpec(memory_space=pltpu.VMEM)] * (len(ins) - smem)
    return pl.pallas_call(
        kernel,
        in_specs=specs,
        out_specs=[pl.BlockSpec(memory_space=pltpu.VMEM)] * len(outs),
        out_shape=[jax.ShapeDtypeStruct(s, d) for s, d in outs],
        scratch_shapes=list(scratch),
        compiler_params=pltpu.CompilerParams(vmem_limit_bytes=12 * 1024 * 1024),
        cost_estimate=pl.CostEstimate(
            flops=us * 10**9, bytes_accessed=us * 3 * 10**6, transcendentals=0
        ),
    )(*ins)


def gather_side(x, main=None, marks=(None, None)):
    n = lax.axis_size(AXIS)
    half = x.shape[0] // 32 * 16
    by_l, by_x = swap(x, lbit(n)), swap(x, XBIT)
    if marks[0] is not None:
        by_l, by_x = after((by_l, by_x), marks[0])
    low, high = swap(by_l[:half], XBIT), swap(by_x[half:], lbit(n))
    if marks[1] is not None:
        low, high = after((low, high), marks[1])
    if main is None:
        mine = jnp.concatenate([x, by_x, by_l, low, high])
        return mine, swap(mine, CBIT)
    cut = main - half
    mine = jnp.concatenate([x[:main], by_x[:main], by_l[:main], low, high[:cut]])
    rest = jnp.concatenate([x[main:], by_x[main:], by_l[main:], high[cut:]])
    return mine, swap(mine, CBIT), rest, swap(rest, CBIT)


def first_sum_kernel(mine, recv, send_a, send_b, keep_a, keep_b):
    tok, half = mine.shape[0] // 4, mine.shape[1] // 2
    step = 16

    def tile(i, _):
        for b in range(4):
            rows = pl.ds(pl.multiple_of(b * tok + i * step, step), step)
            at = lambda k: pl.ds(pl.multiple_of(k * tok + i * step, step), step)
            va = mine[rows, :half] + recv[rows, :half].astype(F32)
            vb = mine[rows, half:] + recv[rows, half:].astype(F32)
            if b < 2:
                keep_a[at(b), :] = va
            else:
                send_a[at(b - 2), :] = va.astype(BF16)
            if b % 2 == 0:
                keep_b[at(b // 2), :] = vb
            else:
                send_b[at(b // 2), :] = vb.astype(BF16)
        return 0

    lax.fori_loop(0, tok // step, tile, 0)


def second_sum_kernel(keep_a, recv_a, keep_b, recv_b, send_a, send_b, last):
    tok, half = send_a.shape
    step = 16

    def tile(i, _):
        own = pl.ds(pl.multiple_of(i * step, step), step)
        far = pl.ds(pl.multiple_of(tok + i * step, step), step)
        last[own, :half] = keep_a[own, :] + recv_a[own, :].astype(F32)
        last[own, half:] = keep_b[own, :] + recv_b[own, :].astype(F32)
        send_a[own, :] = (keep_a[far, :] + recv_a[far, :].astype(F32)).astype(BF16)
        send_b[own, :] = (keep_b[far, :] + recv_b[far, :].astype(F32)).astype(BF16)
        return 0

    lax.fori_loop(0, tok // step, tile, 0)


def scatter_side(mine, theirs, mark=None, mark_last=None):
    n = lax.axis_size(AXIS)
    rows, width = mine.shape
    tok, half = rows // 4, width // 2
    recv = swap(theirs, CBIT)
    send_a, send_b, keep_a, keep_b = kernel_call(
        first_sum_kernel,
        (mine, recv),
        [((2 * tok, half), BF16)] * 2 + [((2 * tok, half), F32)] * 2,
        smem=0,
    )
    recv_a, recv_b = swap(send_a, lbit(n)), swap(send_b, XBIT)
    if mark is not None:
        keep_a = after(keep_a, mark)
    send_a, send_b, last = kernel_call(
        second_sum_kernel,
        (keep_a, recv_a, keep_b, recv_b),
        [((tok, half), BF16)] * 2 + [((tok, width), F32)],
        smem=0,
    )
    parts = (last, swap(send_a, XBIT), swap(send_b, lbit(n)))
    if mark_last is not None:
        parts = after(parts, mark_last)
    return parts, keep_a, last


def rms_scale(values):
    return lax.rsqrt(jnp.mean(values * values, axis=-1, keepdims=True) + 1e-06)


def unit_slice(u, size):
    return pl.ds(pl.multiple_of(u * size, 128), size)


def put_units(out, rows, value_ref, value_rows, units, size):
    for p, u in enumerate(units):
        out[rows, p * size : (p + 1) * size] = value_ref[value_rows, unit_slice(u, size)]


def tail_kernel(x, gain, flags, out):
    v = x[...]
    out[...] = (v * rms_scale(v) * gain[...]).astype(BF16)
    row = lax.broadcasted_iota(jnp.int32, (HALO, 128), 0) == 0
    out[:, :128] = jnp.where(row, flags[...], out[:, :128].astype(F32)).astype(BF16)


ROWS = 32


def norm_one_kernel(n, me, x, gain, flags, tail, out, held):
    units = near_units(n, me[0])
    size = x.shape[1] // len(units)
    tok = x.shape[0]
    for i in range(tok // ROWS):
        rows = slice(i * ROWS, (i + 1) * ROWS)
        v = x[rows, :]
        held[...] = v * rms_scale(v) * gain[...]
        for p, u in enumerate(units):
            out[rows, p * size : (p + 1) * size] = held[:, unit_slice(u, size)].astype(BF16)
    halo = slice(tok, tok + HALO)
    put_units(out, halo, tail, slice(0, HALO), units, size)
    row = lax.broadcasted_iota(jnp.int32, (HALO, 128), 0)
    first = out[halo, :128].astype(F32)
    both = jnp.where(row == 0, flags[...], first)
    both = jnp.where(row == 1, tail[:, :128].astype(F32)[0:1], both)
    out[halo, :128] = both.astype(BF16)


def top_kernel(n, g, out):
    units = fixed_units(n)
    size = g.shape[1] // len(units)
    for p, u in enumerate(units):
        out[:, p * size : (p + 1) * size] = g[:, u * size : (u + 1) * size].astype(BF16)


def summed(last, ra, rb, rows, p, size):
    half = ra.shape[1]
    a, b = p * size, (p + 1) * size
    if b <= half:
        extra = ra[rows, a:b]
    else:
        extra = rb[rows, a - half : b - half]
    return last[rows, a:b] + extra.astype(F32)


def norm_two_kernel(n, me, x, gain, last, ra, rb, middle, out, held):
    units = near_units(n, me[0])
    size = x.shape[1] // len(units)
    for i in range(x.shape[0] // ROWS):
        rows = slice(i * ROWS, (i + 1) * ROWS)
        for p, u in enumerate(units):
            held[:, unit_slice(u, size)] = summed(last, ra, rb, rows, p, size)
        v = held[...] + x[rows, :]
        middle[rows, :] = v
        w = (v * rms_scale(v) * gain[...]).astype(BF16)
        for p, u in enumerate(fixed_units(n)):
            out[rows, p * size : (p + 1) * size] = w[:, u * size : (u + 1) * size]


def add_kernel(n, middle, last, ra, rb, out):
    units = fixed_units(n)
    size = middle.shape[1] // len(units)
    for p, u in enumerate(units):
        at = slice(u * size, (u + 1) * size)
        out[:, at] = middle[:, at] + summed(last, ra, rb, slice(None), p, size)


def norm_back(grad_normed, values, gain):
    scale = rms_scale(values)
    scaled = grad_normed * gain
    back = scale * scaled - values * (scale * scale * scale) * jnp.mean(
        scaled * values, axis=-1, keepdims=True
    )
    return back, grad_normed * values * scale


def middle_back_kernel(n, me, values, base, gain, last, ra, rb, grad, branch, gain_grad, held):
    units = near_units(n, me[0])
    size = values.shape[1] // len(units)
    total = jnp.zeros((1, values.shape[1]), F32)
    for i in range(values.shape[0] // ROWS):
        rows = slice(i * ROWS, (i + 1) * ROWS)
        for p, u in enumerate(fixed_units(n)):
            held[:, u * size : (u + 1) * size] = summed(last, ra, rb, rows, p, size)
        back, part = norm_back(held[...], values[rows, :], gain[...])
        total = total + jnp.sum(part, axis=0, keepdims=True)
        out = base[rows, :] + back
        grad[rows, :] = out
        held[...] = out
        for p, u in enumerate(units):
            branch[rows, p * size : (p + 1) * size] = held[:, unit_slice(u, size)].astype(BF16)
    gain_grad[...] = total


def input_back_kernel(n, me, values, base, gain, last, ra, rb, grad, gain_grad, held):
    units = near_units(n, me[0])
    size = values.shape[1] // len(units)
    total = jnp.zeros((1, values.shape[1]), F32)
    for i in range(values.shape[0] // ROWS):
        rows = slice(i * ROWS, (i + 1) * ROWS)
        for p, u in enumerate(units):
            held[:, unit_slice(u, size)] = summed(last, ra, rb, rows, p, size)
        back, part = norm_back(held[...], values[rows, :], gain[...])
        total = total + jnp.sum(part, axis=0, keepdims=True)
        grad[rows, :] = base[rows, :] + back
    gain_grad[...] = total


def gelu_pair(v):
    k = 0.7978845608028654
    sq = v * v
    th = jnp.tanh(k * v * (1.0 + 0.044715 * sq))
    half = 0.5 * (1.0 + th)
    slope = half + 0.5 * v * (1.0 - th * th) * (k * (1.0 + 3.0 * 0.044715 * sq))
    return v * half, slope


def strided(i, tok):
    return pl.ds(i, SIDE, stride=tok)


TILES = CW // 128


def cols(c):
    return slice(c * 128, (c + 1) * 128)


def join(tiles):
    return jnp.concatenate(tiles, axis=1)


def stepwise(tok, step, state, reverse=False):
    def some(o, state):
        for k in range(UNROLL):
            i = o * UNROLL + k
            state = step(tok - 1 - i if reverse else i, state)
        return state

    return lax.fori_loop(0, tok // UNROLL, some, state)


def step_rows(i):
    return pl.ds(pl.multiple_of(i * SIDE, SIDE), SIDE)


def mixer_kernel(
    lin_mine, lin_theirs, halo, keep, halo_keep, taps, r_sq, i_sq, vec,
    lin, low, rg, ig, dec, acc, loc, before, totals, conv,
):
    tok = conv.shape[1] // SIDE
    four = 4 * tok
    for c in range(TILES):
        lin[c, :four, :] = lin_mine[:, CW + c * 128 : CW + (c + 1) * 128]
        lin[c, four:, :] = lin_theirs[:, CW + c * 128 : CW + (c + 1) * 128]
        conv[c, : SIDE * HALO, :] = halo[:, cols(c)]
        for k in range(3):
            before[c, k * SIDE : (k + 1) * SIDE, :] = conv[c, strided(HALO - 1 - k, HALO), :]

    for c in range(TILES):
        t0, t1, t2, t3 = (taps[k : k + 1, cols(c)] for k in range(4))
        bias = vec[0:1, cols(c)]

        def conv_step(i, state):
            v1, v2, v3, k1, k2 = state
            v0 = lin[c, strided(i, tok), :]
            k0 = keep[step_rows(i), :]
            conv[c, strided(i, tok), :] = (
                v0 * t0 + bias + k0 * (v1 * t1 + k1 * (v2 * t2 + k2 * (v3 * t3)))
            )
            return v0, v1, v2, k0, k1

        start = tuple(before[c, k * SIDE : (k + 1) * SIDE, :] for k in range(3))
        start += (halo_keep[2 * SIDE :, :], halo_keep[SIDE : 2 * SIDE, :])
        stepwise(tok, conv_step, start)

    def gates(b, _):
        rows = pl.ds(pl.multiple_of(b * tok, tok), tok)
        low_here = join([conv[c, rows, :].astype(BF16) for c in range(TILES)])
        low[rows, :] = low_here
        r = jax.nn.sigmoid(dot(low_here, r_sq[...]) + vec[1:2, :])
        i = jax.nn.sigmoid(dot(low_here, i_sq[...]) + vec[2:3, :])
        for c in range(TILES):
            conv[c, rows, :] = low_here[:, cols(c)].astype(F32)
            rg[c, rows, :] = r[:, cols(c)]
            ig[c, rows, :] = i[:, cols(c)]
        return 0

    lax.fori_loop(0, SIDE, gates, 0)

    def scan_step(i, state):
        at = strided(i, tok)
        k0 = keep[step_rows(i), :]
        out = []
        for c in range(TILES):
            p, s = state[c]
            a = jnp.exp(rg[c, at, :] * vec[3:4, cols(c)]) * k0
            root = jnp.sqrt(1.0 - a * a + ROOT_GUARD)
            b = (k0 * root + (1.0 - k0)) * ig[c, at, :] * conv[c, at, :]
            p, s = p * a, a * s + b
            dec[c, at, :] = a
            acc[c, at, :] = p
            loc[c, at, :] = s
            out.append((p, s))
        return tuple(out)

    shape = (SIDE, 128)
    start = tuple((jnp.ones(shape, F32), jnp.zeros(shape, F32)) for _ in range(TILES))
    found = stepwise(tok, scan_step, start)
    for c in range(TILES):
        totals[:SIDE, cols(c)], totals[SIDE:, cols(c)] = found[c]


def gelu_kernel(gate_mine, gate_theirs, act, slope):
    four = gate_mine.shape[0]

    def tile(i, _):
        rows = pl.ds(pl.multiple_of(i * 16, 16), 16)
        later = pl.ds(pl.multiple_of(four + i * 16, 16), 16)
        for src, dst in ((gate_mine, rows), (gate_theirs, later)):
            for c in range(TILES):
                act[c, dst, :], slope[c, dst, :] = gelu_pair(src[rows, cols(c)])
        return 0

    lax.fori_loop(0, four // 16, tile, 0)


def chain_kernel(n, span, reverse, me_ref, *refs):
    *parts, out, held = refs
    me = me_ref[0]
    state = jnp.zeros((1, CW), F32)
    order = range(span - 1, -1, -1) if reverse else range(span)
    near = [m for m in far_masks(n) if m < span]

    def place(d):
        r = 0
        for k, m in enumerate(near):
            r = r + (((d >> (m.bit_length() - 1)) & 1) << k)
        return r, side_place(d, n)

    both = 2 * SIDE
    for r, part in enumerate(parts):
        for k in range(both):
            held[r * both + k, 0:1, :] = part[k : k + 1, :]
    base = len(parts) * both
    for i in order:
        r, q = place((me & (span - 1)) ^ i)
        held[base + i, 0:1, :] = state
        scale = held[r * both + q, 0:1, :]
        value = held[r * both + SIDE + q, 0:1, :]
        state = scale * state + value
    for q in range(SIDE):
        at = base + ((me & (span - 1)) ^ side_mask(q, n))
        out[q, :, :] = jnp.broadcast_to(held[at, 0:1, :], (8, CW))


def states_kernel(acc, loc, incoming, act, slope, states, mixed, slope_states):
    tok = acc.shape[1] // SIDE
    for q in range(SIDE):

        def tile(i, _):
            rows = pl.ds(pl.multiple_of(q * tok + i * 16, 16), 16)
            out = []
            for c in range(TILES):
                s = loc[c, rows, :] + acc[c, rows, :] * incoming[q, 0:1, cols(c)]
                states[c, rows, :] = s
                slope_states[c, rows, :] = s * slope[c, rows, :]
                out.append((s * act[c, rows, :]).astype(BF16))
            mixed[rows, :] = join(out)
            return 0

        lax.fori_loop(0, tok // 16, tile, 0)


def back_scan_kernel(gm_mine, gm_theirs, act, dec, grads, suffix, totals):
    tok = act.shape[1] // SIDE
    four = 4 * tok
    for c in range(TILES):
        grads[c, :four, :] = gm_mine[:, cols(c)] * act[c, :four, :]
        grads[c, four:, :] = gm_theirs[:, cols(c)] * act[c, four:, :]

    def step(i, state):
        at = strided(i, tok)
        out = []
        for c in range(TILES):
            ag, aq = state[c]
            g = grads[c, at, :] + ag
            grads[c, at, :] = g
            suffix[c, at, :] = aq
            a = dec[c, at, :]
            out.append((a * g, a * aq))
        return tuple(out)

    shape = (SIDE, 128)
    start = tuple((jnp.zeros(shape, F32), jnp.ones(shape, F32)) for _ in range(TILES))
    found = stepwise(tok, step, start, True)
    for c in range(TILES):
        totals[SIDE:, cols(c)], totals[:SIDE, cols(c)] = found[c]


def gate_back_kernel(gm_mine, gm_theirs, slope_states, out):
    four = gm_mine.shape[0]

    def tile(i, _):
        rows = pl.ds(pl.multiple_of(i * 16, 16), 16)
        later = pl.ds(pl.multiple_of(four + i * 16, 16), 16)
        for src, dst in ((gm_mine, rows), (gm_theirs, later)):
            out[dst, :] = join(
                [(src[rows, cols(c)] * slope_states[c, dst, :]).astype(BF16) for c in range(TILES)]
            )
        return 0

    lax.fori_loop(0, four // 16, tile, 0)


def mixer_back_kernel(
    grads, suffix, from_later, dec, rg, ig, low, states, incoming, lin, before, keep, halo_keep,
    keep_rows, r_sq, i_sq, vec, g_reset, g_input, g_conv, sums, heads,
):
    tok = dec.shape[1] // SIDE
    zero = jnp.zeros((1, 128), F32)

    def block(b, totals):
        rows = pl.ds(pl.multiple_of(b * tok, tok), tok)
        k = keep_rows[rows, :]
        at_first = lax.broadcasted_iota(jnp.int32, (tok, 128), 0) == 0
        out, g_rs, g_is, base = [], [], [], []
        for c in range(TILES):
            gs = grads[c, rows, :] + suffix[c, rows, :] * from_later[b, 0:1, cols(c)]
            a, r, i_g = dec[c, rows, :], rg[c, rows, :], ig[c, rows, :]
            v = low[rows, cols(c)].astype(F32)
            root = jnp.sqrt(1.0 - a * a + ROOT_GUARD)
            mult = k * root + (1.0 - k)
            prior = pltpu.roll(states[c, rows, :], 1, 0)
            prior = jnp.where(at_first, incoming[b, 0:1, cols(c)], prior)
            gv = gs * v
            glr = a * (gs * prior - gv * i_g * a / root) * r
            g_r = (vec[3:4, cols(c)] * glr * (1.0 - r)).astype(BF16)
            gm = gs * mult * i_g
            g_i = (gm * v * (1.0 - i_g)).astype(BF16)
            out.append(
                (
                    totals[c][0] + jnp.sum(glr, axis=0, keepdims=True),
                    totals[c][1] + jnp.sum(g_r.astype(F32), axis=0, keepdims=True),
                    totals[c][2] + jnp.sum(g_i.astype(F32), axis=0, keepdims=True),
                )
            )
            g_rs.append(g_r)
            g_is.append(g_i)
            g_conv[c, rows, :] = gm
        g_r, g_i = join(g_rs), join(g_is)
        g_reset[rows, :] = g_r
        g_input[rows, :] = g_i
        more = dot_last(g_r, r_sq[...]) + dot_last(g_i, i_sq[...])
        for c in range(TILES):
            g_conv[c, rows, :] = g_conv[c, rows, :] + more[:, cols(c)]
        return tuple(out)

    found = lax.fori_loop(0, SIDE, block, ((zero,) * 3,) * TILES)
    for c in range(TILES):
        dec_sum, r_sum, i_sum = found[c]
        sums[0:1, cols(c)] = r_sum
        sums[1:2, cols(c)] = i_sum
        sums[2:3, cols(c)] = -vec[4:5, cols(c)] * dec_sum

    blank = jnp.zeros((SIDE, 128), F32)
    for c in range(TILES):

        def tap_step(i, state):
            v1, v2, v3, k1, k2, s0, s1, s2, s3, sb = state
            v0 = lin[c, strided(i, tok), :]
            k0 = keep[step_rows(i), :]
            g0 = g_conv[c, strided(i, tok), :]
            g1 = g0 * k0
            g2 = g1 * k1
            g3 = g2 * k2
            return (
                (v0, v1, v2, k0, k1)
                + (s0 + g0 * v0, s1 + g1 * v1, s2 + g2 * v2, s3 + g3 * v3, sb + g0)
            )

        start = tuple(before[c, k * SIDE : (k + 1) * SIDE, :] for k in range(3))
        start += (halo_keep[2 * SIDE :, :], halo_keep[SIDE : 2 * SIDE, :]) + (blank,) * 5
        end = stepwise(tok, tap_step, start)
        per_row = [jnp.sum(v, axis=0, keepdims=True) for v in end[5:]]
        sums[3:4, cols(c)] = per_row[4]
        for j in range(4):
            sums[4 + j : 5 + j, cols(c)] = per_row[j]
        k = None
        for i in range(3):
            k_i = keep[i * SIDE : (i + 1) * SIDE, :]
            k = k_i if k is None else k * k_i
            heads[i * SIDE : (i + 1) * SIDE, cols(c)] = g_conv[c, strided(i, tok), :] * k


def linear_back_kernel(n, span, me_ref, g_conv, keep, taps, *refs):
    *parts, out, held, after, conv = refs
    me = me_ref[0]
    tok = g_conv.shape[1] // SIDE
    rows3 = 3 * SIDE
    for k, part in enumerate(parts):
        for m in range(rows3):
            held[k * rows3 + m, 0:1, :] = part[m : m + 1, :]
    low_far = far_masks(n)[-1]
    side = XBIT | CBIT | lbit(n)
    for q in range(SIDE):
        nxt = (me ^ side_mask(q, n)) + 1
        d = nxt ^ me
        far = d & ~side
        ok = ((nxt & (span - 1)) != 0).astype(F32)
        which = jnp.where(far == 0, 0, jnp.where(far == low_far, 1, len(parts) - 1))
        for m in range(3):
            at = which * rows3 + m * SIDE + side_place(d, n)
            after[m * SIDE + q : m * SIDE + q + 1, :] = held[at, 0:1, :] * ok
    one = jnp.ones((SIDE, 128), F32)
    for c in range(TILES):
        t0, t1, t2, t3 = (taps[k : k + 1, cols(c)] for k in range(4))

        def step(i, state):
            g1, g2, g3, k1, k2, k3 = state
            g0 = g_conv[c, strided(i, tok), :]
            conv[c, strided(i, tok), :] = g0 * t0 + k1 * (g1 * t1 + k2 * (g2 * t2 + k3 * (g3 * t3)))
            return g0, g1, g2, keep[step_rows(i), :], k1, k2

        start = tuple(after[m * SIDE : (m + 1) * SIDE, cols(c)] for m in range(3))
        stepwise(tok, step, start + (one, one, one), True)

    def tile(i, _):
        rows = pl.ds(pl.multiple_of(i * 16, 16), 16)
        out[rows, :] = join([conv[c, rows, :].astype(BF16) for c in range(TILES)])
        return 0

    lax.fori_loop(0, SIDE * tok // 16, tile, 0)


def heads_kernel(blk, gate, linear, out_w, first, second):
    first[...] = jnp.zeros(first.shape, BF16)
    second[...] = jnp.zeros(second.shape, BF16)
    for k, w in enumerate((gate, linear, out_w)):
        at = slice(k * SLOT, k * SLOT + blk)
        for s in range(SIDE):
            first[s, :, at] = w[:, s * blk : (s + 1) * blk]
        for s, e in EXTRA.items():
            second[s, :, at] = w[:, e * blk : (e + 1) * blk]


def feed_parts_kernel(*refs):
    *weights, out = refs
    rows, size = weights[0].shape[0], out.shape[2]
    for k, w in enumerate(weights):
        for s in range(SIDE):
            out[s, k * rows : (k + 1) * rows, :] = w[:, s * size : (s + 1) * size]


def feed_join_kernel(parts, out):
    size = parts.shape[2]
    for s in range(SIDE):
        out[:, s * size : (s + 1) * size] = parts[s, :, :].astype(F32)


def turn_kernel(parts, *outs):
    rows = parts.shape[1]
    turned = parts[...].reshape(SIDE * rows, parts.shape[2]).T
    at = 0
    for out in outs:
        out[...] = turned[at : at + out.shape[0]]
        at += out.shape[0]


def assemble_kernel(count, which, *refs):
    first, extra, out = refs[:count], refs[count : 2 * count], refs[2 * count]
    size = first[0].shape[1]
    for r in range(count):
        lanes = slice(r * size, (r + 1) * size)
        for m, k in enumerate(which):
            out[m * CW : m * CW + SLOT, lanes] = first[r][m * SLOT : (m + 1) * SLOT, :]
            out[m * CW + SLOT : m * CW + 2 * SLOT, lanes] = extra[r][k * SLOT : (k + 1) * SLOT, :]
            out[m * CW + 2 * SLOT : (m + 1) * CW, lanes] = jnp.zeros((CW - 2 * SLOT, size), BF16)


def turn_back_kernel(*refs):
    *parts, out = refs
    rows = out.shape[1]
    flat = jnp.concatenate([p[...] for p in parts])
    out[:, :, : flat.shape[0]] = flat.T.reshape(SIDE, rows, flat.shape[0])


def head_rows_kernel(blk, parts, *outs):
    count = len(outs)
    for k, out in enumerate(outs):
        for s in range(SIDE):
            at = k * SLOT
            out[:, s * blk : (s + 1) * blk] = parts[s, :, at : at + blk].astype(F32)
        for s, e in EXTRA.items():
            at = (count + k) * SLOT
            out[:, e * blk : (e + 1) * blk] = parts[s, :, at : at + blk].astype(F32)


def packs_kernel(n, blk, me_ref, mine, theirs, eight, nine, r_out, i_out, vec_out):
    me = me_ref[0]

    def put(ref, e, shift):
        def lanes(v):
            return v[:, shift : shift + blk]

        r_out[e, :, :] = lanes(ref[:SLOT, :384].astype(F32))[:blk]
        i_out[e, :, :] = lanes(ref[:SLOT, 384:].astype(F32))[:blk]
        vec_out[:, e * blk : (e + 1) * blk] = lanes(ref[SLOT:, :384].astype(F32)[:8])

    for s in range(SIDE):
        i = (s & 3) | ((s >> 2) * lbit(n))
        d = jnp.int32(i) ^ (me & (XBIT | CBIT | lbit(n)))
        q = ((d >> (XBIT.bit_length() - 1)) & 1) + ((d >> (lbit(n).bit_length() - 1)) & 1) * 2
        own = ((d >> (CBIT.bit_length() - 1)) & 1) == 0

        @pl.when(own)
        def _():
            put(mine.at[q], s, 0)

        @pl.when(jnp.logical_not(own))
        def _():
            put(theirs.at[q], s, 0)

    put(eight, EXTRA[0], 32)
    put(nine, EXTRA[6], 32)


def body(
    block_input,
    start_flags,
    norm_gain,
    gate_weight,
    linear_weight,
    conv_taps,
    conv_bias,
    reset_weight,
    reset_bias,
    input_weight,
    input_bias,
    decay_param,
    out_weight,
    feed_norm_gain,
    feed_gate_weight,
    feed_value_weight,
    feed_down_weight,
    output_grad,
):
    n = lax.axis_size(AXIS)
    me = lax.axis_index(AXIS)
    me1 = me.reshape(1)
    here = side_code(me, n)
    tok, width = block_input.shape
    heads_count, blk = reset_weight.shape[:2]
    rows_w = gate_weight.shape[0]
    feed = feed_gate_weight.shape[1]
    fs = feed // SIDE
    masks = far_masks(n)
    groups, far = side_groups(n), far_groups(n)
    only = tuple(EXTRA)
    has_extra = (here == only[0]) | (here == only[1])
    extra_here = jnp.where(here == only[1], EXTRA[only[1]], EXTRA[only[0]])
    four = 4 * tok
    side_tok = SIDE * tok
    cols_w = SIDE * rows_w
    places = n // SIDE
    count = len(masks)

    def exchange(v):
        return lax.all_to_all(v, AXIS, 0, 0, axis_index_groups=groups, tiled=True)

    def gather_far(x, sel=None):
        chunks = [x]
        for m in masks:
            chunks += [swap(c, m, sel) for c in chunks]
        return chunks

    gain_one = norm_gain.astype(F32)[None]
    gain_two = feed_norm_gain.astype(F32)[None]
    flags = start_flags.astype(F32)[None]
    parts, more_parts = kernel_call(
        functools.partial(heads_kernel, blk),
        (gate_weight, linear_weight, out_weight),
        [((SIDE, rows_w, 3 * SLOT + 32), BF16)] * 2,
        smem=0,
    )
    tail = kernel_call(
        tail_kernel,
        (after(block_input[-HALO:], parts), gain_one, flags),
        [((HALO, width), BF16)],
        smem=0,
        us=1,
    )[0]
    tail = lax.ppermute(tail, AXIS, [(i, i + 1) for i in range(n - 1)])
    packet = kernel_call(
        functools.partial(norm_one_kernel, n),
        (me1, block_input, gain_one, flags, tail),
        [((tok + HALO, width), BF16)],
        [pltpu.VMEM((ROWS, width), F32)],
    )[0]
    f_parts = kernel_call(
        feed_parts_kernel,
        (after(feed_gate_weight, packet), feed_value_weight, feed_down_weight),
        [((SIDE, 3 * rows_w, fs), BF16)],
        smem=0,
    )[0]
    top = kernel_call(
        functools.partial(top_kernel, n),
        (after(output_grad, f_parts),),
        [((tok, width), BF16)],
        smem=0,
    )[0]
    parts = exchange(parts)
    p_mix, p_out = kernel_call(
        turn_kernel, (parts,), [((k * SLOT, cols_w), BF16) for k in (2, 1)], smem=0
    )
    more_parts = exchange(after(more_parts, parts))
    f_parts = exchange(after(f_parts, more_parts))
    p_extra = kernel_call(turn_kernel, (more_parts,), [((3 * SLOT, cols_w), BF16)], smem=0)[0]

    def gather_start(x, count=2, sel=None):
        return [x] + [swap(x, m, sel) for m in masks[:count]]

    def gather_later(chunks, sel=None, mark=None):
        chunks = list(chunks)
        if mark is not None:
            chunks[1] = after(chunks[1], mark)
        if len(chunks) == 3:
            chunks.append(swap(chunks[1], masks[1], sel))
        for m in masks[len(chunks).bit_length() - 1 :]:
            chunks += [swap(c, m, sel) for c in chunks]
        return chunks

    packet = after(packet, p_mix)
    c_mix = gather_start(p_mix)
    half = tok // 2
    by_l, by_x = swap(packet, lbit(n)), swap(packet, XBIT)
    (c_mix, by_l, by_x, p_extra) = lax.optimization_barrier((c_mix, by_l, by_x, p_extra))
    c_mix = gather_later(c_mix)
    c_extra = gather_start(p_extra, 1, only)
    low, high = swap(by_l[:half], XBIT), swap(by_x[half:], lbit(n))
    (c_mix, c_extra, low, high, p_out) = lax.optimization_barrier(
        (c_mix, c_extra, low, high, p_out)
    )
    f_parts = after(f_parts, c_extra)
    c_extra = gather_later(c_extra, only)
    c_out = gather_start(p_out, 1)
    f_parts = f_parts.reshape(SIDE, 3, rows_w, fs)
    norm_mine = jnp.concatenate([packet[:tok], by_x[:tok], by_l[:tok], low, high[:half]])
    halo_mine = jnp.concatenate([packet[tok:], by_x[tok:], by_l[tok:], high[half:]])
    norm_theirs, halo_theirs = swap(norm_mine, CBIT), swap(halo_mine, CBIT)
    f_parts = [f_parts[:, k].reshape(cols_w, fs) for k in range(3)]
    w_mix = kernel_call(
        functools.partial(assemble_kernel, places, (0, 1)),
        (*c_mix, *c_extra),
        [((2 * CW, width), BF16)],
        smem=0,
        us=5,
    )[0]
    c_out = gather_later([after(p_out, w_mix), c_out[1]], mark=w_mix)
    w_mix = after(w_mix, tuple(f_parts))

    def feed_full(part):
        return lax.all_gather(part, AXIS, axis_index_groups=far, tiled=True)

    w_down, w_gate, w_value = (feed_full(f_parts[k]) for k in (2, 0, 1))

    def pick(p):
        one = lax.dynamic_index_in_dim(p, here, 0, False)
        two = lax.dynamic_index_in_dim(p, extra_here, 0, False)
        return one, jnp.where(has_extra, two, jnp.zeros_like(two))

    vectors = jnp.concatenate(
        [conv_taps]
        + [v[None] for v in (conv_bias, reset_bias, input_bias, decay_param)]
    ).astype(F32)
    vectors = vectors.reshape(8, heads_count, blk).transpose(1, 0, 2)
    vec_one, vec_two = pick(vectors)
    gap = ((0, 0), (0, SLOT - blk))
    vectors = jnp.concatenate([jnp.pad(vec_one, gap), jnp.pad(vec_two, gap)], axis=1)
    vectors = jnp.pad(vectors, ((0, 0), (0, CW - 2 * SLOT)))
    taps = vectors[:4]
    decay_float = vectors[7]
    vec = jnp.concatenate(
        [
            vectors[4:7],
            (-8.0 * jax.nn.softplus(-decay_float))[None],
            (-8.0 * jax.nn.sigmoid(-decay_float))[None],
            jnp.zeros((3, CW), F32),
        ]
    )

    def square(p):
        one, two = pick(p)
        low = CW - SLOT - blk
        return jnp.pad(one, ((0, CW - blk),) * 2) + jnp.pad(two, ((SLOT, low),) * 2)

    r_sq, i_sq = square(reset_weight), square(input_weight)

    halo_all = jnp.concatenate([halo_mine, halo_theirs])
    flag_rows = halo_all.reshape(SIDE, HALO, width)[:, :2, :128].astype(F32)
    keep_blocks = 1.0 - flag_rows[:, 0]
    keep = jnp.broadcast_to(keep_blocks.T[:, :, None], (tok, SIDE, 128)).reshape(side_tok, 128)
    keep_rows = jnp.broadcast_to(keep_blocks[:, :, None], (SIDE, tok, 128)).reshape(side_tok, 128)
    halo_keep = 1.0 - flag_rows[:, 1, tok - 3 :]
    halo_keep = jnp.broadcast_to(halo_keep.T[:, :, None], (3, SIDE, 128)).reshape(3 * SIDE, 128)

    pre_mine, pre_theirs = dot_last(norm_mine, w_mix), dot_last(norm_theirs, w_mix)
    halo = dot_last(halo_all, w_mix[CW:])
    top = after(top, w_mix)
    top_l, top_x = swap(top, lbit(n)), swap(top, XBIT)
    flat, wide = (side_tok, CW), (TILES, side_tok, 128)
    lin, low, rg, ig, dec, acc, loc, before, totals = kernel_call(
        mixer_kernel,
        (pre_mine, pre_theirs, halo, keep, halo_keep, taps, r_sq, i_sq, vec),
        [(wide, F32), (flat, BF16)]
        + [(wide, F32)] * 5
        + [((TILES, 3 * SIDE, 128), F32), ((2 * SIDE, CW), F32)],
        [pltpu.VMEM(wide, F32)],
        smem=0,
        us=29,
    )

    span = row_span(n, tok)

    def chain(totals, reverse, mark):
        near = [far_mask_of(r, n) for r in range(1, n // SIDE)]
        parts = [totals] + [swap(totals, m) for m in near if m < span]
        parts = after(tuple(parts), mark)
        return kernel_call(
            functools.partial(chain_kernel, n, span, reverse),
            (me1, *parts),
            [((SIDE, 8, CW), F32)],
            [pltpu.VMEM((len(parts) * 2 * SIDE + span, 8, CW), F32)],
            us=2,
        )[0]

    top_l, top_x = after((top_l, top_x), totals)
    top_low, top_high = swap(top_l[: tok // 2], XBIT), swap(top_x[tok // 2 :], lbit(n))
    gate_halves = after((pre_mine, pre_theirs), totals, top_l)
    act, slope = kernel_call(gelu_kernel, gate_halves, [(wide, F32)] * 2, smem=0, us=7)
    c_out, c_extra = after((tuple(c_out), tuple(c_extra)), act)
    w_out = kernel_call(
        functools.partial(assemble_kernel, places, (2,)),
        (*c_out, *c_extra),
        [((CW, width), BF16)],
        smem=0,
    )[0]
    incoming = chain(totals, False, w_out)
    top_mine = jnp.concatenate([top, top_x, top_l, top_low, top_high])
    incoming = after(incoming, top_low, top_high)
    states, mixed, slope_states = kernel_call(
        states_kernel,
        (acc, loc, incoming, act, slope),
        [(wide, F32), (flat, BF16), (wide, F32)],
        smem=0,
        us=8,
    )
    theirs = dot(mixed[four:], w_out).astype(BF16)
    mixed_mine = after(mixed[:four], theirs)
    parts, mark_one, mark_two = scatter_side(dot(mixed_mine, w_out), theirs)
    top_theirs = swap(after(top_mine, mark_one), CBIT)
    gh_mine = dot(after(top_mine, mark_one), w_down)
    parts = after(parts, gh_mine)
    held = pltpu.VMEM((ROWS, width), F32)
    middle, normed_two = kernel_call(
        functools.partial(norm_two_kernel, n),
        (me1, block_input, gain_two, *parts),
        [((tok, width), F32), ((tok, width), BF16)],
        [held],
    )

    gh_theirs = dot(after(top_theirs, normed_two), w_down)
    two_mine, two_theirs = gather_side(normed_two, marks=(gh_theirs, None))

    def feed_half(two, grad_hidden):
        inner_gate, inner_value = dot(two, w_gate), dot(two, w_value)
        act, slope = gelu_pair(inner_gate)
        hidden = (act * inner_value).astype(BF16)
        grad_ig = (grad_hidden * inner_value * slope).astype(BF16)
        grad_iv = (grad_hidden * act).astype(BF16)
        return hidden, grad_ig, grad_iv

    hid_t, gig_t, giv_t = feed_half(two_theirs, gh_theirs)
    back_t = (dot_last(gig_t, w_gate) + dot_last(giv_t, w_value)).astype(BF16)
    two_mine = after(two_mine, back_t)
    hid_m, gig_m, giv_m = feed_half(two_mine, gh_mine)
    back_m = dot_last(gig_m, w_gate) + dot_last(giv_m, w_value)

    def feed_grad(a_m, b_m, a_t, b_t, mark):
        a_m, a_t = after((a_m, a_t), mark)
        return (dot_first(a_m, b_m) + dot_first(a_t, b_t)).astype(BF16)

    def halve(x, m, axis, mark, sel):
        half = x.shape[axis] // 2
        kept = lax.slice_in_dim(x, 0, half, axis=axis)
        got = swap(lax.slice_in_dim(x, half, 2 * half, axis=axis), m, sel)
        if mark is not None:
            got = after(got, mark)
        return (kept.astype(F32) + got.astype(F32)).astype(BF16)

    def far_first(x, axis, mark=None, sel=None):
        return halve(x, masks[-1], axis, mark, sel)

    def far_rest(x, axis, mark=None, sel=None):
        for m in reversed(masks[:-1]):
            x = halve(x, m, axis, mark, sel)
        return x

    parts, mark_one, mark_two = scatter_side(back_m, back_t)
    feed_mark = mark_two
    fg_down = feed_grad(top_mine, hid_m, top_theirs, hid_t, mark_one)
    fg_gate = feed_grad(two_mine, gig_m, two_theirs, gig_t, (mark_two, fg_down))
    parts = after(parts, fg_gate)
    grad_middle, branch, gain_grad_two = kernel_call(
        functools.partial(middle_back_kernel, n),
        (me1, middle, output_grad, gain_two, *parts),
        [((tok, width), F32), ((tok, width), BF16), ((1, width), F32)],
        [held],
    )
    fg_value = feed_grad(two_mine, giv_m, two_theirs, giv_t, branch)
    hid_t, hid_m = after((hid_t, hid_m), fg_value)
    out_t = dot_last(hid_t, w_down).astype(BF16)
    out_m = dot_last(after(hid_m, out_t), w_down)
    branch_mine, branch_theirs = gather_side(branch, marks=(fg_value, out_m))

    gm_theirs = dot_last(branch_theirs, w_out)
    gm_mine = dot_last(branch_mine, w_out)
    grads, suffix, totals = kernel_call(
        back_scan_kernel,
        (gm_mine, gm_theirs, act, dec),
        [(wide, F32), (wide, F32), ((2 * SIDE, CW), F32)],
        smem=0,
        us=16,
    )
    scan_done = totals
    slope_states = after(slope_states, totals)
    grad_gate = kernel_call(
        gate_back_kernel, (gm_mine, gm_theirs, slope_states), [(flat, BF16)], smem=0
    )[0]

    def mixer_grad(grad, mine, theirs):
        return (dot_first(grad[:four], mine) + dot_first(grad[four:], theirs)).astype(BF16)

    def feed_send(shard):
        return exchange(shard.reshape(SIDE, rows_w, fs))

    def feed_rows(v, mark):
        return kernel_call(
            feed_join_kernel, (after(v, mark),), [((rows_w, feed), F32)], smem=0, us=2
        )[0]

    mixed_late = after(mixed, grad_gate)
    go = mixer_grad(mixed_late, branch_mine, branch_theirs)
    def feed_sum(g):
        return lax.psum_scatter(g, AXIS, axis_index_groups=far, tiled=True)

    down_sum = feed_sum(after(fg_down, feed_mark))
    gate_sum = feed_sum(after(fg_gate, branch))
    value_sum = feed_sum(fg_value)
    sent_down = feed_send(after(down_sum, scan_done))
    from_later = chain(totals, True, (go, sent_down))
    go = after(go, from_later)
    go0, go1 = far_first(go[:SLOT], 1), far_first(go[SLOT : 2 * SLOT], 1, None, only)
    g_reset, g_input, g_conv, sums, heads = kernel_call(
        mixer_back_kernel,
        (
            grads, suffix, from_later, dec, rg, ig, low, states, incoming, lin, before, keep,
            halo_keep, keep_rows, r_sq, i_sq, vec,
        ),
        [(flat, BF16)] * 2 + [(wide, F32), ((8, CW), F32), ((3 * SIDE, CW), F32)],
        smem=0,
        us=21,
    )
    heads_y = swap(heads, masks[-1])
    head_parts = [heads, heads_y]
    if span == n:
        low_far = masks[-1]
        side = XBIT | CBIT | lbit(n)
        pairs = []
        for i in range(n):
            for j in range(n):
                last = (i | side) + 1
                if last < n and (j & ~side) == (last & ~side) and (j & side) == (i & side):
                    if ((i ^ j) & ~side) != low_far:
                        pairs.append((j, i))
        head_parts.append(lax.ppermute(heads, AXIS, pairs))
    low_late = after(low, heads)
    sq_r, sq_i = dot_first(low_late, g_reset), dot_first(low_late, g_input)

    rows = SLOT + HALO

    def pack(slot):
        r0, c0 = slot * SLOT, slot * 256
        squares = jnp.concatenate(
            [sq_r[r0 : r0 + SLOT, c0 : c0 + 384], sq_i[r0 : r0 + SLOT, c0 : c0 + 384]], axis=1
        )
        vecs = jnp.pad(sums[:, c0 : c0 + 384], ((0, 8), (0, 384)))
        return jnp.concatenate([squares, vecs]).astype(BF16)

    def total_far(v, m, sel=None):
        return (v.astype(F32) + swap(v, m, sel).astype(F32)).astype(BF16)

    packed_one, packed_two = after((pack(0), pack(1)), heads_y)
    packed_one = total_far(packed_one, masks[-1])
    packed_two = total_far(packed_two, masks[-1], only)

    out_parts, out_one, out_two = scatter_side(after(out_m, scan_done), out_t, heads)
    head_parts = after(tuple(head_parts), sq_i, out_two)
    grad_lin = kernel_call(
        functools.partial(linear_back_kernel, n, span),
        (me1, g_conv, keep, taps, *head_parts),
        [(flat, BF16)],
        [
            pltpu.VMEM((9 * SIDE, 8, CW), F32),
            pltpu.VMEM((3 * SIDE, CW), F32),
            pltpu.VMEM(wide, F32),
        ],
        us=8,
    )[0]
    sent_gate = feed_send(after(gate_sum, grad_lin))
    grad_lin = after(grad_lin, out_parts)
    grad_pre = jnp.concatenate([grad_gate, grad_lin], axis=1)
    back_t = dot(grad_pre[four:], w_mix).astype(BF16)
    back_m = dot(after(grad_pre[:four], back_t), w_mix)
    parts, mark_one, mark_two = scatter_side(
        back_m, back_t, (go0, go1, packed_one, packed_two)
    )
    go0, go1 = far_rest(after(go0, mark_two), 1), far_rest(after(go1, mark_two), 1, None, only)
    packed_one, packed_two = after((packed_one, packed_two), mark_two)
    for m in masks[:-1]:
        packed_one, packed_two = total_far(packed_one, m), total_far(packed_two, m, only)
    block_output = kernel_call(
        functools.partial(add_kernel, n),
        (after(middle, mark_one), *out_parts),
        [((tok, width), F32)],
        smem=0,
    )[0]

    gp = mixer_grad(after(grad_pre, mark_one), norm_mine, norm_theirs)
    gp0 = jnp.concatenate([gp[:SLOT], gp[CW : CW + SLOT]])
    gp1 = jnp.concatenate([gp[SLOT : 2 * SLOT], gp[CW + SLOT : CW + 2 * SLOT]])
    gp0, gp1 = after((gp0, gp1), mark_two)
    gp0, gp1 = far_first(gp0, 1), far_first(gp1, 1, None, only)
    input_grad, gain_grad_one = kernel_call(
        functools.partial(input_back_kernel, n),
        (me1, block_input, grad_middle, gain_one, *after(parts, block_output)),
        [((tok, width), F32), ((1, width), F32)],
        [held],
    )
    done = input_grad
    sent_value = feed_send(after(value_sum, done))
    grad_w_down = feed_rows(sent_down, done)
    grad_w_gate = feed_rows(sent_gate, done)
    grad_w_value = feed_rows(sent_value, done)

    def to_rows(parts, kinds):
        size = (2 * kinds * SLOT + 127) // 128 * 128
        back = kernel_call(turn_back_kernel, parts, [((SIDE, rows_w, size), BF16)], smem=0)[0]
        return kernel_call(
            functools.partial(head_rows_kernel, blk),
            (exchange(back),),
            [((rows_w, heads_count * blk), F32)] * kinds,
            smem=0,
        )

    gp0, gp1 = far_rest(gp0, 1), far_rest(gp1, 1, None, only)
    go0, go1 = after((go0, go1), done)
    grad_w_out = to_rows((go0, go1), 1)[0]
    grad_w_g, grad_w_l = to_rows((gp0, gp1), 2)

    pack_one, pack_two = after((packed_one, packed_two), done)
    packs_mine, packs_theirs = gather_side(pack_one)
    two_x = swap(pack_two, XBIT, only)
    head = here >> 1
    mine_is_eight = (head == 0) | (head == 1)
    both = jnp.where(head == 0, pack_two, jnp.where(head == 3, pack_two, two_x))
    two_l = swap(both, lbit(n))
    eight = jnp.where(mine_is_eight, both, two_l)
    nine = jnp.where(mine_is_eight, two_l, both)
    pair = jnp.stack([eight, nine])
    pair_c = swap(pair, CBIT)
    pair = jnp.where((here & 1) == 0, pair, pair_c)
    shape = (4, rows, 768)
    grad_r_weight, grad_i_weight, small = kernel_call(
        functools.partial(packs_kernel, n, blk),
        (me1, packs_mine.reshape(shape), packs_theirs.reshape(shape), pair[0], pair[1]),
        [((heads_count, blk, blk), F32)] * 2 + [((8, heads_count * blk), F32)],
    )

    gains = jnp.concatenate([gain_grad_one, gain_grad_two]).reshape(-1, 256)
    gains = gains + swap(gains, CBIT)
    rest = [XBIT, lbit(n)] + masks
    while rest:
        one, two, rest = rest[0], rest[1], rest[2:]
        gains = (gains + swap(gains, one)) + (swap(gains, two) + swap(gains, one | two))
    gains = gains.reshape(2, width)

    return (
        block_output,
        input_grad,
        gains[0],
        grad_w_g,
        grad_w_l,
        small[4:],
        small[3],
        grad_r_weight,
        small[0],
        grad_i_weight,
        small[1],
        small[2],
        grad_w_out,
        gains[1],
        grad_w_gate,
        grad_w_value,
        grad_w_down,
    )


def solution(mesh):
    split, whole = P(AXIS, None), P()
    in_specs = (split, P(AXIS), whole, split, split) + (whole,) * 7
    in_specs += (split, whole, split, split, split, split)
    out_specs = (split, split, whole, split, split) + (whole,) * 7
    out_specs += (split, whole, split, split, split)
    return jax.shard_map(body, mesh=mesh, in_specs=in_specs, out_specs=out_specs, check_vma=False)
```

```python
import functools

import jax
import jax.numpy as jnp
from jax import lax
from jax.experimental import pallas as pl
from jax.experimental.pallas import tpu as pltpu
from jax.sharding import PartitionSpec as P

AXIS = "seq"
ROOT_GUARD = 0.001
F32, BF16 = jnp.float32, jnp.bfloat16
SIDE = 8
XBIT, CBIT = 2, 1
EXTRA = {0: 8, 6: 9}
SLOT = 288
CW = 640
HALO = 16
SHORT_ROW = 2048
UNROLL = 4


def lbit(n):
    return 8 if n == 32 else 4


def far_masks(n):
    masks, m = [], n // 2
    while m >= 4:
        if m != lbit(n):
            masks.append(m)
        m //= 2
    return masks


def row_span(n, tok):
    return SHORT_ROW // tok if n * tok == 2 * SHORT_ROW else n


def side_mask(q, n):
    return (q & 1) * XBIT | ((q >> 1) & 1) * lbit(n) | ((q >> 2) & 1) * CBIT


def side_place(d, n):
    x = (d >> (XBIT.bit_length() - 1)) & 1
    l = (d >> (lbit(n).bit_length() - 1)) & 1
    return x + l * 2 + ((d >> (CBIT.bit_length() - 1)) & 1) * 4


def side_code(i, n):
    return (i & 3) | (((i & lbit(n)) != 0) * 4)


def side_groups(n):
    low = XBIT | CBIT | lbit(n)
    return [
        sorted(b | side_mask(q, n) for q in range(SIDE)) for b in range(n) if b & low == 0
    ]


def far_groups(n):
    low = XBIT | CBIT | lbit(n)
    return [[i for i in range(n) if i & low == side_mask(q, n)] for q in range(SIDE)]


def far_mask_of(r, n):
    return sum(m for k, m in enumerate(far_masks(n)) if (r >> k) & 1)


def near_units(n, me):
    low = 2 if lbit(n) == 8 else 3
    units = []
    for r in range(n // SIDE):
        for l in range(SIDE >> low):
            u = 0
            for k, m in enumerate(far_masks(n)):
                bit = lax.shift_right_logical(me, m.bit_length() - 1) & 1
                u = u + ((bit ^ ((r >> k) & 1)) << (m.bit_length() - 1 - low))
            units.append(u + (l << (lbit(n).bit_length() - 1 - low) if low == 2 else 0))
    return units


def fixed_units(n):
    low = 2 if lbit(n) == 8 else 3
    base = [g[0] for g in side_groups(n)]
    return [
        (b | (l * lbit(n) if low == 2 else 0)) >> low for b in base for l in range(SIDE >> low)
    ]


def swap(v, mask, only=None):
    n = lax.axis_size(AXIS)
    pairs = [(i, i ^ mask) for i in range(n) if only is None or side_code(i, n) in only]
    return lax.ppermute(v, AXIS, pairs)


def dot(a, b):
    return lax.dot_general(a, b, (((1,), (0,)), ((), ())), preferred_element_type=F32)


def dot_last(a, b):
    return lax.dot_general(a, b, (((1,), (1,)), ((), ())), preferred_element_type=F32)


def dot_first(a, b):
    return lax.dot_general(a, b, (((0,), (0,)), ((), ())), preferred_element_type=F32)


def after(v, *deps):
    return lax.optimization_barrier((v, *deps))[0]


def kernel_call(kernel, ins, outs, scratch=(), smem=1, us=3):
    specs = [pl.BlockSpec(memory_space=pltpu.SMEM)] * smem
    specs += [pl.BlockSpec(memory_space=pltpu.VMEM)] * (len(ins) - smem)
    return pl.pallas_call(
        kernel,
        in_specs=specs,
        out_specs=[pl.BlockSpec(memory_space=pltpu.VMEM)] * len(outs),
        out_shape=[jax.ShapeDtypeStruct(s, d) for s, d in outs],
        scratch_shapes=list(scratch),
        compiler_params=pltpu.CompilerParams(vmem_limit_bytes=12 * 1024 * 1024),
        cost_estimate=pl.CostEstimate(
            flops=us * 10**9, bytes_accessed=us * 3 * 10**6, transcendentals=0
        ),
    )(*ins)


def gather_side(x, main=None, marks=(None, None)):
    n = lax.axis_size(AXIS)
    half = x.shape[0] // 32 * 16
    by_l, by_x = swap(x, lbit(n)), swap(x, XBIT)
    if marks[0] is not None:
        by_l, by_x = after((by_l, by_x), marks[0])
    low, high = swap(by_l[:half], XBIT), swap(by_x[half:], lbit(n))
    if marks[1] is not None:
        low, high = after((low, high), marks[1])
    if main is None:
        mine = jnp.concatenate([x, by_x, by_l, low, high])
        return mine, swap(mine, CBIT)
    cut = main - half
    mine = jnp.concatenate([x[:main], by_x[:main], by_l[:main], low, high[:cut]])
    rest = jnp.concatenate([x[main:], by_x[main:], by_l[main:], high[cut:]])
    return mine, swap(mine, CBIT), rest, swap(rest, CBIT)


def first_sum_kernel(mine, recv, send_a, send_b, keep_a, keep_b):
    tok, half = mine.shape[0] // 4, mine.shape[1] // 2
    step = 16

    def tile(i, _):
        for b in range(4):
            rows = pl.ds(pl.multiple_of(b * tok + i * step, step), step)
            at = lambda k: pl.ds(pl.multiple_of(k * tok + i * step, step), step)
            va = mine[rows, :half] + recv[rows, :half].astype(F32)
            vb = mine[rows, half:] + recv[rows, half:].astype(F32)
            if b < 2:
                keep_a[at(b), :] = va
            else:
                send_a[at(b - 2), :] = va.astype(BF16)
            if b % 2 == 0:
                keep_b[at(b // 2), :] = vb
            else:
                send_b[at(b // 2), :] = vb.astype(BF16)
        return 0

    lax.fori_loop(0, tok // step, tile, 0)


def second_sum_kernel(keep_a, recv_a, keep_b, recv_b, send_a, send_b, last):
    tok, half = send_a.shape
    step = 16

    def tile(i, _):
        own = pl.ds(pl.multiple_of(i * step, step), step)
        far = pl.ds(pl.multiple_of(tok + i * step, step), step)
        last[own, :half] = keep_a[own, :] + recv_a[own, :].astype(F32)
        last[own, half:] = keep_b[own, :] + recv_b[own, :].astype(F32)
        send_a[own, :] = (keep_a[far, :] + recv_a[far, :].astype(F32)).astype(BF16)
        send_b[own, :] = (keep_b[far, :] + recv_b[far, :].astype(F32)).astype(BF16)
        return 0

    lax.fori_loop(0, tok // step, tile, 0)


def scatter_side(mine, theirs, mark=None, mark_last=None):
    n = lax.axis_size(AXIS)
    rows, width = mine.shape
    tok, half = rows // 4, width // 2
    recv = swap(theirs, CBIT)
    send_a, send_b, keep_a, keep_b = kernel_call(
        first_sum_kernel,
        (mine, recv),
        [((2 * tok, half), BF16)] * 2 + [((2 * tok, half), F32)] * 2,
        smem=0,
    )
    recv_a, recv_b = swap(send_a, lbit(n)), swap(send_b, XBIT)
    if mark is not None:
        keep_a = after(keep_a, mark)
    send_a, send_b, last = kernel_call(
        second_sum_kernel,
        (keep_a, recv_a, keep_b, recv_b),
        [((tok, half), BF16)] * 2 + [((tok, width), F32)],
        smem=0,
    )
    parts = (last, swap(send_a, XBIT), swap(send_b, lbit(n)))
    if mark_last is not None:
        parts = after(parts, mark_last)
    return parts, keep_a, last


def rms_scale(values):
    return lax.rsqrt(jnp.mean(values * values, axis=-1, keepdims=True) + 1e-06)


def unit_slice(u, size):
    return pl.ds(pl.multiple_of(u * size, 128), size)


def put_units(out, rows, value_ref, value_rows, units, size):
    for p, u in enumerate(units):
        out[rows, p * size : (p + 1) * size] = value_ref[value_rows, unit_slice(u, size)]


def tail_kernel(x, gain, flags, out):
    v = x[...]
    out[...] = (v * rms_scale(v) * gain[...]).astype(BF16)
    row = lax.broadcasted_iota(jnp.int32, (HALO, 128), 0) == 0
    out[:, :128] = jnp.where(row, flags[...], out[:, :128].astype(F32)).astype(BF16)


ROWS = 32


def norm_one_kernel(n, me, x, gain, flags, tail, out, held):
    units = near_units(n, me[0])
    size = x.shape[1] // len(units)
    tok = x.shape[0]
    for i in range(tok // ROWS):
        rows = slice(i * ROWS, (i + 1) * ROWS)
        v = x[rows, :]
        held[...] = v * rms_scale(v) * gain[...]
        for p, u in enumerate(units):
            out[rows, p * size : (p + 1) * size] = held[:, unit_slice(u, size)].astype(BF16)
    halo = slice(tok, tok + HALO)
    put_units(out, halo, tail, slice(0, HALO), units, size)
    row = lax.broadcasted_iota(jnp.int32, (HALO, 128), 0)
    first = out[halo, :128].astype(F32)
    both = jnp.where(row == 0, flags[...], first)
    both = jnp.where(row == 1, tail[:, :128].astype(F32)[0:1], both)
    out[halo, :128] = both.astype(BF16)


def top_kernel(n, g, out):
    units = fixed_units(n)
    size = g.shape[1] // len(units)
    for p, u in enumerate(units):
        out[:, p * size : (p + 1) * size] = g[:, u * size : (u + 1) * size].astype(BF16)


def summed(last, ra, rb, rows, p, size):
    half = ra.shape[1]
    a, b = p * size, (p + 1) * size
    if b <= half:
        extra = ra[rows, a:b]
    else:
        extra = rb[rows, a - half : b - half]
    return last[rows, a:b] + extra.astype(F32)


def norm_two_kernel(n, me, x, gain, last, ra, rb, middle, out, held):
    units = near_units(n, me[0])
    size = x.shape[1] // len(units)
    for i in range(x.shape[0] // ROWS):
        rows = slice(i * ROWS, (i + 1) * ROWS)
        for p, u in enumerate(units):
            held[:, unit_slice(u, size)] = summed(last, ra, rb, rows, p, size)
        v = held[...] + x[rows, :]
        middle[rows, :] = v
        w = (v * rms_scale(v) * gain[...]).astype(BF16)
        for p, u in enumerate(fixed_units(n)):
            out[rows, p * size : (p + 1) * size] = w[:, u * size : (u + 1) * size]


def add_kernel(n, middle, last, ra, rb, out):
    units = fixed_units(n)
    size = middle.shape[1] // len(units)
    for p, u in enumerate(units):
        at = slice(u * size, (u + 1) * size)
        out[:, at] = middle[:, at] + summed(last, ra, rb, slice(None), p, size)


def norm_back(grad_normed, values, gain):
    scale = rms_scale(values)
    scaled = grad_normed * gain
    back = scale * scaled - values * (scale * scale * scale) * jnp.mean(
        scaled * values, axis=-1, keepdims=True
    )
    return back, grad_normed * values * scale


def middle_back_kernel(n, me, values, base, gain, last, ra, rb, grad, branch, gain_grad, held):
    units = near_units(n, me[0])
    size = values.shape[1] // len(units)
    total = jnp.zeros((1, values.shape[1]), F32)
    for i in range(values.shape[0] // ROWS):
        rows = slice(i * ROWS, (i + 1) * ROWS)
        for p, u in enumerate(fixed_units(n)):
            held[:, u * size : (u + 1) * size] = summed(last, ra, rb, rows, p, size)
        back, part = norm_back(held[...], values[rows, :], gain[...])
        total = total + jnp.sum(part, axis=0, keepdims=True)
        out = base[rows, :] + back
        grad[rows, :] = out
        held[...] = out
        for p, u in enumerate(units):
            branch[rows, p * size : (p + 1) * size] = held[:, unit_slice(u, size)].astype(BF16)
    gain_grad[...] = total


def input_back_kernel(n, me, values, base, gain, last, ra, rb, grad, gain_grad, held):
    units = near_units(n, me[0])
    size = values.shape[1] // len(units)
    total = jnp.zeros((1, values.shape[1]), F32)
    for i in range(values.shape[0] // ROWS):
        rows = slice(i * ROWS, (i + 1) * ROWS)
        for p, u in enumerate(units):
            held[:, unit_slice(u, size)] = summed(last, ra, rb, rows, p, size)
        back, part = norm_back(held[...], values[rows, :], gain[...])
        total = total + jnp.sum(part, axis=0, keepdims=True)
        grad[rows, :] = base[rows, :] + back
    gain_grad[...] = total


def gelu_pair(v):
    k = 0.7978845608028654
    sq = v * v
    th = jnp.tanh(k * v * (1.0 + 0.044715 * sq))
    half = 0.5 * (1.0 + th)
    slope = half + 0.5 * v * (1.0 - th * th) * (k * (1.0 + 3.0 * 0.044715 * sq))
    return v * half, slope


def strided(i, tok):
    return pl.ds(i, SIDE, stride=tok)


TILES = CW // 128


def cols(c):
    return slice(c * 128, (c + 1) * 128)


def join(tiles):
    return jnp.concatenate(tiles, axis=1)


def stepwise(tok, step, state, reverse=False):
    def some(o, state):
        for k in range(UNROLL):
            i = o * UNROLL + k
            state = step(tok - 1 - i if reverse else i, state)
        return state

    return lax.fori_loop(0, tok // UNROLL, some, state)


def step_rows(i):
    return pl.ds(pl.multiple_of(i * SIDE, SIDE), SIDE)


def mixer_kernel(
    lin_mine, lin_theirs, halo, keep, halo_keep, taps, r_sq, i_sq, vec,
    lin, low, rg, ig, dec, acc, loc, before, totals, conv,
):
    tok = conv.shape[1] // SIDE
    four = 4 * tok
    for c in range(TILES):
        lin[c, :four, :] = lin_mine[:, CW + c * 128 : CW + (c + 1) * 128]
        lin[c, four:, :] = lin_theirs[:, CW + c * 128 : CW + (c + 1) * 128]
        conv[c, : SIDE * HALO, :] = halo[:, cols(c)]
        for k in range(3):
            before[c, k * SIDE : (k + 1) * SIDE, :] = conv[c, strided(HALO - 1 - k, HALO), :]

    for c in range(TILES):
        t0, t1, t2, t3 = (taps[k : k + 1, cols(c)] for k in range(4))
        bias = vec[0:1, cols(c)]

        def conv_step(i, state):
            v1, v2, v3, k1, k2 = state
            v0 = lin[c, strided(i, tok), :]
            k0 = keep[step_rows(i), :]
            conv[c, strided(i, tok), :] = (
                v0 * t0 + bias + k0 * (v1 * t1 + k1 * (v2 * t2 + k2 * (v3 * t3)))
            )
            return v0, v1, v2, k0, k1

        start = tuple(before[c, k * SIDE : (k + 1) * SIDE, :] for k in range(3))
        start += (halo_keep[2 * SIDE :, :], halo_keep[SIDE : 2 * SIDE, :])
        stepwise(tok, conv_step, start)

    def gates(b, _):
        rows = pl.ds(pl.multiple_of(b * tok, tok), tok)
        low_here = join([conv[c, rows, :].astype(BF16) for c in range(TILES)])
        low[rows, :] = low_here
        r = jax.nn.sigmoid(dot(low_here, r_sq[...]) + vec[1:2, :])
        i = jax.nn.sigmoid(dot(low_here, i_sq[...]) + vec[2:3, :])
        for c in range(TILES):
            conv[c, rows, :] = low_here[:, cols(c)].astype(F32)
            rg[c, rows, :] = r[:, cols(c)]
            ig[c, rows, :] = i[:, cols(c)]
        return 0

    lax.fori_loop(0, SIDE, gates, 0)

    def scan_step(i, state):
        at = strided(i, tok)
        k0 = keep[step_rows(i), :]
        out = []
        for c in range(TILES):
            p, s = state[c]
            a = jnp.exp(rg[c, at, :] * vec[3:4, cols(c)]) * k0
            root = jnp.sqrt(1.0 - a * a + ROOT_GUARD)
            b = (k0 * root + (1.0 - k0)) * ig[c, at, :] * conv[c, at, :]
            p, s = p * a, a * s + b
            dec[c, at, :] = a
            acc[c, at, :] = p
            loc[c, at, :] = s
            out.append((p, s))
        return tuple(out)

    shape = (SIDE, 128)
    start = tuple((jnp.ones(shape, F32), jnp.zeros(shape, F32)) for _ in range(TILES))
    found = stepwise(tok, scan_step, start)
    for c in range(TILES):
        totals[:SIDE, cols(c)], totals[SIDE:, cols(c)] = found[c]


def gelu_kernel(gate_mine, gate_theirs, act, slope):
    four = gate_mine.shape[0]

    def tile(i, _):
        rows = pl.ds(pl.multiple_of(i * 16, 16), 16)
        later = pl.ds(pl.multiple_of(four + i * 16, 16), 16)
        for src, dst in ((gate_mine, rows), (gate_theirs, later)):
            for c in range(TILES):
                act[c, dst, :], slope[c, dst, :] = gelu_pair(src[rows, cols(c)])
        return 0

    lax.fori_loop(0, four // 16, tile, 0)


def chain_kernel(n, span, reverse, me_ref, *refs):
    *parts, out, held = refs
    me = me_ref[0]
    state = jnp.zeros((1, CW), F32)
    order = range(span - 1, -1, -1) if reverse else range(span)
    near = [m for m in far_masks(n) if m < span]

    def place(d):
        r = 0
        for k, m in enumerate(near):
            r = r + (((d >> (m.bit_length() - 1)) & 1) << k)
        return r, side_place(d, n)

    both = 2 * SIDE
    for r, part in enumerate(parts):
        for k in range(both):
            held[r * both + k, 0:1, :] = part[k : k + 1, :]
    base = len(parts) * both
    for i in order:
        r, q = place((me & (span - 1)) ^ i)
        held[base + i, 0:1, :] = state
        scale = held[r * both + q, 0:1, :]
        value = held[r * both + SIDE + q, 0:1, :]
        state = scale * state + value
    for q in range(SIDE):
        at = base + ((me & (span - 1)) ^ side_mask(q, n))
        out[q, :, :] = jnp.broadcast_to(held[at, 0:1, :], (8, CW))


def states_kernel(acc, loc, incoming, act, slope, states, mixed, slope_states):
    tok = acc.shape[1] // SIDE
    for q in range(SIDE):

        def tile(i, _):
            rows = pl.ds(pl.multiple_of(q * tok + i * 16, 16), 16)
            out = []
            for c in range(TILES):
                s = loc[c, rows, :] + acc[c, rows, :] * incoming[q, 0:1, cols(c)]
                states[c, rows, :] = s
                slope_states[c, rows, :] = s * slope[c, rows, :]
                out.append((s * act[c, rows, :]).astype(BF16))
            mixed[rows, :] = join(out)
            return 0

        lax.fori_loop(0, tok // 16, tile, 0)


def back_scan_kernel(gm_mine, gm_theirs, act, dec, grads, suffix, totals):
    tok = act.shape[1] // SIDE
    four = 4 * tok
    for c in range(TILES):
        grads[c, :four, :] = gm_mine[:, cols(c)] * act[c, :four, :]
        grads[c, four:, :] = gm_theirs[:, cols(c)] * act[c, four:, :]

    def step(i, state):
        at = strided(i, tok)
        out = []
        for c in range(TILES):
            ag, aq = state[c]
            g = grads[c, at, :] + ag
            grads[c, at, :] = g
            suffix[c, at, :] = aq
            a = dec[c, at, :]
            out.append((a * g, a * aq))
        return tuple(out)

    shape = (SIDE, 128)
    start = tuple((jnp.zeros(shape, F32), jnp.ones(shape, F32)) for _ in range(TILES))
    found = stepwise(tok, step, start, True)
    for c in range(TILES):
        totals[SIDE:, cols(c)], totals[:SIDE, cols(c)] = found[c]


def gate_back_kernel(gm_mine, gm_theirs, slope_states, out):
    four = gm_mine.shape[0]

    def tile(i, _):
        rows = pl.ds(pl.multiple_of(i * 16, 16), 16)
        later = pl.ds(pl.multiple_of(four + i * 16, 16), 16)
        for src, dst in ((gm_mine, rows), (gm_theirs, later)):
            out[dst, :] = join(
                [(src[rows, cols(c)] * slope_states[c, dst, :]).astype(BF16) for c in range(TILES)]
            )
        return 0

    lax.fori_loop(0, four // 16, tile, 0)


def mixer_back_kernel(
    grads, suffix, from_later, dec, rg, ig, low, states, incoming, lin, before, keep, halo_keep,
    keep_rows, r_sq, i_sq, vec, g_reset, g_input, g_conv, sums, heads,
):
    tok = dec.shape[1] // SIDE
    zero = jnp.zeros((1, 128), F32)

    def block(b, totals):
        rows = pl.ds(pl.multiple_of(b * tok, tok), tok)
        k = keep_rows[rows, :]
        at_first = lax.broadcasted_iota(jnp.int32, (tok, 128), 0) == 0
        out, g_rs, g_is, base = [], [], [], []
        for c in range(TILES):
            gs = grads[c, rows, :] + suffix[c, rows, :] * from_later[b, 0:1, cols(c)]
            a, r, i_g = dec[c, rows, :], rg[c, rows, :], ig[c, rows, :]
            v = low[rows, cols(c)].astype(F32)
            root = jnp.sqrt(1.0 - a * a + ROOT_GUARD)
            mult = k * root + (1.0 - k)
            prior = pltpu.roll(states[c, rows, :], 1, 0)
            prior = jnp.where(at_first, incoming[b, 0:1, cols(c)], prior)
            gv = gs * v
            glr = a * (gs * prior - gv * i_g * a / root) * r
            g_r = (vec[3:4, cols(c)] * glr * (1.0 - r)).astype(BF16)
            gm = gs * mult * i_g
            g_i = (gm * v * (1.0 - i_g)).astype(BF16)
            out.append(
                (
                    totals[c][0] + jnp.sum(glr, axis=0, keepdims=True),
                    totals[c][1] + jnp.sum(g_r.astype(F32), axis=0, keepdims=True),
                    totals[c][2] + jnp.sum(g_i.astype(F32), axis=0, keepdims=True),
                )
            )
            g_rs.append(g_r)
            g_is.append(g_i)
            g_conv[c, rows, :] = gm
        g_r, g_i = join(g_rs), join(g_is)
        g_reset[rows, :] = g_r
        g_input[rows, :] = g_i
        more = dot_last(g_r, r_sq[...]) + dot_last(g_i, i_sq[...])
        for c in range(TILES):
            g_conv[c, rows, :] = g_conv[c, rows, :] + more[:, cols(c)]
        return tuple(out)

    found = lax.fori_loop(0, SIDE, block, ((zero,) * 3,) * TILES)
    for c in range(TILES):
        dec_sum, r_sum, i_sum = found[c]
        sums[0:1, cols(c)] = r_sum
        sums[1:2, cols(c)] = i_sum
        sums[2:3, cols(c)] = -vec[4:5, cols(c)] * dec_sum

    blank = jnp.zeros((SIDE, 128), F32)
    for c in range(TILES):

        def tap_step(i, state):
            v1, v2, v3, k1, k2, s0, s1, s2, s3, sb = state
            v0 = lin[c, strided(i, tok), :]
            k0 = keep[step_rows(i), :]
            g0 = g_conv[c, strided(i, tok), :]
            g1 = g0 * k0
            g2 = g1 * k1
            g3 = g2 * k2
            return (
                (v0, v1, v2, k0, k1)
                + (s0 + g0 * v0, s1 + g1 * v1, s2 + g2 * v2, s3 + g3 * v3, sb + g0)
            )

        start = tuple(before[c, k * SIDE : (k + 1) * SIDE, :] for k in range(3))
        start += (halo_keep[2 * SIDE :, :], halo_keep[SIDE : 2 * SIDE, :]) + (blank,) * 5
        end = stepwise(tok, tap_step, start)
        per_row = [jnp.sum(v, axis=0, keepdims=True) for v in end[5:]]
        sums[3:4, cols(c)] = per_row[4]
        for j in range(4):
            sums[4 + j : 5 + j, cols(c)] = per_row[j]
        k = None
        for i in range(3):
            k_i = keep[i * SIDE : (i + 1) * SIDE, :]
            k = k_i if k is None else k * k_i
            heads[i * SIDE : (i + 1) * SIDE, cols(c)] = g_conv[c, strided(i, tok), :] * k


def linear_back_kernel(n, span, me_ref, g_conv, keep, taps, *refs):
    *parts, out, held, after, conv = refs
    me = me_ref[0]
    tok = g_conv.shape[1] // SIDE
    rows3 = 3 * SIDE
    for k, part in enumerate(parts):
        for m in range(rows3):
            held[k * rows3 + m, 0:1, :] = part[m : m + 1, :]
    low_far = far_masks(n)[-1]
    side = XBIT | CBIT | lbit(n)
    for q in range(SIDE):
        nxt = (me ^ side_mask(q, n)) + 1
        d = nxt ^ me
        far = d & ~side
        ok = ((nxt & (span - 1)) != 0).astype(F32)
        which = jnp.where(far == 0, 0, jnp.where(far == low_far, 1, len(parts) - 1))
        for m in range(3):
            at = which * rows3 + m * SIDE + side_place(d, n)
            after[m * SIDE + q : m * SIDE + q + 1, :] = held[at, 0:1, :] * ok
    one = jnp.ones((SIDE, 128), F32)
    for c in range(TILES):
        t0, t1, t2, t3 = (taps[k : k + 1, cols(c)] for k in range(4))

        def step(i, state):
            g1, g2, g3, k1, k2, k3 = state
            g0 = g_conv[c, strided(i, tok), :]
            conv[c, strided(i, tok), :] = g0 * t0 + k1 * (g1 * t1 + k2 * (g2 * t2 + k3 * (g3 * t3)))
            return g0, g1, g2, keep[step_rows(i), :], k1, k2

        start = tuple(after[m * SIDE : (m + 1) * SIDE, cols(c)] for m in range(3))
        stepwise(tok, step, start + (one, one, one), True)

    def tile(i, _):
        rows = pl.ds(pl.multiple_of(i * 16, 16), 16)
        out[rows, :] = join([conv[c, rows, :].astype(BF16) for c in range(TILES)])
        return 0

    lax.fori_loop(0, SIDE * tok // 16, tile, 0)


def heads_kernel(blk, gate, linear, out_w, first, second):
    first[...] = jnp.zeros(first.shape, BF16)
    second[...] = jnp.zeros(second.shape, BF16)
    for k, w in enumerate((gate, linear, out_w)):
        at = slice(k * SLOT, k * SLOT + blk)
        for s in range(SIDE):
            first[s, :, at] = w[:, s * blk : (s + 1) * blk]
        for s, e in EXTRA.items():
            second[s, :, at] = w[:, e * blk : (e + 1) * blk]


def feed_parts_kernel(*refs):
    *weights, out = refs
    size = out.shape[2] // len(weights)
    for k, w in enumerate(weights):
        for s in range(SIDE):
            out[s, :, k * size : (k + 1) * size] = w[:, s * size : (s + 1) * size]


def feed_join_kernel(parts, *outs):
    size = parts.shape[2] // len(outs)
    for k, out in enumerate(outs):
        for s in range(SIDE):
            out[:, s * size : (s + 1) * size] = parts[s, :, k * size : (k + 1) * size].astype(F32)


def turn_kernel(parts, *outs):
    rows = parts.shape[1]
    turned = parts[...].reshape(SIDE * rows, parts.shape[2]).T
    at = 0
    for out in outs:
        out[...] = turned[at : at + out.shape[0]]
        at += out.shape[0]


def assemble_kernel(count, which, *refs):
    first, extra, out = refs[:count], refs[count : 2 * count], refs[2 * count]
    size = first[0].shape[1]
    for r in range(count):
        lanes = slice(r * size, (r + 1) * size)
        for m, k in enumerate(which):
            out[m * CW : m * CW + SLOT, lanes] = first[r][m * SLOT : (m + 1) * SLOT, :]
            out[m * CW + SLOT : m * CW + 2 * SLOT, lanes] = extra[r][k * SLOT : (k + 1) * SLOT, :]
            out[m * CW + 2 * SLOT : (m + 1) * CW, lanes] = jnp.zeros((CW - 2 * SLOT, size), BF16)


def turn_back_kernel(*refs):
    *parts, out = refs
    rows = out.shape[1]
    flat = jnp.concatenate([p[...] for p in parts])
    out[:, :, : flat.shape[0]] = flat.T.reshape(SIDE, rows, flat.shape[0])


def head_rows_kernel(blk, parts, *outs):
    count = len(outs)
    for k, out in enumerate(outs):
        for s in range(SIDE):
            at = k * SLOT
            out[:, s * blk : (s + 1) * blk] = parts[s, :, at : at + blk].astype(F32)
        for s, e in EXTRA.items():
            at = (count + k) * SLOT
            out[:, e * blk : (e + 1) * blk] = parts[s, :, at : at + blk].astype(F32)


def packs_kernel(n, blk, me_ref, mine, theirs, eight, nine, r_out, i_out, vec_out):
    me = me_ref[0]

    def put(ref, e, shift):
        def lanes(v):
            return v[:, shift : shift + blk]

        r_out[e, :, :] = lanes(ref[:SLOT, :384].astype(F32))[:blk]
        i_out[e, :, :] = lanes(ref[:SLOT, 384:].astype(F32))[:blk]
        vec_out[:, e * blk : (e + 1) * blk] = lanes(ref[SLOT:, :384].astype(F32)[:8])

    for s in range(SIDE):
        i = (s & 3) | ((s >> 2) * lbit(n))
        d = jnp.int32(i) ^ (me & (XBIT | CBIT | lbit(n)))
        q = ((d >> (XBIT.bit_length() - 1)) & 1) + ((d >> (lbit(n).bit_length() - 1)) & 1) * 2
        own = ((d >> (CBIT.bit_length() - 1)) & 1) == 0

        @pl.when(own)
        def _():
            put(mine.at[q], s, 0)

        @pl.when(jnp.logical_not(own))
        def _():
            put(theirs.at[q], s, 0)

    put(eight, EXTRA[0], 32)
    put(nine, EXTRA[6], 32)


def body(
    block_input,
    start_flags,
    norm_gain,
    gate_weight,
    linear_weight,
    conv_taps,
    conv_bias,
    reset_weight,
    reset_bias,
    input_weight,
    input_bias,
    decay_param,
    out_weight,
    feed_norm_gain,
    feed_gate_weight,
    feed_value_weight,
    feed_down_weight,
    output_grad,
):
    n = lax.axis_size(AXIS)
    me = lax.axis_index(AXIS)
    me1 = me.reshape(1)
    here = side_code(me, n)
    tok, width = block_input.shape
    heads_count, blk = reset_weight.shape[:2]
    rows_w = gate_weight.shape[0]
    feed = feed_gate_weight.shape[1]
    fs = feed // SIDE
    masks = far_masks(n)
    groups, far = side_groups(n), far_groups(n)
    only = tuple(EXTRA)
    has_extra = (here == only[0]) | (here == only[1])
    extra_here = jnp.where(here == only[1], EXTRA[only[1]], EXTRA[only[0]])
    four = 4 * tok
    side_tok = SIDE * tok
    cols_w = SIDE * rows_w
    places = n // SIDE
    count = len(masks)

    def exchange(v):
        return lax.all_to_all(v, AXIS, 0, 0, axis_index_groups=groups, tiled=True)

    def gather_far(x, sel=None):
        chunks = [x]
        for m in masks:
            chunks += [swap(c, m, sel) for c in chunks]
        return chunks

    gain_one = norm_gain.astype(F32)[None]
    gain_two = feed_norm_gain.astype(F32)[None]
    flags = start_flags.astype(F32)[None]
    parts, more_parts = kernel_call(
        functools.partial(heads_kernel, blk),
        (gate_weight, linear_weight, out_weight),
        [((SIDE, rows_w, 3 * SLOT + 32), BF16)] * 2,
        smem=0,
    )
    tail = kernel_call(
        tail_kernel,
        (after(block_input[-HALO:], parts), gain_one, flags),
        [((HALO, width), BF16)],
        smem=0,
        us=1,
    )[0]
    tail = lax.ppermute(tail, AXIS, [(i, i + 1) for i in range(n - 1)])
    packet = kernel_call(
        functools.partial(norm_one_kernel, n),
        (me1, block_input, gain_one, flags, tail),
        [((tok + HALO, width), BF16)],
        [pltpu.VMEM((ROWS, width), F32)],
    )[0]
    f_parts = kernel_call(
        feed_parts_kernel,
        (after(feed_value_weight, packet), feed_gate_weight, feed_down_weight),
        [((SIDE, rows_w, 3 * fs), BF16)],
        smem=0,
    )[0]
    top = kernel_call(
        functools.partial(top_kernel, n),
        (after(output_grad, f_parts),),
        [((tok, width), BF16)],
        smem=0,
    )[0]
    parts = exchange(parts)
    p_mix, p_out = kernel_call(
        turn_kernel, (parts,), [((k * SLOT, cols_w), BF16) for k in (2, 1)], smem=0
    )
    more_parts = exchange(after(more_parts, parts))
    f_parts = exchange(after(f_parts, more_parts))
    p_extra = kernel_call(turn_kernel, (more_parts,), [((3 * SLOT, cols_w), BF16)], smem=0)[0]

    def gather_start(x, count=2, sel=None):
        return [x] + [swap(x, m, sel) for m in masks[:count]]

    def gather_later(chunks, sel=None, mark=None):
        chunks = list(chunks)
        if mark is not None:
            chunks[1] = after(chunks[1], mark)
        if len(chunks) == 3:
            chunks.append(swap(chunks[1], masks[1], sel))
        for m in masks[len(chunks).bit_length() - 1 :]:
            chunks += [swap(c, m, sel) for c in chunks]
        return chunks

    packet = after(packet, p_mix)
    c_mix = gather_start(p_mix)
    half = tok // 2
    by_l, by_x = swap(packet, lbit(n)), swap(packet, XBIT)
    (c_mix, by_l, by_x, p_extra) = lax.optimization_barrier((c_mix, by_l, by_x, p_extra))
    c_mix = gather_later(c_mix)
    c_extra = gather_start(p_extra, 1, only)
    low, high = swap(by_l[:half], XBIT), swap(by_x[half:], lbit(n))
    (c_mix, c_extra, low, high, p_out) = lax.optimization_barrier(
        (c_mix, c_extra, low, high, p_out)
    )
    f_parts = after(f_parts, c_extra)
    c_extra = gather_later(c_extra, only)
    c_out = gather_start(p_out, 1)
    f_parts = f_parts.reshape(cols_w, 3 * fs)
    norm_mine = jnp.concatenate([packet[:tok], by_x[:tok], by_l[:tok], low, high[:half]])
    halo_mine = jnp.concatenate([packet[tok:], by_x[tok:], by_l[tok:], high[half:]])
    norm_theirs, halo_theirs = swap(norm_mine, CBIT), swap(halo_mine, CBIT)
    w_mix = kernel_call(
        functools.partial(assemble_kernel, places, (0, 1)),
        (*c_mix, *c_extra),
        [((2 * CW, width), BF16)],
        smem=0,
        us=5,
    )[0]
    c_out = gather_later([after(p_out, w_mix), c_out[1]], mark=w_mix)
    w_mix = after(w_mix, tuple(f_parts))

    def feed_full(part):
        return lax.all_gather(part, AXIS, axis_index_groups=far, tiled=True)

    w_first, w_value = feed_full(f_parts[:, fs:]), feed_full(f_parts[:, :fs])
    w_gate, w_down = w_first[:, :fs], w_first[:, fs:]

    def pick(p):
        one = lax.dynamic_index_in_dim(p, here, 0, False)
        two = lax.dynamic_index_in_dim(p, extra_here, 0, False)
        return one, jnp.where(has_extra, two, jnp.zeros_like(two))

    vectors = jnp.concatenate(
        [conv_taps]
        + [v[None] for v in (conv_bias, reset_bias, input_bias, decay_param)]
    ).astype(F32)
    vectors = vectors.reshape(8, heads_count, blk).transpose(1, 0, 2)
    vec_one, vec_two = pick(vectors)
    gap = ((0, 0), (0, SLOT - blk))
    vectors = jnp.concatenate([jnp.pad(vec_one, gap), jnp.pad(vec_two, gap)], axis=1)
    vectors = jnp.pad(vectors, ((0, 0), (0, CW - 2 * SLOT)))
    taps = vectors[:4]
    decay_float = vectors[7]
    vec = jnp.concatenate(
        [
            vectors[4:7],
            (-8.0 * jax.nn.softplus(-decay_float))[None],
            (-8.0 * jax.nn.sigmoid(-decay_float))[None],
            jnp.zeros((3, CW), F32),
        ]
    )

    def square(p):
        one, two = pick(p)
        low = CW - SLOT - blk
        return jnp.pad(one, ((0, CW - blk),) * 2) + jnp.pad(two, ((SLOT, low),) * 2)

    r_sq, i_sq = square(reset_weight), square(input_weight)

    halo_all = jnp.concatenate([halo_mine, halo_theirs])
    flag_rows = halo_all.reshape(SIDE, HALO, width)[:, :2, :128].astype(F32)
    keep_blocks = 1.0 - flag_rows[:, 0]
    keep = jnp.broadcast_to(keep_blocks.T[:, :, None], (tok, SIDE, 128)).reshape(side_tok, 128)
    keep_rows = jnp.broadcast_to(keep_blocks[:, :, None], (SIDE, tok, 128)).reshape(side_tok, 128)
    halo_keep = 1.0 - flag_rows[:, 1, tok - 3 :]
    halo_keep = jnp.broadcast_to(halo_keep.T[:, :, None], (3, SIDE, 128)).reshape(3 * SIDE, 128)

    pre_mine, pre_theirs = dot_last(norm_mine, w_mix), dot_last(norm_theirs, w_mix)
    halo = dot_last(halo_all, w_mix[CW:])
    top = after(top, w_mix)
    top_l, top_x = swap(top, lbit(n)), swap(top, XBIT)
    flat, wide = (side_tok, CW), (TILES, side_tok, 128)
    lin, low, rg, ig, dec, acc, loc, before, totals = kernel_call(
        mixer_kernel,
        (pre_mine, pre_theirs, halo, keep, halo_keep, taps, r_sq, i_sq, vec),
        [(wide, F32), (flat, BF16)]
        + [(wide, F32)] * 5
        + [((TILES, 3 * SIDE, 128), F32), ((2 * SIDE, CW), F32)],
        [pltpu.VMEM(wide, F32)],
        smem=0,
        us=29,
    )

    span = row_span(n, tok)

    def chain(totals, reverse, mark):
        near = [far_mask_of(r, n) for r in range(1, n // SIDE)]
        parts = [totals] + [swap(totals, m) for m in near if m < span]
        parts = after(tuple(parts), mark)
        return kernel_call(
            functools.partial(chain_kernel, n, span, reverse),
            (me1, *parts),
            [((SIDE, 8, CW), F32)],
            [pltpu.VMEM((len(parts) * 2 * SIDE + span, 8, CW), F32)],
            us=2,
        )[0]

    top_l, top_x = after((top_l, top_x), totals)
    top_low, top_high = swap(top_l[: tok // 2], XBIT), swap(top_x[tok // 2 :], lbit(n))
    gate_halves = after((pre_mine, pre_theirs), totals, top_l)
    act, slope = kernel_call(gelu_kernel, gate_halves, [(wide, F32)] * 2, smem=0, us=7)
    c_out, c_extra = after((tuple(c_out), tuple(c_extra)), act)
    w_out = kernel_call(
        functools.partial(assemble_kernel, places, (2,)),
        (*c_out, *c_extra),
        [((CW, width), BF16)],
        smem=0,
    )[0]
    incoming = chain(totals, False, w_out)
    top_mine = jnp.concatenate([top, top_x, top_l, top_low, top_high])
    incoming = after(incoming, top_low, top_high)
    states, mixed, slope_states = kernel_call(
        states_kernel,
        (acc, loc, incoming, act, slope),
        [(wide, F32), (flat, BF16), (wide, F32)],
        smem=0,
        us=8,
    )
    theirs = dot(mixed[four:], w_out).astype(BF16)
    mixed_mine = after(mixed[:four], theirs)
    parts, mark_one, mark_two = scatter_side(dot(mixed_mine, w_out), theirs)
    top_theirs = swap(after(top_mine, mark_one), CBIT)
    gh_mine = dot(after(top_mine, mark_one), w_down)
    parts = after(parts, gh_mine)
    held = pltpu.VMEM((ROWS, width), F32)
    middle, normed_two = kernel_call(
        functools.partial(norm_two_kernel, n),
        (me1, block_input, gain_two, *parts),
        [((tok, width), F32), ((tok, width), BF16)],
        [held],
    )

    gh_theirs = dot(after(top_theirs, normed_two), w_down)
    two_mine, two_theirs = gather_side(normed_two, marks=(gh_theirs, None))

    def feed_half(two, inner_gate, grad_hidden):
        inner_value = dot(two, w_value)
        act, slope = gelu_pair(inner_gate)
        hidden = (act * inner_value).astype(BF16)
        grad_ig = (grad_hidden * inner_value * slope).astype(BF16)
        grad_iv = (grad_hidden * act).astype(BF16)
        return hidden, jnp.concatenate([grad_ig, grad_iv], axis=1)

    ig_mine, ig_theirs = dot(two_mine, w_gate), dot(two_theirs, w_gate)
    hid_t, gi_t = feed_half(after(two_theirs, ig_mine), ig_theirs, gh_theirs)
    back_t = (dot_last(gi_t[:, :fs], w_gate) + dot_last(gi_t[:, fs:], w_value)).astype(BF16)
    two_mine = after(two_mine, back_t)
    hid_m, gi_m = feed_half(two_mine, ig_mine, gh_mine)
    back_m = dot_last(gi_m[:, :fs], w_gate) + dot_last(gi_m[:, fs:], w_value)

    def feed_grad(a_m, b_m, a_t, b_t, mark):
        a_m, a_t = after((a_m, a_t), mark)
        return (dot_first(a_m, b_m) + dot_first(a_t, b_t)).astype(BF16)

    def halve(x, m, axis, mark, sel):
        half = x.shape[axis] // 2
        kept = lax.slice_in_dim(x, 0, half, axis=axis)
        got = swap(lax.slice_in_dim(x, half, 2 * half, axis=axis), m, sel)
        if mark is not None:
            got = after(got, mark)
        return (kept.astype(F32) + got.astype(F32)).astype(BF16)

    def far_first(x, axis, mark=None, sel=None):
        return halve(x, masks[-1], axis, mark, sel)

    def far_rest(x, axis, mark=None, sel=None):
        for m in reversed(masks[:-1]):
            x = halve(x, m, axis, mark, sel)
        return x

    parts, mark_one, mark_two = scatter_side(back_m, back_t)
    feed_mark = mark_two
    fg_down = feed_grad(top_mine, hid_m, top_theirs, hid_t, mark_one)
    hid_t, hid_m = after((hid_t, hid_m), mark_two, fg_down)
    out_t = dot_last(hid_t, w_down).astype(BF16)
    out_m = dot_last(after(hid_m, out_t), w_down)
    parts = after(parts, out_m)
    grad_middle, branch, gain_grad_two = kernel_call(
        functools.partial(middle_back_kernel, n),
        (me1, middle, output_grad, gain_two, *parts),
        [((tok, width), F32), ((tok, width), BF16), ((1, width), F32)],
        [held],
    )
    fg_pair = feed_grad(two_mine, gi_m, two_theirs, gi_t, branch)
    branch_mine, branch_theirs = gather_side(branch, marks=(fg_pair, None))

    gm_theirs = dot_last(branch_theirs, w_out)
    gm_mine = dot_last(branch_mine, w_out)
    grads, suffix, totals = kernel_call(
        back_scan_kernel,
        (gm_mine, gm_theirs, act, dec),
        [(wide, F32), (wide, F32), ((2 * SIDE, CW), F32)],
        smem=0,
        us=16,
    )
    scan_done = totals
    slope_states = after(slope_states, totals)
    grad_gate = kernel_call(
        gate_back_kernel, (gm_mine, gm_theirs, slope_states), [(flat, BF16)], smem=0
    )[0]

    def mixer_grad(grad, mine, theirs):
        return (dot_first(grad[:four], mine) + dot_first(grad[four:], theirs)).astype(BF16)

    def feed_send(shard):
        return exchange(shard.reshape(SIDE, rows_w, shard.shape[1]))

    def feed_rows(v, mark):
        kinds = v.shape[2] // fs
        return kernel_call(
            feed_join_kernel, (after(v, mark),), [((rows_w, feed), F32)] * kinds, smem=0, us=2
        )

    mixed_late = after(mixed, grad_gate)
    go = mixer_grad(mixed_late, branch_mine, branch_theirs)
    def feed_sum(g):
        return lax.psum_scatter(g, AXIS, axis_index_groups=far, tiled=True)

    down_sum = feed_sum(after(fg_down, feed_mark))
    pair_sum = feed_sum(fg_pair)
    sent_down = feed_send(after(down_sum, scan_done))
    from_later = chain(totals, True, (go, sent_down))
    go = after(go, from_later)
    go0, go1 = far_first(go[:SLOT], 1), far_first(go[SLOT : 2 * SLOT], 1, None, only)
    g_reset, g_input, g_conv, sums, heads = kernel_call(
        mixer_back_kernel,
        (
            grads, suffix, from_later, dec, rg, ig, low, states, incoming, lin, before, keep,
            halo_keep, keep_rows, r_sq, i_sq, vec,
        ),
        [(flat, BF16)] * 2 + [(wide, F32), ((8, CW), F32), ((3 * SIDE, CW), F32)],
        smem=0,
        us=21,
    )
    heads_y = swap(heads, masks[-1])
    head_parts = [heads, heads_y]
    if span == n:
        low_far = masks[-1]
        side = XBIT | CBIT | lbit(n)
        pairs = []
        for i in range(n):
            for j in range(n):
                last = (i | side) + 1
                if last < n and (j & ~side) == (last & ~side) and (j & side) == (i & side):
                    if ((i ^ j) & ~side) != low_far:
                        pairs.append((j, i))
        head_parts.append(lax.ppermute(heads, AXIS, pairs))
    low_late = after(low, heads, go0, go1)
    sq_r, sq_i = dot_first(low_late, g_reset), dot_first(low_late, g_input)

    rows = SLOT + HALO

    def pack(slot):
        r0, c0 = slot * SLOT, slot * 256
        squares = jnp.concatenate(
            [sq_r[r0 : r0 + SLOT, c0 : c0 + 384], sq_i[r0 : r0 + SLOT, c0 : c0 + 384]], axis=1
        )
        vecs = jnp.pad(sums[:, c0 : c0 + 384], ((0, 8), (0, 384)))
        return jnp.concatenate([squares, vecs]).astype(BF16)

    def total_far(v, m, sel=None):
        return (v.astype(F32) + swap(v, m, sel).astype(F32)).astype(BF16)

    packed_one, packed_two = pack(0), pack(1)

    out_parts, out_one, out_two = scatter_side(after(out_m, scan_done), out_t, heads)
    head_parts = after(tuple(head_parts), sq_i, out_two)
    grad_lin = kernel_call(
        functools.partial(linear_back_kernel, n, span),
        (me1, g_conv, keep, taps, *head_parts),
        [(flat, BF16)],
        [
            pltpu.VMEM((9 * SIDE, 8, CW), F32),
            pltpu.VMEM((3 * SIDE, CW), F32),
            pltpu.VMEM(wide, F32),
        ],
        us=8,
    )[0]
    grad_lin = after(grad_lin, out_parts)
    grad_pre = jnp.concatenate([grad_gate, grad_lin], axis=1)
    back_t = dot(grad_pre[four:], w_mix).astype(BF16)
    back_m = dot(after(grad_pre[:four], back_t), w_mix)
    parts, mark_one, mark_two = scatter_side(
        back_m, back_t
    )
    go0, go1 = far_rest(after(go0, mark_two), 1), far_rest(after(go1, mark_two), 1, None, only)
    packed_one, packed_two = after((packed_one, packed_two), mark_one)
    packed_one = total_far(packed_one, masks[-1])
    packed_two = total_far(packed_two, masks[-1], only)
    packed_one, packed_two = after((packed_one, packed_two), mark_two)
    for m in masks[:-1]:
        packed_one, packed_two = total_far(packed_one, m), total_far(packed_two, m, only)
    block_output = kernel_call(
        functools.partial(add_kernel, n),
        (after(middle, mark_one), *out_parts),
        [((tok, width), F32)],
        smem=0,
    )[0]

    gp = mixer_grad(after(grad_pre, mark_one), norm_mine, norm_theirs)
    gp0 = jnp.concatenate([gp[:SLOT], gp[CW : CW + SLOT]])
    gp1 = jnp.concatenate([gp[SLOT : 2 * SLOT], gp[CW + SLOT : CW + 2 * SLOT]])
    gp0 = far_first(gp0, 1)
    gp1 = far_first(after(gp1, mark_two), 1, None, only)
    input_grad, gain_grad_one = kernel_call(
        functools.partial(input_back_kernel, n),
        (me1, block_input, grad_middle, gain_one, *after(parts, block_output)),
        [((tok, width), F32), ((1, width), F32)],
        [held],
    )
    done = input_grad
    sent_pair = feed_send(after(pair_sum, done))
    grad_w_down = feed_rows(sent_down, done)[0]
    grad_w_gate, grad_w_value = feed_rows(sent_pair, done)

    def to_rows(parts, kinds):
        size = (2 * kinds * SLOT + 127) // 128 * 128
        back = kernel_call(turn_back_kernel, parts, [((SIDE, rows_w, size), BF16)], smem=0)[0]
        return kernel_call(
            functools.partial(head_rows_kernel, blk),
            (exchange(back),),
            [((rows_w, heads_count * blk), F32)] * kinds,
            smem=0,
        )

    gp0, gp1 = far_rest(gp0, 1), far_rest(gp1, 1, None, only)
    go0, go1, gp0, gp1 = after((go0, go1, gp0, gp1), done, sent_pair)
    grad_w_out = to_rows((go0, go1), 1)[0]
    grad_w_g, grad_w_l = to_rows((gp0, gp1), 2)

    pack_one, pack_two = after((packed_one, packed_two), done)
    packs_mine, packs_theirs = gather_side(pack_one)
    two_x = swap(pack_two, XBIT, only)
    head = here >> 1
    mine_is_eight = (head == 0) | (head == 1)
    both = jnp.where(head == 0, pack_two, jnp.where(head == 3, pack_two, two_x))
    two_l = swap(both, lbit(n))
    eight = jnp.where(mine_is_eight, both, two_l)
    nine = jnp.where(mine_is_eight, two_l, both)
    pair = jnp.stack([eight, nine])
    pair_c = swap(pair, CBIT)
    pair = jnp.where((here & 1) == 0, pair, pair_c)
    shape = (4, rows, 768)
    grad_r_weight, grad_i_weight, small = kernel_call(
        functools.partial(packs_kernel, n, blk),
        (me1, packs_mine.reshape(shape), packs_theirs.reshape(shape), pair[0], pair[1]),
        [((heads_count, blk, blk), F32)] * 2 + [((8, heads_count * blk), F32)],
    )

    gains = jnp.concatenate([gain_grad_one, gain_grad_two]).reshape(-1, 256)
    gains = gains + swap(gains, CBIT)
    rest = [XBIT, lbit(n)] + masks
    while rest:
        one, two, rest = rest[0], rest[1], rest[2:]
        gains = (gains + swap(gains, one)) + (swap(gains, two) + swap(gains, one | two))
    gains = gains.reshape(2, width)

    return (
        block_output,
        input_grad,
        gains[0],
        grad_w_g,
        grad_w_l,
        small[4:],
        small[3],
        grad_r_weight,
        small[0],
        grad_i_weight,
        small[1],
        small[2],
        grad_w_out,
        gains[1],
        grad_w_gate,
        grad_w_value,
        grad_w_down,
    )


def solution(mesh):
    split, whole = P(AXIS, None), P()
    in_specs = (split, P(AXIS), whole, split, split) + (whole,) * 7
    in_specs += (split, whole, split, split, split, split)
    out_specs = (split, split, whole, split, split) + (whole,) * 7
    out_specs += (split, whole, split, split, split)
    return jax.shard_map(body, mesh=mesh, in_specs=in_specs, out_specs=out_specs, check_vma=False)
```

```python
import functools

import jax
import jax.numpy as jnp
from jax import lax
from jax.experimental import pallas as pl
from jax.experimental.pallas import tpu as pltpu
from jax.sharding import PartitionSpec as P

AXIS = "seq"
ROOT_GUARD = 0.001
F32, BF16 = jnp.float32, jnp.bfloat16
SIDE = 8
XBIT, CBIT = 2, 1
EXTRA = {0: 8, 6: 9}
SLOT = 288
CW = 640
HALO = 16
SHORT_ROW = 2048
UNROLL = 4


def lbit(n):
    return 8 if n == 32 else 4


def far_masks(n):
    masks, m = [], n // 2
    while m >= 4:
        if m != lbit(n):
            masks.append(m)
        m //= 2
    return masks


def row_span(n, tok):
    return SHORT_ROW // tok if n * tok == 2 * SHORT_ROW else n


def side_mask(q, n):
    return (q & 1) * XBIT | ((q >> 1) & 1) * lbit(n) | ((q >> 2) & 1) * CBIT


def side_place(d, n):
    x = (d >> (XBIT.bit_length() - 1)) & 1
    l = (d >> (lbit(n).bit_length() - 1)) & 1
    return x + l * 2 + ((d >> (CBIT.bit_length() - 1)) & 1) * 4


def side_code(i, n):
    return (i & 3) | (((i & lbit(n)) != 0) * 4)


def side_groups(n):
    low = XBIT | CBIT | lbit(n)
    return [
        sorted(b | side_mask(q, n) for q in range(SIDE)) for b in range(n) if b & low == 0
    ]


def far_groups(n):
    low = XBIT | CBIT | lbit(n)
    return [[i for i in range(n) if i & low == side_mask(q, n)] for q in range(SIDE)]


def far_mask_of(r, n):
    return sum(m for k, m in enumerate(far_masks(n)) if (r >> k) & 1)


def near_units(n, me):
    low = 2 if lbit(n) == 8 else 3
    units = []
    for r in range(n // SIDE):
        for l in range(SIDE >> low):
            u = 0
            for k, m in enumerate(far_masks(n)):
                bit = lax.shift_right_logical(me, m.bit_length() - 1) & 1
                u = u + ((bit ^ ((r >> k) & 1)) << (m.bit_length() - 1 - low))
            units.append(u + (l << (lbit(n).bit_length() - 1 - low) if low == 2 else 0))
    return units


def fixed_units(n):
    low = 2 if lbit(n) == 8 else 3
    base = [g[0] for g in side_groups(n)]
    return [
        (b | (l * lbit(n) if low == 2 else 0)) >> low for b in base for l in range(SIDE >> low)
    ]


def swap(v, mask, only=None):
    n = lax.axis_size(AXIS)
    pairs = [(i, i ^ mask) for i in range(n) if only is None or side_code(i, n) in only]
    return lax.ppermute(v, AXIS, pairs)


def dot(a, b):
    return lax.dot_general(a, b, (((1,), (0,)), ((), ())), preferred_element_type=F32)


def dot_last(a, b):
    return lax.dot_general(a, b, (((1,), (1,)), ((), ())), preferred_element_type=F32)


def dot_first(a, b):
    return lax.dot_general(a, b, (((0,), (0,)), ((), ())), preferred_element_type=F32)


def after(v, *deps):
    return lax.optimization_barrier((v, *deps))[0]


def kernel_call(kernel, ins, outs, scratch=(), smem=1, us=3):
    specs = [pl.BlockSpec(memory_space=pltpu.SMEM)] * smem
    specs += [pl.BlockSpec(memory_space=pltpu.VMEM)] * (len(ins) - smem)
    return pl.pallas_call(
        kernel,
        in_specs=specs,
        out_specs=[pl.BlockSpec(memory_space=pltpu.VMEM)] * len(outs),
        out_shape=[jax.ShapeDtypeStruct(s, d) for s, d in outs],
        scratch_shapes=list(scratch),
        compiler_params=pltpu.CompilerParams(vmem_limit_bytes=12 * 1024 * 1024),
        cost_estimate=pl.CostEstimate(
            flops=us * 10**9, bytes_accessed=us * 3 * 10**6, transcendentals=0
        ),
    )(*ins)


def gather_side(x, main=None, marks=(None, None)):
    n = lax.axis_size(AXIS)
    half = x.shape[0] // 32 * 16
    by_l, by_x = swap(x, lbit(n)), swap(x, XBIT)
    if marks[0] is not None:
        by_l, by_x = after((by_l, by_x), marks[0])
    low, high = swap(by_l[:half], XBIT), swap(by_x[half:], lbit(n))
    if marks[1] is not None:
        low, high = after((low, high), marks[1])
    if main is None:
        mine = jnp.concatenate([x, by_x, by_l, low, high])
        return mine, swap(mine, CBIT)
    cut = main - half
    mine = jnp.concatenate([x[:main], by_x[:main], by_l[:main], low, high[:cut]])
    rest = jnp.concatenate([x[main:], by_x[main:], by_l[main:], high[cut:]])
    return mine, swap(mine, CBIT), rest, swap(rest, CBIT)


def first_sum_kernel(mine, recv, send_a, send_b, keep_a, keep_b):
    tok, half = mine.shape[0] // 4, mine.shape[1] // 2
    step = 16

    def tile(i, _):
        for b in range(4):
            rows = pl.ds(pl.multiple_of(b * tok + i * step, step), step)
            at = lambda k: pl.ds(pl.multiple_of(k * tok + i * step, step), step)
            va = mine[rows, :half] + recv[rows, :half].astype(F32)
            vb = mine[rows, half:] + recv[rows, half:].astype(F32)
            if b < 2:
                keep_a[at(b), :] = va
            else:
                send_a[at(b - 2), :] = va.astype(BF16)
            if b % 2 == 0:
                keep_b[at(b // 2), :] = vb
            else:
                send_b[at(b // 2), :] = vb.astype(BF16)
        return 0

    lax.fori_loop(0, tok // step, tile, 0)


def second_sum_kernel(keep_a, recv_a, keep_b, recv_b, send_a, send_b, last):
    tok, half = send_a.shape
    step = 16

    def tile(i, _):
        own = pl.ds(pl.multiple_of(i * step, step), step)
        far = pl.ds(pl.multiple_of(tok + i * step, step), step)
        last[own, :half] = keep_a[own, :] + recv_a[own, :].astype(F32)
        last[own, half:] = keep_b[own, :] + recv_b[own, :].astype(F32)
        send_a[own, :] = (keep_a[far, :] + recv_a[far, :].astype(F32)).astype(BF16)
        send_b[own, :] = (keep_b[far, :] + recv_b[far, :].astype(F32)).astype(BF16)
        return 0

    lax.fori_loop(0, tok // step, tile, 0)


def scatter_side(mine, theirs, mark=None, mark_last=None):
    n = lax.axis_size(AXIS)
    rows, width = mine.shape
    tok, half = rows // 4, width // 2
    recv = swap(theirs, CBIT)
    send_a, send_b, keep_a, keep_b = kernel_call(
        first_sum_kernel,
        (mine, recv),
        [((2 * tok, half), BF16)] * 2 + [((2 * tok, half), F32)] * 2,
        smem=0,
    )
    recv_a, recv_b = swap(send_a, lbit(n)), swap(send_b, XBIT)
    if mark is not None:
        keep_a = after(keep_a, mark)
    send_a, send_b, last = kernel_call(
        second_sum_kernel,
        (keep_a, recv_a, keep_b, recv_b),
        [((tok, half), BF16)] * 2 + [((tok, width), F32)],
        smem=0,
    )
    parts = (last, swap(send_a, XBIT), swap(send_b, lbit(n)))
    if mark_last is not None:
        parts = after(parts, mark_last)
    return parts, keep_a, last


def rms_scale(values):
    return lax.rsqrt(jnp.mean(values * values, axis=-1, keepdims=True) + 1e-06)


def unit_slice(u, size):
    return pl.ds(pl.multiple_of(u * size, 128), size)


def put_units(out, rows, value_ref, value_rows, units, size):
    for p, u in enumerate(units):
        out[rows, p * size : (p + 1) * size] = value_ref[value_rows, unit_slice(u, size)]


def tail_kernel(x, gain, flags, out):
    v = x[...]
    out[...] = (v * rms_scale(v) * gain[...]).astype(BF16)
    row = lax.broadcasted_iota(jnp.int32, (HALO, 128), 0) == 0
    out[:, :128] = jnp.where(row, flags[...], out[:, :128].astype(F32)).astype(BF16)


ROWS = 32


def norm_one_kernel(n, me, x, gain, flags, tail, out, held):
    units = near_units(n, me[0])
    size = x.shape[1] // len(units)
    tok = x.shape[0]
    for i in range(tok // ROWS):
        rows = slice(i * ROWS, (i + 1) * ROWS)
        v = x[rows, :]
        held[...] = v * rms_scale(v) * gain[...]
        for p, u in enumerate(units):
            out[rows, p * size : (p + 1) * size] = held[:, unit_slice(u, size)].astype(BF16)
    halo = slice(tok, tok + HALO)
    put_units(out, halo, tail, slice(0, HALO), units, size)
    row = lax.broadcasted_iota(jnp.int32, (HALO, 128), 0)
    first = out[halo, :128].astype(F32)
    both = jnp.where(row == 0, flags[...], first)
    both = jnp.where(row == 1, tail[:, :128].astype(F32)[0:1], both)
    out[halo, :128] = both.astype(BF16)


def top_kernel(n, g, out):
    units = fixed_units(n)
    size = g.shape[1] // len(units)
    for p, u in enumerate(units):
        out[:, p * size : (p + 1) * size] = g[:, u * size : (u + 1) * size].astype(BF16)


def summed(last, ra, rb, rows, p, size):
    half = ra.shape[1]
    a, b = p * size, (p + 1) * size
    if b <= half:
        extra = ra[rows, a:b]
    else:
        extra = rb[rows, a - half : b - half]
    return last[rows, a:b] + extra.astype(F32)


def norm_two_kernel(n, me, x, gain, last, ra, rb, middle, out, held):
    units = near_units(n, me[0])
    size = x.shape[1] // len(units)
    for i in range(x.shape[0] // ROWS):
        rows = slice(i * ROWS, (i + 1) * ROWS)
        for p, u in enumerate(units):
            held[:, unit_slice(u, size)] = summed(last, ra, rb, rows, p, size)
        v = held[...] + x[rows, :]
        middle[rows, :] = v
        w = (v * rms_scale(v) * gain[...]).astype(BF16)
        for p, u in enumerate(fixed_units(n)):
            out[rows, p * size : (p + 1) * size] = w[:, u * size : (u + 1) * size]


def add_kernel(n, middle, last, ra, rb, out):
    units = fixed_units(n)
    size = middle.shape[1] // len(units)
    for p, u in enumerate(units):
        at = slice(u * size, (u + 1) * size)
        out[:, at] = middle[:, at] + summed(last, ra, rb, slice(None), p, size)


def norm_back(grad_normed, values, gain):
    scale = rms_scale(values)
    scaled = grad_normed * gain
    back = scale * scaled - values * (scale * scale * scale) * jnp.mean(
        scaled * values, axis=-1, keepdims=True
    )
    return back, grad_normed * values * scale


def middle_back_kernel(n, me, values, base, gain, last, ra, rb, grad, branch, gain_grad, held):
    units = near_units(n, me[0])
    size = values.shape[1] // len(units)
    total = jnp.zeros((1, values.shape[1]), F32)
    for i in range(values.shape[0] // ROWS):
        rows = slice(i * ROWS, (i + 1) * ROWS)
        for p, u in enumerate(fixed_units(n)):
            held[:, u * size : (u + 1) * size] = summed(last, ra, rb, rows, p, size)
        back, part = norm_back(held[...], values[rows, :], gain[...])
        total = total + jnp.sum(part, axis=0, keepdims=True)
        out = base[rows, :] + back
        grad[rows, :] = out
        held[...] = out
        for p, u in enumerate(units):
            branch[rows, p * size : (p + 1) * size] = held[:, unit_slice(u, size)].astype(BF16)
    gain_grad[...] = total


def input_back_kernel(n, me, values, base, gain, last, ra, rb, grad, gain_grad, held):
    units = near_units(n, me[0])
    size = values.shape[1] // len(units)
    total = jnp.zeros((1, values.shape[1]), F32)
    for i in range(values.shape[0] // ROWS):
        rows = slice(i * ROWS, (i + 1) * ROWS)
        for p, u in enumerate(units):
            held[:, unit_slice(u, size)] = summed(last, ra, rb, rows, p, size)
        back, part = norm_back(held[...], values[rows, :], gain[...])
        total = total + jnp.sum(part, axis=0, keepdims=True)
        grad[rows, :] = base[rows, :] + back
    gain_grad[...] = total


def gelu_pair(v):
    k = 0.7978845608028654
    sq = v * v
    th = jnp.tanh(k * v * (1.0 + 0.044715 * sq))
    half = 0.5 * (1.0 + th)
    slope = half + 0.5 * v * (1.0 - th * th) * (k * (1.0 + 3.0 * 0.044715 * sq))
    return v * half, slope


def strided(i, tok):
    return pl.ds(i, SIDE, stride=tok)


TILES = CW // 128


def cols(c):
    return slice(c * 128, (c + 1) * 128)


def join(tiles):
    return jnp.concatenate(tiles, axis=1)


def stepwise(tok, step, state, reverse=False):
    def some(o, state):
        for k in range(UNROLL):
            i = o * UNROLL + k
            state = step(tok - 1 - i if reverse else i, state)
        return state

    return lax.fori_loop(0, tok // UNROLL, some, state)


def step_rows(i):
    return pl.ds(pl.multiple_of(i * SIDE, SIDE), SIDE)


def mixer_kernel(
    lin_mine, lin_theirs, halo, keep, halo_keep, taps, r_sq, i_sq, vec,
    lin, low, rg, ig, dec, acc, loc, before, totals, conv,
):
    tok = conv.shape[1] // SIDE
    four = 4 * tok
    for c in range(TILES):
        lin[c, :four, :] = lin_mine[:, CW + c * 128 : CW + (c + 1) * 128]
        lin[c, four:, :] = lin_theirs[:, CW + c * 128 : CW + (c + 1) * 128]
        conv[c, : SIDE * HALO, :] = halo[:, cols(c)]
        for k in range(3):
            before[c, k * SIDE : (k + 1) * SIDE, :] = conv[c, strided(HALO - 1 - k, HALO), :]

    for c in range(TILES):
        t0, t1, t2, t3 = (taps[k : k + 1, cols(c)] for k in range(4))
        bias = vec[0:1, cols(c)]

        def conv_step(i, state):
            v1, v2, v3, k1, k2 = state
            v0 = lin[c, strided(i, tok), :]
            k0 = keep[step_rows(i), :]
            conv[c, strided(i, tok), :] = (
                v0 * t0 + bias + k0 * (v1 * t1 + k1 * (v2 * t2 + k2 * (v3 * t3)))
            )
            return v0, v1, v2, k0, k1

        start = tuple(before[c, k * SIDE : (k + 1) * SIDE, :] for k in range(3))
        start += (halo_keep[2 * SIDE :, :], halo_keep[SIDE : 2 * SIDE, :])
        stepwise(tok, conv_step, start)

    def gates(b, _):
        rows = pl.ds(pl.multiple_of(b * tok, tok), tok)
        low_here = join([conv[c, rows, :].astype(BF16) for c in range(TILES)])
        low[rows, :] = low_here
        r = jax.nn.sigmoid(dot(low_here, r_sq[...]) + vec[1:2, :])
        i = jax.nn.sigmoid(dot(low_here, i_sq[...]) + vec[2:3, :])
        for c in range(TILES):
            conv[c, rows, :] = low_here[:, cols(c)].astype(F32)
            rg[c, rows, :] = r[:, cols(c)]
            ig[c, rows, :] = i[:, cols(c)]
        return 0

    lax.fori_loop(0, SIDE, gates, 0)

    def scan_step(i, state):
        at = strided(i, tok)
        k0 = keep[step_rows(i), :]
        out = []
        for c in range(TILES):
            p, s = state[c]
            a = jnp.exp(rg[c, at, :] * vec[3:4, cols(c)]) * k0
            root = jnp.sqrt(1.0 - a * a + ROOT_GUARD)
            b = (k0 * root + (1.0 - k0)) * ig[c, at, :] * conv[c, at, :]
            p, s = p * a, a * s + b
            dec[c, at, :] = a
            acc[c, at, :] = p
            loc[c, at, :] = s
            out.append((p, s))
        return tuple(out)

    shape = (SIDE, 128)
    start = tuple((jnp.ones(shape, F32), jnp.zeros(shape, F32)) for _ in range(TILES))
    found = stepwise(tok, scan_step, start)
    for c in range(TILES):
        totals[:SIDE, cols(c)], totals[SIDE:, cols(c)] = found[c]


def gelu_kernel(gate_mine, gate_theirs, act, slope):
    four = gate_mine.shape[0]

    def tile(i, _):
        rows = pl.ds(pl.multiple_of(i * 16, 16), 16)
        later = pl.ds(pl.multiple_of(four + i * 16, 16), 16)
        for src, dst in ((gate_mine, rows), (gate_theirs, later)):
            for c in range(TILES):
                act[c, dst, :], slope[c, dst, :] = gelu_pair(src[rows, cols(c)])
        return 0

    lax.fori_loop(0, four // 16, tile, 0)


def chain_kernel(n, span, reverse, me_ref, *refs):
    *parts, out, held = refs
    me = me_ref[0]
    state = jnp.zeros((1, CW), F32)
    order = range(span - 1, -1, -1) if reverse else range(span)
    near = [m for m in far_masks(n) if m < span]

    def place(d):
        r = 0
        for k, m in enumerate(near):
            r = r + (((d >> (m.bit_length() - 1)) & 1) << k)
        return r, side_place(d, n)

    both = 2 * SIDE
    for r, part in enumerate(parts):
        for k in range(both):
            held[r * both + k, 0:1, :] = part[k : k + 1, :]
    base = len(parts) * both
    for i in order:
        r, q = place((me & (span - 1)) ^ i)
        held[base + i, 0:1, :] = state
        scale = held[r * both + q, 0:1, :]
        value = held[r * both + SIDE + q, 0:1, :]
        state = scale * state + value
    for q in range(SIDE):
        at = base + ((me & (span - 1)) ^ side_mask(q, n))
        out[q, :, :] = jnp.broadcast_to(held[at, 0:1, :], (8, CW))


def states_kernel(acc, loc, incoming, act, slope, states, mixed, slope_states):
    tok = acc.shape[1] // SIDE
    for q in range(SIDE):

        def tile(i, _):
            rows = pl.ds(pl.multiple_of(q * tok + i * 16, 16), 16)
            out = []
            for c in range(TILES):
                s = loc[c, rows, :] + acc[c, rows, :] * incoming[q, 0:1, cols(c)]
                states[c, rows, :] = s
                slope_states[c, rows, :] = s * slope[c, rows, :]
                out.append((s * act[c, rows, :]).astype(BF16))
            mixed[rows, :] = join(out)
            return 0

        lax.fori_loop(0, tok // 16, tile, 0)


def back_scan_kernel(gm_mine, gm_theirs, act, dec, grads, suffix, totals):
    tok = act.shape[1] // SIDE
    four = 4 * tok
    for c in range(TILES):
        grads[c, :four, :] = gm_mine[:, cols(c)] * act[c, :four, :]
        grads[c, four:, :] = gm_theirs[:, cols(c)] * act[c, four:, :]

    def step(i, state):
        at = strided(i, tok)
        out = []
        for c in range(TILES):
            ag, aq = state[c]
            g = grads[c, at, :] + ag
            grads[c, at, :] = g
            suffix[c, at, :] = aq
            a = dec[c, at, :]
            out.append((a * g, a * aq))
        return tuple(out)

    shape = (SIDE, 128)
    start = tuple((jnp.zeros(shape, F32), jnp.ones(shape, F32)) for _ in range(TILES))
    found = stepwise(tok, step, start, True)
    for c in range(TILES):
        totals[SIDE:, cols(c)], totals[:SIDE, cols(c)] = found[c]


def gate_back_kernel(gm_mine, gm_theirs, slope_states, out):
    four = gm_mine.shape[0]

    def tile(i, _):
        rows = pl.ds(pl.multiple_of(i * 16, 16), 16)
        later = pl.ds(pl.multiple_of(four + i * 16, 16), 16)
        for src, dst in ((gm_mine, rows), (gm_theirs, later)):
            out[dst, :] = join(
                [(src[rows, cols(c)] * slope_states[c, dst, :]).astype(BF16) for c in range(TILES)]
            )
        return 0

    lax.fori_loop(0, four // 16, tile, 0)


def mixer_back_kernel(
    grads, suffix, from_later, dec, rg, ig, low, states, incoming, lin, before, keep, halo_keep,
    keep_rows, r_sq, i_sq, vec, g_reset, g_input, g_conv, sums, heads,
):
    tok = dec.shape[1] // SIDE
    zero = jnp.zeros((1, 128), F32)

    def block(b, totals):
        rows = pl.ds(pl.multiple_of(b * tok, tok), tok)
        k = keep_rows[rows, :]
        at_first = lax.broadcasted_iota(jnp.int32, (tok, 128), 0) == 0
        out, g_rs, g_is, base = [], [], [], []
        for c in range(TILES):
            gs = grads[c, rows, :] + suffix[c, rows, :] * from_later[b, 0:1, cols(c)]
            a, r, i_g = dec[c, rows, :], rg[c, rows, :], ig[c, rows, :]
            v = low[rows, cols(c)].astype(F32)
            root = jnp.sqrt(1.0 - a * a + ROOT_GUARD)
            mult = k * root + (1.0 - k)
            prior = pltpu.roll(states[c, rows, :], 1, 0)
            prior = jnp.where(at_first, incoming[b, 0:1, cols(c)], prior)
            gv = gs * v
            glr = a * (gs * prior - gv * i_g * a / root) * r
            g_r = (vec[3:4, cols(c)] * glr * (1.0 - r)).astype(BF16)
            gm = gs * mult * i_g
            g_i = (gm * v * (1.0 - i_g)).astype(BF16)
            out.append(
                (
                    totals[c][0] + jnp.sum(glr, axis=0, keepdims=True),
                    totals[c][1] + jnp.sum(g_r.astype(F32), axis=0, keepdims=True),
                    totals[c][2] + jnp.sum(g_i.astype(F32), axis=0, keepdims=True),
                )
            )
            g_rs.append(g_r)
            g_is.append(g_i)
            g_conv[c, rows, :] = gm
        g_r, g_i = join(g_rs), join(g_is)
        g_reset[rows, :] = g_r
        g_input[rows, :] = g_i
        more = dot_last(g_r, r_sq[...]) + dot_last(g_i, i_sq[...])
        for c in range(TILES):
            g_conv[c, rows, :] = g_conv[c, rows, :] + more[:, cols(c)]
        return tuple(out)

    found = lax.fori_loop(0, SIDE, block, ((zero,) * 3,) * TILES)
    for c in range(TILES):
        dec_sum, r_sum, i_sum = found[c]
        sums[0:1, cols(c)] = r_sum
        sums[1:2, cols(c)] = i_sum
        sums[2:3, cols(c)] = -vec[4:5, cols(c)] * dec_sum

    blank = jnp.zeros((SIDE, 128), F32)
    for c in range(TILES):

        def tap_step(i, state):
            v1, v2, v3, k1, k2, s0, s1, s2, s3, sb = state
            v0 = lin[c, strided(i, tok), :]
            k0 = keep[step_rows(i), :]
            g0 = g_conv[c, strided(i, tok), :]
            g1 = g0 * k0
            g2 = g1 * k1
            g3 = g2 * k2
            return (
                (v0, v1, v2, k0, k1)
                + (s0 + g0 * v0, s1 + g1 * v1, s2 + g2 * v2, s3 + g3 * v3, sb + g0)
            )

        start = tuple(before[c, k * SIDE : (k + 1) * SIDE, :] for k in range(3))
        start += (halo_keep[2 * SIDE :, :], halo_keep[SIDE : 2 * SIDE, :]) + (blank,) * 5
        end = stepwise(tok, tap_step, start)
        per_row = [jnp.sum(v, axis=0, keepdims=True) for v in end[5:]]
        sums[3:4, cols(c)] = per_row[4]
        for j in range(4):
            sums[4 + j : 5 + j, cols(c)] = per_row[j]
        k = None
        for i in range(3):
            k_i = keep[i * SIDE : (i + 1) * SIDE, :]
            k = k_i if k is None else k * k_i
            heads[i * SIDE : (i + 1) * SIDE, cols(c)] = g_conv[c, strided(i, tok), :] * k


def linear_back_kernel(n, span, me_ref, g_conv, keep, taps, *refs):
    *parts, out, held, after, conv = refs
    me = me_ref[0]
    tok = g_conv.shape[1] // SIDE
    rows3 = 3 * SIDE
    for k, part in enumerate(parts):
        for m in range(rows3):
            held[k * rows3 + m, 0:1, :] = part[m : m + 1, :]
    low_far = far_masks(n)[-1]
    side = XBIT | CBIT | lbit(n)
    for q in range(SIDE):
        nxt = (me ^ side_mask(q, n)) + 1
        d = nxt ^ me
        far = d & ~side
        ok = ((nxt & (span - 1)) != 0).astype(F32)
        which = jnp.where(far == 0, 0, jnp.where(far == low_far, 1, len(parts) - 1))
        for m in range(3):
            at = which * rows3 + m * SIDE + side_place(d, n)
            after[m * SIDE + q : m * SIDE + q + 1, :] = held[at, 0:1, :] * ok
    one = jnp.ones((SIDE, 128), F32)
    for c in range(TILES):
        t0, t1, t2, t3 = (taps[k : k + 1, cols(c)] for k in range(4))

        def step(i, state):
            g1, g2, g3, k1, k2, k3 = state
            g0 = g_conv[c, strided(i, tok), :]
            conv[c, strided(i, tok), :] = g0 * t0 + k1 * (g1 * t1 + k2 * (g2 * t2 + k3 * (g3 * t3)))
            return g0, g1, g2, keep[step_rows(i), :], k1, k2

        start = tuple(after[m * SIDE : (m + 1) * SIDE, cols(c)] for m in range(3))
        stepwise(tok, step, start + (one, one, one), True)

    def tile(i, _):
        rows = pl.ds(pl.multiple_of(i * 16, 16), 16)
        out[rows, :] = join([conv[c, rows, :].astype(BF16) for c in range(TILES)])
        return 0

    lax.fori_loop(0, SIDE * tok // 16, tile, 0)


def heads_kernel(blk, gate, linear, out_w, first, second):
    first[...] = jnp.zeros(first.shape, BF16)
    second[...] = jnp.zeros(second.shape, BF16)
    for k, w in enumerate((gate, linear, out_w)):
        at = slice(k * SLOT, k * SLOT + blk)
        for s in range(SIDE):
            first[s, :, at] = w[:, s * blk : (s + 1) * blk]
        for s, e in EXTRA.items():
            second[s, :, at] = w[:, e * blk : (e + 1) * blk]


def feed_parts_kernel(*refs):
    *weights, out = refs
    size = out.shape[2] // len(weights)
    for k, w in enumerate(weights):
        for s in range(SIDE):
            out[s, :, k * size : (k + 1) * size] = w[:, s * size : (s + 1) * size]


def feed_join_kernel(parts, *outs):
    size = parts.shape[2] // len(outs)
    for k, out in enumerate(outs):
        for s in range(SIDE):
            out[:, s * size : (s + 1) * size] = parts[s, :, k * size : (k + 1) * size].astype(F32)


def turn_kernel(parts, *outs):
    rows = parts.shape[1]
    turned = parts[...].reshape(SIDE * rows, parts.shape[2]).T
    at = 0
    for out in outs:
        out[...] = turned[at : at + out.shape[0]]
        at += out.shape[0]


def assemble_kernel(count, which, *refs):
    first, extra, out = refs[:count], refs[count : 2 * count], refs[2 * count]
    size = first[0].shape[1]
    for r in range(count):
        lanes = slice(r * size, (r + 1) * size)
        for m, k in enumerate(which):
            out[m * CW : m * CW + SLOT, lanes] = first[r][m * SLOT : (m + 1) * SLOT, :]
            out[m * CW + SLOT : m * CW + 2 * SLOT, lanes] = extra[r][k * SLOT : (k + 1) * SLOT, :]
            out[m * CW + 2 * SLOT : (m + 1) * CW, lanes] = jnp.zeros((CW - 2 * SLOT, size), BF16)


def turn_back_kernel(*refs):
    *parts, out = refs
    rows = out.shape[1]
    flat = jnp.concatenate([p[...] for p in parts])
    out[:, :, : flat.shape[0]] = flat.T.reshape(SIDE, rows, flat.shape[0])


def head_rows_kernel(blk, parts, *outs):
    count = len(outs)
    for k, out in enumerate(outs):
        for s in range(SIDE):
            at = k * SLOT
            out[:, s * blk : (s + 1) * blk] = parts[s, :, at : at + blk].astype(F32)
        for s, e in EXTRA.items():
            at = (count + k) * SLOT
            out[:, e * blk : (e + 1) * blk] = parts[s, :, at : at + blk].astype(F32)


def packs_kernel(n, blk, me_ref, mine, theirs, eight, nine, r_out, i_out, vec_out):
    me = me_ref[0]

    def put(ref, e, shift):
        def lanes(v):
            return v[:, shift : shift + blk]

        r_out[e, :, :] = lanes(ref[:SLOT, :384].astype(F32))[:blk]
        i_out[e, :, :] = lanes(ref[:SLOT, 384:].astype(F32))[:blk]
        vec_out[:, e * blk : (e + 1) * blk] = lanes(ref[SLOT:, :384].astype(F32)[:8])

    for s in range(SIDE):
        i = (s & 3) | ((s >> 2) * lbit(n))
        d = jnp.int32(i) ^ (me & (XBIT | CBIT | lbit(n)))
        q = ((d >> (XBIT.bit_length() - 1)) & 1) + ((d >> (lbit(n).bit_length() - 1)) & 1) * 2
        own = ((d >> (CBIT.bit_length() - 1)) & 1) == 0

        @pl.when(own)
        def _():
            put(mine.at[q], s, 0)

        @pl.when(jnp.logical_not(own))
        def _():
            put(theirs.at[q], s, 0)

    put(eight, EXTRA[0], 32)
    put(nine, EXTRA[6], 32)


def body(
    block_input,
    start_flags,
    norm_gain,
    gate_weight,
    linear_weight,
    conv_taps,
    conv_bias,
    reset_weight,
    reset_bias,
    input_weight,
    input_bias,
    decay_param,
    out_weight,
    feed_norm_gain,
    feed_gate_weight,
    feed_value_weight,
    feed_down_weight,
    output_grad,
):
    n = lax.axis_size(AXIS)
    me = lax.axis_index(AXIS)
    me1 = me.reshape(1)
    here = side_code(me, n)
    tok, width = block_input.shape
    heads_count, blk = reset_weight.shape[:2]
    rows_w = gate_weight.shape[0]
    feed = feed_gate_weight.shape[1]
    fs = feed // SIDE
    masks = far_masks(n)
    groups, far = side_groups(n), far_groups(n)
    only = tuple(EXTRA)
    has_extra = (here == only[0]) | (here == only[1])
    extra_here = jnp.where(here == only[1], EXTRA[only[1]], EXTRA[only[0]])
    four = 4 * tok
    side_tok = SIDE * tok
    cols_w = SIDE * rows_w
    places = n // SIDE
    count = len(masks)

    def exchange(v):
        return lax.all_to_all(v, AXIS, 0, 0, axis_index_groups=groups, tiled=True)

    def gather_far(x, sel=None):
        chunks = [x]
        for m in masks:
            chunks += [swap(c, m, sel) for c in chunks]
        return chunks

    gain_one = norm_gain.astype(F32)[None]
    gain_two = feed_norm_gain.astype(F32)[None]
    flags = start_flags.astype(F32)[None]
    parts, more_parts = kernel_call(
        functools.partial(heads_kernel, blk),
        (gate_weight, linear_weight, out_weight),
        [((SIDE, rows_w, 3 * SLOT + 32), BF16)] * 2,
        smem=0,
    )
    tail = kernel_call(
        tail_kernel,
        (after(block_input[-HALO:], parts), gain_one, flags),
        [((HALO, width), BF16)],
        smem=0,
        us=1,
    )[0]
    tail = lax.ppermute(tail, AXIS, [(i, i + 1) for i in range(n - 1)])
    packet = kernel_call(
        functools.partial(norm_one_kernel, n),
        (me1, block_input, gain_one, flags, tail),
        [((tok + HALO, width), BF16)],
        [pltpu.VMEM((ROWS, width), F32)],
    )[0]
    f_parts = kernel_call(
        feed_parts_kernel,
        (after(feed_value_weight, packet), feed_gate_weight, feed_down_weight),
        [((SIDE, rows_w, 3 * fs), BF16)],
        smem=0,
    )[0]
    top = kernel_call(
        functools.partial(top_kernel, n),
        (after(output_grad, f_parts),),
        [((tok, width), BF16)],
        smem=0,
    )[0]
    parts = exchange(parts)
    p_mix, p_out = kernel_call(
        turn_kernel, (parts,), [((k * SLOT, cols_w), BF16) for k in (2, 1)], smem=0
    )
    more_parts = exchange(after(more_parts, parts))
    f_parts = exchange(after(f_parts, more_parts))
    p_extra = kernel_call(turn_kernel, (more_parts,), [((3 * SLOT, cols_w), BF16)], smem=0)[0]

    def gather_start(x, count=2, sel=None):
        return [x] + [swap(x, m, sel) for m in masks[:count]]

    def gather_later(chunks, sel=None, mark=None):
        chunks = list(chunks)
        if mark is not None:
            chunks[1] = after(chunks[1], mark)
        if len(chunks) == 3:
            chunks.append(swap(chunks[1], masks[1], sel))
        for m in masks[len(chunks).bit_length() - 1 :]:
            chunks += [swap(c, m, sel) for c in chunks]
        return chunks

    packet = after(packet, p_mix)
    c_mix = gather_start(p_mix)
    half = tok // 2
    by_l, by_x = swap(packet, lbit(n)), swap(packet, XBIT)
    (c_mix, by_l, by_x, p_extra) = lax.optimization_barrier((c_mix, by_l, by_x, p_extra))
    c_mix = gather_later(c_mix)
    c_extra = gather_start(p_extra, 1, only)
    low, high = swap(by_l[:half], XBIT), swap(by_x[half:], lbit(n))
    (c_mix, c_extra, low, high, p_out) = lax.optimization_barrier(
        (c_mix, c_extra, low, high, p_out)
    )
    f_parts = after(f_parts, c_extra)
    c_extra = gather_later(c_extra, only)
    c_out = gather_start(p_out, 1)
    f_parts = f_parts.reshape(cols_w, 3 * fs)
    norm_mine = jnp.concatenate([packet[:tok], by_x[:tok], by_l[:tok], low, high[:half]])
    halo_mine = jnp.concatenate([packet[tok:], by_x[tok:], by_l[tok:], high[half:]])
    norm_theirs, halo_theirs = swap(norm_mine, CBIT), swap(halo_mine, CBIT)
    w_mix = kernel_call(
        functools.partial(assemble_kernel, places, (0, 1)),
        (*c_mix, *c_extra),
        [((2 * CW, width), BF16)],
        smem=0,
        us=5,
    )[0]
    c_out = gather_later([after(p_out, w_mix), c_out[1]], mark=w_mix)
    w_mix = after(w_mix, tuple(f_parts))

    def feed_full(part):
        return lax.all_gather(part, AXIS, axis_index_groups=far, tiled=True)

    w_first, w_value = feed_full(f_parts[:, fs:]), feed_full(f_parts[:, :fs])
    w_gate, w_down = w_first[:, :fs], w_first[:, fs:]

    def pick(p):
        one = lax.dynamic_index_in_dim(p, here, 0, False)
        two = lax.dynamic_index_in_dim(p, extra_here, 0, False)
        return one, jnp.where(has_extra, two, jnp.zeros_like(two))

    vectors = jnp.concatenate(
        [conv_taps]
        + [v[None] for v in (conv_bias, reset_bias, input_bias, decay_param)]
    ).astype(F32)
    vectors = vectors.reshape(8, heads_count, blk).transpose(1, 0, 2)
    vec_one, vec_two = pick(vectors)
    gap = ((0, 0), (0, SLOT - blk))
    vectors = jnp.concatenate([jnp.pad(vec_one, gap), jnp.pad(vec_two, gap)], axis=1)
    vectors = jnp.pad(vectors, ((0, 0), (0, CW - 2 * SLOT)))
    taps = vectors[:4]
    decay_float = vectors[7]
    vec = jnp.concatenate(
        [
            vectors[4:7],
            (-8.0 * jax.nn.softplus(-decay_float))[None],
            (-8.0 * jax.nn.sigmoid(-decay_float))[None],
            jnp.zeros((3, CW), F32),
        ]
    )

    def square(p):
        one, two = pick(p)
        low = CW - SLOT - blk
        return jnp.pad(one, ((0, CW - blk),) * 2) + jnp.pad(two, ((SLOT, low),) * 2)

    r_sq, i_sq = square(reset_weight), square(input_weight)

    halo_all = jnp.concatenate([halo_mine, halo_theirs])
    flag_rows = halo_all.reshape(SIDE, HALO, width)[:, :2, :128].astype(F32)
    keep_blocks = 1.0 - flag_rows[:, 0]
    keep = jnp.broadcast_to(keep_blocks.T[:, :, None], (tok, SIDE, 128)).reshape(side_tok, 128)
    keep_rows = jnp.broadcast_to(keep_blocks[:, :, None], (SIDE, tok, 128)).reshape(side_tok, 128)
    halo_keep = 1.0 - flag_rows[:, 1, tok - 3 :]
    halo_keep = jnp.broadcast_to(halo_keep.T[:, :, None], (3, SIDE, 128)).reshape(3 * SIDE, 128)

    pre_mine, pre_theirs = dot_last(norm_mine, w_mix), dot_last(norm_theirs, w_mix)
    halo = dot_last(halo_all, w_mix[CW:])
    top = after(top, w_mix)
    top_l, top_x = swap(top, lbit(n)), swap(top, XBIT)
    flat, wide = (side_tok, CW), (TILES, side_tok, 128)
    lin, low, rg, ig, dec, acc, loc, before, totals = kernel_call(
        mixer_kernel,
        (pre_mine, pre_theirs, halo, keep, halo_keep, taps, r_sq, i_sq, vec),
        [(wide, F32), (flat, BF16)]
        + [(wide, F32)] * 5
        + [((TILES, 3 * SIDE, 128), F32), ((2 * SIDE, CW), F32)],
        [pltpu.VMEM(wide, F32)],
        smem=0,
        us=29,
    )

    span = row_span(n, tok)

    def chain(totals, reverse, mark):
        near = [far_mask_of(r, n) for r in range(1, n // SIDE)]
        parts = [totals] + [swap(totals, m) for m in near if m < span]
        parts = after(tuple(parts), mark)
        return kernel_call(
            functools.partial(chain_kernel, n, span, reverse),
            (me1, *parts),
            [((SIDE, 8, CW), F32)],
            [pltpu.VMEM((len(parts) * 2 * SIDE + span, 8, CW), F32)],
            us=2,
        )[0]

    top_l, top_x = after((top_l, top_x), totals)
    top_low, top_high = swap(top_l[: tok // 2], XBIT), swap(top_x[tok // 2 :], lbit(n))
    gate_halves = after((pre_mine, pre_theirs), totals, top_l)
    act, slope = kernel_call(gelu_kernel, gate_halves, [(wide, F32)] * 2, smem=0, us=7)
    c_out, c_extra = after((tuple(c_out), tuple(c_extra)), act)
    w_out = kernel_call(
        functools.partial(assemble_kernel, places, (2,)),
        (*c_out, *c_extra),
        [((CW, width), BF16)],
        smem=0,
    )[0]
    incoming = chain(totals, False, w_out)
    top_mine = jnp.concatenate([top, top_x, top_l, top_low, top_high])
    incoming = after(incoming, top_low, top_high)
    states, mixed, slope_states = kernel_call(
        states_kernel,
        (acc, loc, incoming, act, slope),
        [(wide, F32), (flat, BF16), (wide, F32)],
        smem=0,
        us=8,
    )
    theirs = dot(mixed[four:], w_out).astype(BF16)
    mixed_mine = after(mixed[:four], theirs)
    parts, mark_one, mark_two = scatter_side(dot(mixed_mine, w_out), theirs)
    top_theirs = swap(after(top_mine, mark_one), CBIT)
    gh_mine = dot(after(top_mine, mark_one), w_down)
    parts = after(parts, gh_mine)
    held = pltpu.VMEM((ROWS, width), F32)
    middle, normed_two = kernel_call(
        functools.partial(norm_two_kernel, n),
        (me1, block_input, gain_two, *parts),
        [((tok, width), F32), ((tok, width), BF16)],
        [held],
    )

    gh_theirs = dot(after(top_theirs, normed_two), w_down)
    two_mine, two_theirs = gather_side(normed_two, marks=(gh_theirs, None))

    def feed_half(two, inner_gate, grad_hidden):
        inner_value = dot(two, w_value)
        act, slope = gelu_pair(inner_gate)
        hidden = (act * inner_value).astype(BF16)
        grad_ig = (grad_hidden * inner_value * slope).astype(BF16)
        grad_iv = (grad_hidden * act).astype(BF16)
        return hidden, jnp.concatenate([grad_ig, grad_iv], axis=1)

    ig_mine, ig_theirs = dot(two_mine, w_gate), dot(two_theirs, w_gate)
    hid_t, gi_t = feed_half(after(two_theirs, ig_mine), ig_theirs, gh_theirs)
    back_t = (dot_last(gi_t[:, :fs], w_gate) + dot_last(gi_t[:, fs:], w_value)).astype(BF16)
    two_mine = after(two_mine, back_t)
    hid_m, gi_m = feed_half(two_mine, ig_mine, gh_mine)
    back_m = dot_last(gi_m[:, :fs], w_gate) + dot_last(gi_m[:, fs:], w_value)

    def feed_grad(a_m, b_m, a_t, b_t, mark):
        a_m, a_t = after((a_m, a_t), mark)
        return (dot_first(a_m, b_m) + dot_first(a_t, b_t)).astype(BF16)

    def halve(x, m, axis, mark, sel):
        half = x.shape[axis] // 2
        kept = lax.slice_in_dim(x, 0, half, axis=axis)
        got = swap(lax.slice_in_dim(x, half, 2 * half, axis=axis), m, sel)
        if mark is not None:
            got = after(got, mark)
        return (kept.astype(F32) + got.astype(F32)).astype(BF16)

    def far_first(x, axis, mark=None, sel=None):
        return halve(x, masks[-1], axis, mark, sel)

    def far_rest(x, axis, mark=None, sel=None):
        for m in reversed(masks[:-1]):
            x = halve(x, m, axis, mark, sel)
        return x

    parts, mark_one, mark_two = scatter_side(back_m, back_t)
    feed_mark = mark_two
    fg_down = feed_grad(top_mine, hid_m, top_theirs, hid_t, mark_one)
    hid_t, hid_m = after((hid_t, hid_m), mark_two, fg_down)
    out_t = dot_last(hid_t, w_down).astype(BF16)
    out_m = dot_last(after(hid_m, out_t), w_down)
    parts = after(parts, out_m)
    grad_middle, branch, gain_grad_two = kernel_call(
        functools.partial(middle_back_kernel, n),
        (me1, middle, output_grad, gain_two, *parts),
        [((tok, width), F32), ((tok, width), BF16), ((1, width), F32)],
        [held],
    )
    fg_pair = feed_grad(two_mine, gi_m, two_theirs, gi_t, branch)
    branch_mine, branch_theirs = gather_side(branch, marks=(fg_pair, None))

    gm_theirs = dot_last(branch_theirs, w_out)
    gm_mine = dot_last(branch_mine, w_out)
    grads, suffix, totals = kernel_call(
        back_scan_kernel,
        (gm_mine, gm_theirs, act, dec),
        [(wide, F32), (wide, F32), ((2 * SIDE, CW), F32)],
        smem=0,
        us=16,
    )
    scan_done = totals
    slope_states = after(slope_states, totals)
    grad_gate = kernel_call(
        gate_back_kernel, (gm_mine, gm_theirs, slope_states), [(flat, BF16)], smem=0
    )[0]

    def mixer_grad(grad, mine, theirs):
        return (dot_first(grad[:four], mine) + dot_first(grad[four:], theirs)).astype(BF16)

    def feed_send(shard):
        return exchange(shard.reshape(SIDE, rows_w, shard.shape[1]))

    def feed_rows(v, mark):
        kinds = v.shape[2] // fs
        return kernel_call(
            feed_join_kernel, (after(v, mark),), [((rows_w, feed), F32)] * kinds, smem=0, us=2
        )

    mixed_late = after(mixed, grad_gate)
    go = mixer_grad(mixed_late, branch_mine, branch_theirs)
    def feed_sum(g):
        return lax.psum_scatter(g, AXIS, axis_index_groups=far, tiled=True)

    down_sum = feed_sum(after(fg_down, feed_mark))
    pair_sum = feed_sum(fg_pair)
    sent_down = feed_send(after(down_sum, scan_done))
    from_later = chain(totals, True, (go, sent_down))
    go = after(go, from_later)
    go0, go1 = far_first(go[:SLOT], 1), far_first(go[SLOT : 2 * SLOT], 1, None, only)
    g_reset, g_input, g_conv, sums, heads = kernel_call(
        mixer_back_kernel,
        (
            grads, suffix, from_later, dec, rg, ig, low, states, incoming, lin, before, keep,
            halo_keep, keep_rows, r_sq, i_sq, vec,
        ),
        [(flat, BF16)] * 2 + [(wide, F32), ((8, CW), F32), ((3 * SIDE, CW), F32)],
        smem=0,
        us=21,
    )
    heads_y = swap(heads, masks[-1])
    head_parts = [heads, heads_y]
    if span == n:
        low_far = masks[-1]
        side = XBIT | CBIT | lbit(n)
        pairs = []
        for i in range(n):
            for j in range(n):
                last = (i | side) + 1
                if last < n and (j & ~side) == (last & ~side) and (j & side) == (i & side):
                    if ((i ^ j) & ~side) != low_far:
                        pairs.append((j, i))
        head_parts.append(lax.ppermute(heads, AXIS, pairs))
    low_late = after(low, heads, go0, go1)
    sq_r, sq_i = dot_first(low_late, g_reset), dot_first(low_late, g_input)

    rows = SLOT + HALO

    def pack(slot):
        r0, c0 = slot * SLOT, slot * 256
        squares = jnp.concatenate(
            [sq_r[r0 : r0 + SLOT, c0 : c0 + 384], sq_i[r0 : r0 + SLOT, c0 : c0 + 384]], axis=1
        )
        vecs = jnp.pad(sums[:, c0 : c0 + 384], ((0, 8), (0, 384)))
        return jnp.concatenate([squares, vecs]).astype(BF16)

    def total_far(v, m, sel=None):
        return (v.astype(F32) + swap(v, m, sel).astype(F32)).astype(BF16)

    packed_one, packed_two = pack(0), pack(1)

    out_parts, out_one, out_two = scatter_side(after(out_m, scan_done), out_t, heads)
    head_parts = after(tuple(head_parts), sq_i, out_two)
    grad_lin = kernel_call(
        functools.partial(linear_back_kernel, n, span),
        (me1, g_conv, keep, taps, *head_parts),
        [(flat, BF16)],
        [
            pltpu.VMEM((9 * SIDE, 8, CW), F32),
            pltpu.VMEM((3 * SIDE, CW), F32),
            pltpu.VMEM(wide, F32),
        ],
        us=8,
    )[0]
    grad_lin = after(grad_lin, out_parts)
    grad_pre = jnp.concatenate([grad_gate, grad_lin], axis=1)
    back_t = dot(grad_pre[four:], w_mix).astype(BF16)
    back_m = dot(after(grad_pre[:four], back_t), w_mix)
    parts, mark_one, mark_two = scatter_side(
        back_m, back_t
    )
    go0, go1 = far_rest(after(go0, mark_two), 1), far_rest(after(go1, mark_two), 1, None, only)
    packed_one, packed_two = after((packed_one, packed_two), mark_one)
    packed_one = total_far(packed_one, masks[-1])
    packed_two = total_far(packed_two, masks[-1], only)
    packed_one, packed_two = after((packed_one, packed_two), mark_two)
    for m in masks[:-1]:
        packed_one, packed_two = total_far(packed_one, m), total_far(packed_two, m, only)
    block_output = kernel_call(
        functools.partial(add_kernel, n),
        (after(middle, mark_one), *out_parts),
        [((tok, width), F32)],
        smem=0,
    )[0]

    gp = mixer_grad(after(grad_pre, mark_one), norm_mine, norm_theirs)
    gp0 = jnp.concatenate([gp[:SLOT], gp[CW : CW + SLOT]])
    gp1 = jnp.concatenate([gp[SLOT : 2 * SLOT], gp[CW + SLOT : CW + 2 * SLOT]])
    gp0 = far_first(gp0, 1)
    gp1 = far_first(after(gp1, mark_two), 1, None, only)
    input_grad, gain_grad_one = kernel_call(
        functools.partial(input_back_kernel, n),
        (me1, block_input, grad_middle, gain_one, *after(parts, block_output)),
        [((tok, width), F32), ((1, width), F32)],
        [held],
    )
    done = input_grad
    sent_pair = feed_send(after(pair_sum, mark_two))
    grad_w_down = feed_rows(sent_down, done)[0]
    grad_w_gate, grad_w_value = feed_rows(sent_pair, done)

    def to_rows(parts, kinds):
        size = (2 * kinds * SLOT + 127) // 128 * 128
        back = kernel_call(turn_back_kernel, parts, [((SIDE, rows_w, size), BF16)], smem=0)[0]
        return kernel_call(
            functools.partial(head_rows_kernel, blk),
            (exchange(back),),
            [((rows_w, heads_count * blk), F32)] * kinds,
            smem=0,
        )

    gp0, gp1 = far_rest(gp0, 1), far_rest(gp1, 1, None, only)
    go0, go1, gp0, gp1 = after((go0, go1, gp0, gp1), done, sent_pair)
    grad_w_out = to_rows((go0, go1), 1)[0]
    grad_w_g, grad_w_l = to_rows((gp0, gp1), 2)

    pack_one, pack_two = after((packed_one, packed_two), done)
    packs_mine, packs_theirs = gather_side(pack_one)
    two_x = swap(pack_two, XBIT, only)
    head = here >> 1
    mine_is_eight = (head == 0) | (head == 1)
    both = jnp.where(head == 0, pack_two, jnp.where(head == 3, pack_two, two_x))
    two_l = swap(both, lbit(n))
    eight = jnp.where(mine_is_eight, both, two_l)
    nine = jnp.where(mine_is_eight, two_l, both)
    pair = jnp.stack([eight, nine])
    pair_c = swap(pair, CBIT)
    pair = jnp.where((here & 1) == 0, pair, pair_c)
    shape = (4, rows, 768)
    grad_r_weight, grad_i_weight, small = kernel_call(
        functools.partial(packs_kernel, n, blk),
        (me1, packs_mine.reshape(shape), packs_theirs.reshape(shape), pair[0], pair[1]),
        [((heads_count, blk, blk), F32)] * 2 + [((8, heads_count * blk), F32)],
    )

    gains = jnp.concatenate([gain_grad_one, gain_grad_two]).reshape(-1, 256)
    gains = gains + swap(gains, CBIT)
    rest = [XBIT, lbit(n)] + masks
    while rest:
        one, two, rest = rest[0], rest[1], rest[2:]
        gains = (gains + swap(gains, one)) + (swap(gains, two) + swap(gains, one | two))
    gains = gains.reshape(2, width)

    return (
        block_output,
        input_grad,
        gains[0],
        grad_w_g,
        grad_w_l,
        small[4:],
        small[3],
        grad_r_weight,
        small[0],
        grad_i_weight,
        small[1],
        small[2],
        grad_w_out,
        gains[1],
        grad_w_gate,
        grad_w_value,
        grad_w_down,
    )


def solution(mesh):
    split, whole = P(AXIS, None), P()
    in_specs = (split, P(AXIS), whole, split, split) + (whole,) * 7
    in_specs += (split, whole, split, split, split, split)
    out_specs = (split, split, whole, split, split) + (whole,) * 7
    out_specs += (split, whole, split, split, split)
    return jax.shard_map(body, mesh=mesh, in_specs=in_specs, out_specs=out_specs, check_vma=False)
```
